32 devices in a mesh: ep: 8 (over y, x, core), tp: 4 (over z).
Axes of the slice: x: 2, y: 2, z: 4, core: 2. Of those that a mesh axis runs over, the one named last changes fastest.
Arguments:
- hidden_in: bfloat16 [2048, 2048], P('ep'), may hold values from -6 to 6
- expert_ids: int32 [2048, 8], P('ep'), may hold values from 0 to 31, all different within a row; in each aligned block of 256 rows (0 to 255, 256 to 511, ...) at most 128 rows name the same one
- attention_gain: bfloat16 [2048], P('ep'), may hold values from 0.5 to 1.5
- query_gain: bfloat16 [128], P('ep'), may hold values from 0.5 to 1.5
- key_gain: bfloat16 [128], P('ep'), may hold values from 0.5 to 1.5
- query_weight: bfloat16 [2048, 4096], P('ep', 'tp'), may hold values from -0.125 to 0.125
- key_matrix: bfloat16 [2048, 512], P('ep', 'tp'), may hold values from -0.125 to 0.125
- value_matrix: bfloat16 [2048, 512], P('ep', 'tp'), may hold values from -0.125 to 0.125
- output_weight: bfloat16 [4096, 2048], P('tp'), may hold values from -1.5 to 1.5
- expert_gain: bfloat16 [2048], P('ep'), may hold values from 0.5 to 1.5
- router_weight: bfloat16 [2048, 32], P('ep'), may hold values from -0.0625 to 0.0625
- gate_up_weight: bfloat16 [32, 2048, 1536], P('ep', None, 'tp'), may hold values from -0.125 to 0.125
- down_weight: bfloat16 [32, 768, 2048], P('ep', 'tp'), may hold values from -1.75 to 1.75
- output_grad: bfloat16 [2048, 2048], P('ep'), may hold values from -6 to 6
Outputs:
- block_out: bfloat16 [2048, 2048], P('ep')
- input_grad: float32 [2048, 2048], P('ep')
- attention_gain_grad: float32 [2048], P('ep')
- query_gain_grad: float32 [128], P('ep')
- key_gain_grad: float32 [128], P('ep')
- query_weight_grad: float32 [2048, 4096], P('ep', 'tp')
- key_weight_grad: float32 [2048, 512], P('ep', 'tp')
- value_weight_grad: float32 [2048, 512], P('ep', 'tp')
- output_weight_grad: float32 [4096, 2048], P('tp')
- expert_gain_grad: float32 [2048], P('ep')
- router_weight_grad: float32 [2048, 32], P('ep')
- gate_up_weight_grad: float32 [32, 2048, 1536], P('ep', None, 'tp')
- down_weight_grad: float32 [32, 768, 2048], P('ep', 'tp')
The draws below stay inside these ranges and needn't reach their ends.
Inputs may be any that keep to these rules, and one draw needn't show every extreme that they name: `expert_ids`: each row names 8 different experts. Among the tokens of one index of ep (aligned blocks of 256 rows) no expert is named by more than 128 rows, a bound that some block reaches.
All inputs are finite; a program needn't handle non-finite values.
Results may differ from the reference program's by a relative error of at most 0.024.
Values may be sent and summed in bfloat16 or wider, within the bound.
No kernel may reach another device: no remote copies, remote signals or barrier semaphores. Data moves between devices by JAX's collectives and lax.ppermute only.
A program may use at most 320 MiB of HBM per device.

```python
import math
import jax
import jax.numpy as jnp
import numpy as np
from jax import lax

MODEL_WIDTH = 2048
QUERY_HEADS = 32
KEY_VALUE_HEADS = 4
HEAD_SIZE = 128
FF = 768
TOP = 8
PAIR = 64
TOK_DEV = 256
EXPERTS = 32
TOKEN_COUNT = 2048
SEQUENCE_LENGTH = 256
CAP = 128
N_EP = 8


def shard_levels(rng, shape, split, least, high):
    def one(axis_at, shards_of):
        draws = jax.random.uniform(jax.random.fold_in(jax.random.fold_in(rng, 6), axis_at), (shards_of,), jnp.float32, least / len(split), high / len(split))
        return jnp.repeat(jnp.exp(draws), shape[axis_at] // shards_of).reshape((-1,) + (1,) * (len(shape) - axis_at - 1))

    factor_of = one(*split[0])
    for cut in split[1:]:
        factor_of = factor_of * one(*cut)
    return factor_of


def routed_block(stream_key, own, number, rows, amount, top, bound, slope):
    sequence = jax.random.permutation(stream_key, amount)
    crowded, ordinary = portions_of(amount, rows * top, bound, slope, True), portions_of(amount, rows * top, bound, slope, False)
    places = jnp.arange(amount)

    def named(sizes, turn):
        used = int((sizes > 0).sum())
        fixed = max(1, used // 4)
        shifted = fixed + (places - fixed + turn * (used - fixed)) % max(1, amount - fixed)
        return jnp.zeros((amount,), jnp.int32).at[sequence[jnp.where(places < fixed, places, shifted)]].set(jnp.asarray(sizes, jnp.int32))

    sizes = jnp.where(number % 4 == 0, named(crowded, number // 4), named(ordinary, number - number // 4 - 1))
    mixed = jax.random.permutation(jax.random.fold_in(own, 3), amount)
    source_of, taker = mixed[0:amount // 2 * 2:2], mixed[1:amount // 2 * 2:2]
    margin = jnp.minimum(sizes[source_of] - 1, bound - sizes[taker]) // 2
    margin = jnp.where((source_of == sequence[0]) | (taker == sequence[0]) | (sizes[taker] == 0), 0, jnp.maximum(margin, 0))
    shifted = jax.random.randint(jax.random.fold_in(own, 4), (amount // 2,), 0, 1 << 20) % (margin + 1)
    sizes = sizes.at[source_of].add(-shifted).at[taker].add(shifted)
    items = jnp.searchsorted(jnp.cumsum(sizes), jnp.arange(rows * top), side="right").astype(jnp.int32)
    grid = items.reshape(top, rows).T
    grid = grid[jax.random.permutation(jax.random.fold_in(own, 1), rows)]
    turn = jax.random.randint(jax.random.fold_in(own, 2), (rows, 1), 0, top)
    return jnp.take_along_axis(grid, (jnp.arange(top)[None, :] + turn) % top, axis=1)


def portions_of(count, total, most, slope, full):
    weights = [(1 << 20) // math.isqrt(grade ** slope) + 1 for grade in range(1, count + 1)]
    largest = most if full else min(most, max(-(-total // count), total * weights[0] // sum(weights)))
    least = 1 if total - largest >= count - 1 else 0
    given, rest = [largest] + [least] * (count - 1), total - largest - least * (count - 1)
    while rest > 0:
        free = [i for i in range(1, count) if given[i] < largest] or [i for i in range(1, count) if given[i] < most]
        mass, budget = sum([weights[i] for i in free]), rest
        for i in free:
            more = min(most - given[i], max(1, budget * weights[i] // mass), rest)
            given[i] = given[i] + more
            rest = rest - more
    return np.array(given)


def bell_draw(rng, shape, scale, reach, cuts=(), held_as=jnp.bfloat16):
    level = shard_levels(rng, shape, cuts, -0.22, 0.18) if cuts else 1.0
    values = jax.random.normal(rng, shape, jnp.float32) * scale * level
    return jnp.minimum(jnp.maximum(values, -reach), reach).astype(held_as)


def setup_inputs(seed: int = 0) -> dict:
    splits = jax.random.split(jax.random.key(seed), 15)
    hidden_in = bell_draw(splits[0], (TOKEN_COUNT, MODEL_WIDTH), 1.0, 6.0, ((0, 8),))
    expert_ids_keys = jax.random.split(jax.random.fold_in(splits[1], 1), TOKEN_COUNT // TOK_DEV)
    expert_ids_turns = jax.random.permutation(jax.random.fold_in(splits[1], 3), TOKEN_COUNT // TOK_DEV)
    expert_ids = jax.vmap(lambda own, number: routed_block(jax.random.fold_in(splits[1], 2), own, number, TOK_DEV, EXPERTS, TOP, CAP, 1))(expert_ids_keys, expert_ids_turns).reshape((TOKEN_COUNT, TOP))
    attention_gain = jnp.clip(1.0 + 0.1 * jax.random.normal(splits[2], (MODEL_WIDTH,), jnp.float32), 0.5, 1.5).astype(jnp.bfloat16)
    query_gain = jnp.clip(1.0 + 0.1 * jax.random.normal(splits[3], (HEAD_SIZE,), jnp.float32), 0.5, 1.5).astype(jnp.bfloat16)
    key_gain = jnp.clip(1.0 + 0.1 * jax.random.normal(splits[4], (HEAD_SIZE,), jnp.float32), 0.5, 1.5).astype(jnp.bfloat16)
    query_weight = bell_draw(splits[5], (MODEL_WIDTH, QUERY_HEADS * HEAD_SIZE), MODEL_WIDTH ** -0.5, 0.125, ((0, 8), (1, 4)))
    key_matrix = bell_draw(splits[6], (MODEL_WIDTH, KEY_VALUE_HEADS * HEAD_SIZE), MODEL_WIDTH ** -0.5, 0.125, ((0, 8), (1, 4)))
    value_matrix = bell_draw(splits[7], (MODEL_WIDTH, KEY_VALUE_HEADS * HEAD_SIZE), MODEL_WIDTH ** -0.5, 0.125, ((0, 8), (1, 4)))
    output_weight = bell_draw(splits[8], (QUERY_HEADS * HEAD_SIZE, MODEL_WIDTH), (QUERY_HEADS * HEAD_SIZE // 256) ** -0.5, 1.5, ((0, 4),))
    expert_gain = jnp.clip(1.0 + 0.1 * jax.random.normal(splits[9], (MODEL_WIDTH,), jnp.float32), 0.5, 1.5).astype(jnp.bfloat16)
    router_weight = bell_draw(splits[10], (MODEL_WIDTH, EXPERTS), (4 * MODEL_WIDTH) ** -0.5, 0.0625, ((0, 8),))
    gate_up_weight = bell_draw(splits[11], (EXPERTS, MODEL_WIDTH, 2 * FF), MODEL_WIDTH ** -0.5, 0.125, ((0, 8), (2, 4)))
    down_weight = bell_draw(splits[12], (EXPERTS, FF, MODEL_WIDTH), (FF // 64) ** -0.5, 1.75, ((0, 8), (1, 4)))
    output_grad = bell_draw(splits[13], (TOKEN_COUNT, MODEL_WIDTH), 1.0, 6.0, ((0, 8),))
    return dict(hidden_in=hidden_in, expert_ids=expert_ids, attention_gain=attention_gain, query_gain=query_gain, key_gain=key_gain, query_weight=query_weight, key_matrix=key_matrix, value_matrix=value_matrix, output_weight=output_weight, expert_gain=expert_gain, router_weight=router_weight, gate_up_weight=gate_up_weight, down_weight=down_weight, output_grad=output_grad)


@jax.custom_vjp
def reduced_precision(v):
    return lax.optimization_barrier(v.astype(jnp.bfloat16)).astype(jnp.float32)

@jax.custom_vjp
def reduced_precision_backward(v):
    return v

def low_keep(v):
    return (reduced_precision(v), None)

def low_pass(kept, grad):
    return (grad,)

def back_keep(v):
    return (v, None)

def back_low(kept, grad):
    return (reduced_precision(grad),)
reduced_precision.defvjp(low_keep, low_pass)
reduced_precision_backward.defvjp(back_keep, back_low)
EPSILON = 1e-06
THETA = 1000000.0
HIGHEST = lax.Precision.HIGHEST

def matrix_product(left, right):
    return jnp.dot(left, right, precision=HIGHEST, preferred_element_type=jnp.float32)

def norm_rows(value_rows, norm_gain):
    return value_rows * lax.rsqrt(lax.optimization_barrier(jnp.mean(value_rows * value_rows, axis=-1, keepdims=True)) + EPSILON) * norm_gain

def rotary(value_rows, positions):
    halfway = value_rows.shape[-1] // 2
    inverse = THETA ** (-(jnp.arange(halfway, dtype=jnp.float32) * 2.0) / value_rows.shape[-1])
    angles = positions.astype(jnp.float32)[:, None] * inverse[None, :]
    cosine = jnp.cos(angles)[:, None, :]
    sine_table = jnp.sin(angles)[:, None, :]
    first_half = value_rows[..., :halfway]
    second_half = value_rows[..., halfway:]
    return jnp.concatenate([first_half * cosine - second_half * sine_table, second_half * cosine + first_half * sine_table], axis=-1)

def slot_index(chosen_ids):
    onehot = (chosen_ids[:, None] == jnp.arange(EXPERTS, dtype=jnp.int32)[None, :]).astype(jnp.int32)
    earlier = jnp.cumsum(onehot, axis=0) - onehot
    return chosen_ids * CAP + lax.optimization_barrier(jnp.sum(earlier * onehot, axis=1))

def fill_table(slots):
    return jnp.full((EXPERTS * CAP,), TOK_DEV * TOP, jnp.int32).at[slots].set(jnp.arange(TOK_DEV * TOP, dtype=jnp.int32))

def attention_forward(block):
    query_rows, key_rows, value_rows = block
    heads_per_group = QUERY_HEADS // KEY_VALUE_HEADS
    query_rows = query_rows.reshape(SEQUENCE_LENGTH, KEY_VALUE_HEADS, heads_per_group, HEAD_SIZE)
    scores = jnp.einsum('ikgd,jkd->kgij', query_rows, key_rows, precision=HIGHEST) / math.sqrt(HEAD_SIZE)
    scores = reduced_precision_backward(scores)
    allowed = jnp.arange(SEQUENCE_LENGTH)[:, None] >= jnp.arange(SEQUENCE_LENGTH)[None, :]
    scores = jnp.where(allowed, scores, -jnp.inf)
    row_max = lax.optimization_barrier(jnp.max(scores, axis=-1, keepdims=True))
    weights = jnp.exp(scores - row_max)
    probs = weights / lax.optimization_barrier(jnp.sum(weights, axis=-1, keepdims=True))
    attention_output = jnp.einsum('kgij,jkd->ikgd', reduced_precision(probs), value_rows, precision=HIGHEST)
    return reduced_precision(reduced_precision_backward(attention_output)).reshape(SEQUENCE_LENGTH, QUERY_HEADS * HEAD_SIZE)

def reference(hidden_in, expert_ids, attention_gain, query_gain, key_gain, query_weight, key_matrix, value_matrix, output_weight, expert_gain, router_weight, gate_up_weight, down_weight, output_grad):
    slots = jax.vmap(slot_index)(expert_ids.reshape(N_EP, TOK_DEV * TOP))
    tables = jax.vmap(fill_table)(slots)
    live_rows = (tables < TOK_DEV * TOP).astype(jnp.float32)
    owners = jnp.arange(N_EP, dtype=jnp.int32)[:, None] * TOK_DEV
    token_rows = owners + jnp.minimum(tables, TOK_DEV * TOP - 1) // TOP
    row_index = token_rows.reshape(N_EP, EXPERTS, CAP).transpose(1, 0, 2).reshape(EXPERTS, N_EP * CAP)
    row_live = live_rows.reshape(N_EP, EXPERTS, CAP).transpose(1, 0, 2).reshape(EXPERTS, N_EP * CAP)
    sources = jnp.arange(TOKEN_COUNT, dtype=jnp.int32) // TOK_DEV
    in_block = slots.reshape(TOKEN_COUNT, TOP) - expert_ids * CAP
    pair_row = (expert_ids * N_EP + sources[:, None]) * CAP + in_block
    positions = jnp.arange(TOKEN_COUNT, dtype=jnp.int32) % SEQUENCE_LENGTH
    sequence_batch = TOKEN_COUNT // SEQUENCE_LENGTH

    def forward(params):
        hidden, attn_gain, q_gain, k_gain, w_query, key_projection_weight, value_projection_weight, w_output, mlp_gain, w_router, w_gate_up, w_down = params
        normalized_input = reduced_precision(norm_rows(hidden, attn_gain))
        query_rows = reduced_precision_backward(matrix_product(normalized_input, w_query)).reshape(TOKEN_COUNT, QUERY_HEADS, HEAD_SIZE)
        key_rows = reduced_precision_backward(matrix_product(normalized_input, key_projection_weight)).reshape(TOKEN_COUNT, KEY_VALUE_HEADS, HEAD_SIZE)
        value_rows = reduced_precision(reduced_precision_backward(matrix_product(normalized_input, value_projection_weight))).reshape(TOKEN_COUNT, KEY_VALUE_HEADS, HEAD_SIZE)
        query_rows = reduced_precision(rotary(norm_rows(query_rows, q_gain), positions))
        key_rows = reduced_precision(rotary(norm_rows(key_rows, k_gain), positions))
        attention_output = lax.map(jax.checkpoint(attention_forward), (query_rows.reshape(sequence_batch, SEQUENCE_LENGTH, QUERY_HEADS, HEAD_SIZE), key_rows.reshape(sequence_batch, SEQUENCE_LENGTH, KEY_VALUE_HEADS, HEAD_SIZE), value_rows.reshape(sequence_batch, SEQUENCE_LENGTH, KEY_VALUE_HEADS, HEAD_SIZE)))
        attended = reduced_precision_backward(matrix_product(attention_output.reshape(TOKEN_COUNT, QUERY_HEADS * HEAD_SIZE), w_output))
        resid = hidden + attended
        routed = reduced_precision(norm_rows(resid, mlp_gain))
        logits = reduced_precision_backward(matrix_product(routed, w_router))
        logit_max = lax.optimization_barrier(jnp.max(logits, axis=-1, keepdims=True))
        exponent = jnp.exp(logits - logit_max)
        router = exponent / lax.optimization_barrier(jnp.sum(exponent, axis=-1, keepdims=True))
        chosen = jnp.take_along_axis(router, expert_ids, axis=1)
        gates = chosen / lax.optimization_barrier(jnp.sum(chosen, axis=1, keepdims=True))

        def expert(inputs):
            joined_mat, down_mat, index_rows, live_mask = inputs
            parted = joined_mat.reshape(MODEL_WIDTH, FF // PAIR, 2, PAIR)
            gate_mat = parted[:, :, 0, :].reshape(MODEL_WIDTH, FF)
            up_mat = parted[:, :, 1, :].reshape(MODEL_WIDTH, FF)
            rows = reduced_precision_backward(routed[index_rows] * live_mask[:, None])
            activation = reduced_precision_backward(matrix_product(rows, gate_mat))
            upper = reduced_precision_backward(matrix_product(rows, up_mat))
            inner = reduced_precision(jax.nn.silu(activation) * upper)
            return reduced_precision_backward(reduced_precision(matrix_product(inner, down_mat)))
        outputs = lax.map(jax.checkpoint(expert), (w_gate_up, w_down, row_index, row_live))
        paired = outputs.reshape(EXPERTS * N_EP * CAP, MODEL_WIDTH)[pair_row]
        mixture = jnp.einsum('tk,tkd->td', gates, paired, precision=HIGHEST)
        return resid + mixture
    params = (hidden_in.astype(jnp.float32), attention_gain.astype(jnp.float32), query_gain.astype(jnp.float32), key_gain.astype(jnp.float32), query_weight.astype(jnp.float32), key_matrix.astype(jnp.float32), value_matrix.astype(jnp.float32), output_weight.astype(jnp.float32), expert_gain.astype(jnp.float32), router_weight.astype(jnp.float32), gate_up_weight.astype(jnp.float32), down_weight.astype(jnp.float32))
    result, pullback = jax.vjp(forward, params)
    grads = pullback(output_grad.astype(jnp.float32))[0]
    return (result.astype(jnp.bfloat16), grads[0], grads[1], grads[2], grads[3], grads[4], grads[5], grads[6], grads[7], grads[8], grads[9], grads[10], grads[11])
```

```python
import functools
import math

import jax
import jax.numpy as jnp
from jax import lax
from jax.experimental import pallas as pl
from jax.experimental.pallas import tpu as pltpu
from jax.sharding import PartitionSpec as P

HEAD_SIZE = 128
TOP = 8
PAIR = 64
LANES = 128

EPSILON = 1e-06
THETA = 1000000.0
F32 = jnp.float32
BF16 = jnp.bfloat16


def norm_rows(value_rows, norm_gain):
    return (
        value_rows
        * lax.rsqrt(jnp.mean(value_rows * value_rows, axis=-1, keepdims=True) + EPSILON)
        * norm_gain
    )


def norm_back(value_rows, norm_gain, upstream):
    scaling = lax.rsqrt(jnp.mean(value_rows * value_rows, axis=-1, keepdims=True) + EPSILON)
    normal = value_rows * scaling
    weighted = upstream * norm_gain
    inward = scaling * (weighted - normal * jnp.mean(weighted * normal, axis=-1, keepdims=True))
    return (inward, upstream * normal)


def rope_tables(positions, head_size):
    halfway = head_size // 2
    inverse = THETA ** (-(jnp.arange(halfway, dtype=jnp.float32) * 2.0) / head_size)
    angles = positions.astype(jnp.float32)[:, None] * inverse[None, :]
    return (jnp.cos(angles)[:, None, :], jnp.sin(angles)[:, None, :])


def rotate(value_rows, cosine, sine_table):
    halfway = value_rows.shape[-1] // 2
    first_half = value_rows[..., :halfway]
    second_half = value_rows[..., halfway:]
    return jnp.concatenate(
        [
            first_half * cosine - second_half * sine_table,
            second_half * cosine + first_half * sine_table,
        ],
        axis=-1,
    )


def rotate_back(upstream, cosine, sine_table):
    halfway = upstream.shape[-1] // 2
    first_half = upstream[..., :halfway]
    second_half = upstream[..., halfway:]
    return jnp.concatenate(
        [
            first_half * cosine + second_half * sine_table,
            second_half * cosine - first_half * sine_table,
        ],
        axis=-1,
    )


SWAPPED = 8


def swap(value, axis, mask):
    count = lax.axis_size(axis)
    return lax.ppermute(value, axis, [(i, i ^ mask) for i in range(count)])


def link_bits(reverse):
    count = lax.axis_size("ep")
    bits = [1 << i for i in range(1, count.bit_length() - 1)]
    return bits[::-1] if reverse else bits


def gather_half(value, reverse):
    blocks = {0: value}
    for bit in link_bits(reverse):
        blocks.update({m | bit: swap(v, "ep", bit) for m, v in blocks.items()})
    blocks.update({m | 1: swap(v, "ep", 1) for m, v in blocks.items()})
    return [blocks[m] for m in range(lax.axis_size("ep"))]


def gather_blocks(value):
    if lax.axis_size("ep") > SWAPPED:
        return lax.all_gather(value, "ep", axis=0, tiled=True)
    half = value.shape[0] // 2
    upper = gather_half(value[:half], False)
    lower = gather_half(value[half:], True)
    return jnp.concatenate([v for pair in zip(upper, lower) for v in pair], axis=0)


def plus(left, right):
    return (left.astype(F32) + right.astype(F32)).astype(BF16)


def scatter_half(blocks, reverse):
    for bit in link_bits(reverse):
        blocks = {
            m: plus(v, swap(blocks[m | bit], "ep", bit)) for m, v in blocks.items() if not m & bit
        }
    return blocks[0]


def scatter_blocks(value):
    count = lax.axis_size("ep")
    if count > SWAPPED:
        return [lax.psum_scatter(value, "ep", scatter_dimension=0, tiled=True)]
    rows = value.shape[0] // count
    half = rows // 2
    piece = lambda m, h: value[m * rows + h * half : m * rows + (h + 1) * half]
    halves = []
    for h in range(2):
        blocks = {
            m: plus(piece(m, h), swap(piece(m | 1, h), "ep", 1)) for m in range(0, count, 2)
        }
        halves.append(scatter_half(blocks, h == 1))
    return halves


def sum_chunks(value):
    parts = lax.axis_size("tp")
    mine = lax.axis_index("tp")
    rows = value.shape[0] // parts
    take = lambda i: lax.dynamic_slice_in_dim(value, i * rows, rows, 0)
    total = take(mine).astype(F32)
    for mask in range(1, parts):
        total = total + swap(take(mine ^ mask), "tp", mask).astype(F32)
    return total


def spread_chunks(chunk):
    parts = lax.axis_size("tp")
    mine = lax.axis_index("tp")
    rows = chunk.shape[0]
    result = jnp.zeros((parts * rows,) + chunk.shape[1:], chunk.dtype)
    for mask in range(parts):
        piece = swap(chunk, "tp", mask) if mask else chunk
        result = lax.dynamic_update_slice_in_dim(result, piece, (mine ^ mask) * rows, 0)
    return result


def sum_tp(value):
    return spread_chunks(sum_chunks(value).astype(BF16))


def reorder(value, axis):
    count = lax.axis_size("ep")
    if count > SWAPPED:
        return value
    mine = lax.axis_index("ep")
    size = value.shape[axis] // count
    return jnp.concatenate(
        [lax.dynamic_slice_in_dim(value, (mine ^ m) * size, size, axis) for m in range(count)],
        axis=axis,
    )


def expert_kernel(
    base_ref, x_ref, g_ref, ids_ref, router_ref, wgu_ref, wd_ref, dx_ref, joined_ref, hidden_ref
):
    rows = x_ref.shape[0]
    features = x_ref.shape[1]
    expert_count = router_ref.shape[1]
    hidden_count = wd_ref.shape[0]
    extra = dx_ref.shape[1] - features
    base = base_ref[0]
    local = base_ref.shape[0] - 1
    x = x_ref[...]
    logits = jnp.dot(x, router_ref[...], preferred_element_type=F32)
    lane = lax.broadcasted_iota(jnp.int32, (rows, expert_count), 1)
    named = ids_ref[:, 0:1] == lane
    for k in range(1, TOP):
        named = named | (ids_ref[:, k : k + 1] == lane)
    exponent = jnp.exp(logits - jnp.max(logits, axis=1, keepdims=True))
    router = exponent / jnp.sum(exponent, axis=1, keepdims=True)
    chosen = jnp.where(named, router, 0.0)
    gates = chosen / jnp.sum(chosen, axis=1, keepdims=True)
    gate = [
        jnp.sum(jnp.where(lane == base + j, gates, 0.0), axis=1, keepdims=True)
        for j in range(local)
    ]
    act = jnp.dot(x, wgu_ref[...], preferred_element_type=F32)
    back = lax.dot_general(
        g_ref[...], wd_ref[...], (((1,), (1,)), ((), ())), preferred_element_type=F32
    )
    left = lax.broadcasted_iota(jnp.int32, (rows, LANES), 1) < PAIR
    per_expert = hidden_count // local // PAIR
    gate_sum = [jnp.zeros((rows, LANES), F32) for _ in range(local)]
    for p in range(hidden_count // LANES):
        one, two = 2 * p // per_expert, (2 * p + 1) // per_expert
        first = act[:, 2 * p * LANES : (2 * p + 1) * LANES]
        second = act[:, (2 * p + 1) * LANES : (2 * p + 2) * LANES]
        g = jnp.where(left, first, pltpu.roll(second, PAIR, 1))
        u = jnp.where(left, pltpu.roll(first, PAIR, 1), second)
        gh = back[:, p * LANES : (p + 1) * LANES]
        if one == two:
            scale = jnp.broadcast_to(gate[one], (rows, LANES))
        else:
            scale = jnp.where(left, gate[one], gate[two])
        sig = 1.0 / (1.0 + jnp.exp(-g))
        silu = g * sig
        hid = silu * u
        product = hid * gh
        if one == two:
            gate_sum[one] += product
        else:
            gate_sum[one] += jnp.where(left, product, 0.0)
            gate_sum[two] += jnp.where(left, 0.0, product)
        hidden_ref[:, p * LANES : (p + 1) * LANES] = (hid * scale).astype(BF16)
        gs = gh * scale
        dg = gs * u * sig * (1.0 + g * (1.0 - sig))
        du = gs * silu
        joined_ref[:, 2 * p * LANES : (2 * p + 1) * LANES] = jnp.where(
            left, dg, pltpu.roll(du, PAIR, 1)
        ).astype(BF16)
        joined_ref[:, (2 * p + 1) * LANES : (2 * p + 2) * LANES] = jnp.where(
            left, pltpu.roll(dg, PAIR, 1), du
        ).astype(BF16)
    dx = lax.dot_general(
        joined_ref[...], wgu_ref[...], (((1,), (1,)), ((), ())), preferred_element_type=F32
    )
    dx_ref[:, :features] = dx.astype(BF16)
    wide = lax.broadcasted_iota(jnp.int32, (rows, extra), 1)
    tail = jnp.zeros((rows, extra), F32)
    for j in range(local):
        total = jnp.sum(gate_sum[j], axis=1, keepdims=True)
        high = total.astype(BF16).astype(F32)
        tail = jnp.where(wide == base + j, high, tail)
        tail = jnp.where(wide == expert_count + base + j, total - high, tail)
    dx_ref[:, features:] = tail.astype(BF16)


def run_experts(x, g, ids, router, wgu, wd, local):
    tokens, features = x.shape
    tile = 256
    expert_count = router.shape[1]
    extra = -(-2 * expert_count // LANES) * LANES
    base = jnp.full((local + 1,), lax.axis_index("ep") * local, jnp.int32)
    whole = lambda v: pl.BlockSpec(v.shape, lambda i, s: (0, 0), pipeline_mode=pl.Buffered(1))
    by_rows = lambda width: pl.BlockSpec((tile, width), lambda i, s: (i, 0))
    return pl.pallas_call(
        expert_kernel,
        grid_spec=pltpu.PrefetchScalarGridSpec(
            num_scalar_prefetch=1,
            grid=(tokens // tile,),
            in_specs=[
                by_rows(features),
                by_rows(features),
                by_rows(TOP),
                whole(router),
                whole(wgu),
                whole(wd),
            ],
            out_specs=[by_rows(features + extra), by_rows(wgu.shape[1]), by_rows(wd.shape[0])],
        ),
        out_shape=[
            jax.ShapeDtypeStruct((tokens, features + extra), BF16),
            jax.ShapeDtypeStruct((tokens, wgu.shape[1]), BF16),
            jax.ShapeDtypeStruct((tokens, wd.shape[0]), BF16),
        ],
        compiler_params=pltpu.CompilerParams(vmem_limit_bytes=48 * 1024 * 1024),
        cost_estimate=pl.CostEstimate(
            flops=2 * tokens * features * (2 * wgu.shape[1] + wd.shape[0]),
            bytes_accessed=2 * tokens * features * 3 + 2 * features * 2 * wgu.shape[1],
            transcendentals=tokens * wd.shape[0],
        ),
    )(base, x, g, ids, router, wgu, wd)


def shards(
    hidden_in,
    expert_ids,
    attention_gain,
    query_gain,
    key_gain,
    query_weight,
    key_matrix,
    value_matrix,
    output_weight,
    expert_gain,
    router_weight,
    gate_up_weight,
    down_weight,
    output_grad,
):
    tokens, features = hidden_in.shape
    owners = lax.axis_size("ep")
    local_experts = gate_up_weight.shape[0]
    expert_count = local_experts * owners
    everyone = lambda v: lax.all_gather(v, "ep", axis=0, tiled=True)

    weights = jnp.concatenate([query_weight, key_matrix, value_matrix], axis=1)
    weights_rel = gather_blocks(weights)
    packed = everyone(
        jnp.concatenate([router_weight, attention_gain[:, None], expert_gain[:, None]], axis=1)
    )
    router_full = packed[:, :expert_count]
    attn_gain_full = packed[:, expert_count].astype(F32)
    mlp_gain_full = packed[:, expert_count + 1].astype(F32)
    head_gains = everyone(jnp.stack([query_gain, key_gain], axis=1)).astype(F32)
    query_gain_full = head_gains[:, 0]
    key_gain_full = head_gains[:, 1]
    ids_rel = gather_blocks(expert_ids)
    grads_rel = gather_blocks(output_grad)
    wgu = gate_up_weight.transpose(1, 0, 2).reshape(features, -1)
    wd = down_weight.reshape(-1, features)

    hidden_f = hidden_in.astype(F32)
    normed_low = norm_rows(hidden_f, attn_gain_full).astype(BF16)
    normed_rel = reorder(normed_low, 1)
    query_width = query_weight.shape[1]
    key_width = key_matrix.shape[1]
    query_heads = query_width // HEAD_SIZE
    key_heads = key_width // HEAD_SIZE
    heads_per_group = query_heads // key_heads
    raw = jnp.dot(normed_rel, weights_rel, preferred_element_type=F32)
    query_raw = raw[:, :query_width].reshape(tokens, query_heads, HEAD_SIZE)
    key_raw = raw[:, query_width : query_width + key_width].reshape(tokens, key_heads, HEAD_SIZE)
    value_low = raw[:, query_width + key_width :].astype(BF16)
    positions = jnp.arange(tokens, dtype=jnp.int32)
    cosine, sine_table = rope_tables(positions, HEAD_SIZE)
    query_low = rotate(norm_rows(query_raw, query_gain_full), cosine, sine_table).astype(BF16)
    all_keys = rotate(norm_rows(key_raw, key_gain_full), cosine, sine_table).astype(BF16)
    all_values = value_low.reshape(tokens, key_heads, HEAD_SIZE)
    allowed = jnp.arange(tokens)[None, :] <= jnp.arange(tokens)[:, None]
    grouped_queries = query_low.reshape(tokens, key_heads, heads_per_group, HEAD_SIZE)

    def score_block():
        raw_scores = jnp.einsum(
            "ikgd,jkd->kgij", grouped_queries, all_keys, preferred_element_type=F32
        ) / math.sqrt(HEAD_SIZE)
        return jnp.where(allowed, raw_scores, -jnp.inf)

    scores = score_block()
    row_max = jnp.max(scores, axis=-1, keepdims=True)
    exps = jnp.exp(scores - row_max)
    row_total = jnp.sum(exps, axis=-1, keepdims=True)
    probs = exps / row_total
    log_total = row_max + jnp.log(row_total)
    attention_output = (
        jnp.einsum("kgij,jkd->ikgd", probs.astype(BF16), all_values, preferred_element_type=F32)
        .astype(BF16)
        .reshape(tokens, query_heads * HEAD_SIZE)
    )
    head_part = jnp.dot(attention_output, output_weight, preferred_element_type=F32)
    attended = sum_tp(head_part.astype(BF16)).astype(F32)
    resid = hidden_f + attended
    routed_low = norm_rows(resid, mlp_gain_full).astype(BF16)
    routed_rel = gather_blocks(routed_low)
    logits = jnp.dot(routed_low, router_full, preferred_element_type=F32)
    logit_max = jnp.max(logits, axis=-1, keepdims=True)
    exponent = jnp.exp(logits - logit_max)
    router = exponent / jnp.sum(exponent, axis=-1, keepdims=True)
    every_expert = jnp.arange(expert_count, dtype=jnp.int32)
    named = jnp.any(expert_ids[:, :, None] == every_expert[None, None, :], axis=1)
    chosen = jnp.where(named, router, 0.0)
    chosen_total = jnp.sum(chosen, axis=1, keepdims=True)
    gates = chosen / chosen_total

    grad_parts, joined, hidden = run_experts(
        routed_rel, grads_rel, ids_rel, router_full, wgu, wd, local_experts
    )
    returned = sum_tp(jnp.concatenate(scatter_blocks(grad_parts), axis=0))

    mixture_parts = jnp.dot(hidden, wd, preferred_element_type=F32).astype(BF16)
    mixture = sum_tp(jnp.concatenate(scatter_blocks(mixture_parts), axis=0))
    block_out = (resid + mixture.astype(F32)).astype(BF16)
    down_grad = lax.dot_general(
        hidden, grads_rel, (((0,), (0,)), ((), ())), preferred_element_type=F32
    ).reshape(down_weight.shape)
    gate_up_grad = jnp.einsum(
        "td,ten->edn",
        routed_rel,
        joined.reshape(joined.shape[0], local_experts, -1),
        preferred_element_type=F32,
    )

    grad_out = output_grad.astype(F32)
    tail = returned[:, features:].astype(F32)
    grad_gates = tail[:, :expert_count] + tail[:, expert_count : 2 * expert_count]
    grad_gates = jnp.where(named, grad_gates, 0.0)
    grad_router = jnp.where(
        named,
        (grad_gates - jnp.sum(grad_gates * gates, axis=1, keepdims=True)) / chosen_total,
        0.0,
    )
    grad_logits = (
        router * (grad_router - jnp.sum(router * grad_router, axis=1, keepdims=True))
    ).astype(BF16)
    router_grad = jnp.dot(routed_low.T, grad_logits, preferred_element_type=F32)
    grad_routed = returned[:, :features].astype(F32) + jnp.dot(
        grad_logits, router_full.T, preferred_element_type=F32
    )
    grad_resid_norm, mlp_terms = norm_back(resid, mlp_gain_full, grad_routed)
    mlp_gain_grad = jnp.sum(mlp_terms, axis=0)
    grad_resid = grad_out + grad_resid_norm
    grad_attended = grad_resid.astype(BF16)
    output_local = jnp.dot(
        reorder(attention_output, 1).T, grad_attended, preferred_element_type=F32
    ).astype(BF16)
    output_rows = jnp.concatenate(scatter_blocks(output_local), axis=0)
    output_weight_grad = reorder(gather_blocks(output_rows), 0).astype(F32)
    grad_mixed = (
        jnp.dot(grad_attended, output_weight.T, preferred_element_type=F32)
        .astype(BF16)
        .reshape(tokens, key_heads, heads_per_group, HEAD_SIZE)
    )
    probs_again = jnp.exp(score_block() - log_total)
    grad_probs = jnp.einsum("ikgd,jkd->kgij", grad_mixed, all_values, preferred_element_type=F32)
    grad_values = jnp.einsum(
        "kgij,ikgd->jkd", probs_again.astype(BF16), grad_mixed, preferred_element_type=F32
    )
    grad_scores = (
        probs_again * (grad_probs - jnp.sum(probs_again * grad_probs, axis=-1, keepdims=True))
    ).astype(BF16)
    grad_queries = jnp.einsum(
        "kgij,jkd->ikgd", grad_scores, all_keys, preferred_element_type=F32
    ) / math.sqrt(HEAD_SIZE)
    grad_keys = jnp.einsum(
        "kgij,ikgd->jkd", grad_scores, grouped_queries, preferred_element_type=F32
    ) / math.sqrt(HEAD_SIZE)
    grad_query_rot = rotate_back(
        grad_queries.reshape(tokens, query_heads, HEAD_SIZE), cosine, sine_table
    )
    grad_query_raw, query_terms = norm_back(query_raw, query_gain_full, grad_query_rot)
    grad_key_rot = rotate_back(grad_keys, cosine, sine_table)
    grad_key_raw, key_terms = norm_back(key_raw, key_gain_full, grad_key_rot)
    grad_raw = jnp.concatenate(
        [
            grad_query_raw.reshape(tokens, -1).astype(BF16),
            grad_key_raw.reshape(tokens, -1).astype(BF16),
            grad_values.reshape(tokens, -1).astype(BF16),
        ],
        axis=1,
    )
    weights_grad = jnp.dot(normed_rel.T, grad_raw, preferred_element_type=F32).astype(BF16)
    weights_rows = jnp.concatenate(scatter_blocks(weights_grad), axis=0).astype(F32)
    feature_part = lax.dot_general(
        grad_raw, weights_rel, (((1,), (1,)), ((), ())), preferred_element_type=F32
    ).astype(BF16)
    grad_normed = reorder(sum_tp(feature_part), 1).astype(F32)
    grad_input_norm, attn_terms = norm_back(hidden_f, attn_gain_full, grad_normed)
    input_grad = grad_resid + grad_input_norm
    attn_gain_grad = jnp.sum(attn_terms, axis=0)
    small = lax.psum_scatter(
        jnp.concatenate(
            [router_grad, attn_gain_grad[:, None], mlp_gain_grad[:, None]], axis=1
        ).astype(BF16),
        "ep",
        scatter_dimension=0,
        tiled=True,
    ).astype(F32)
    head_grads = jnp.stack(
        [jnp.sum(query_terms, axis=(0, 1)), jnp.sum(key_terms, axis=(0, 1))], axis=1
    )
    head_grads = lax.psum(head_grads.astype(BF16), ("ep", "tp")).astype(F32)
    share = HEAD_SIZE // owners
    head_grads = lax.dynamic_slice_in_dim(head_grads, lax.axis_index("ep") * share, share, 0)
    return (
        block_out,
        input_grad,
        small[:, expert_count],
        head_grads[:, 0],
        head_grads[:, 1],
        weights_rows[:, :query_width],
        weights_rows[:, query_width : query_width + key_width],
        weights_rows[:, query_width + key_width :],
        output_weight_grad,
        small[:, expert_count + 1],
        small[:, :expert_count],
        gate_up_grad,
        down_grad,
    )


def solution(mesh):
    in_specs = (
        P("ep", None),
        P("ep", None),
        P("ep"),
        P("ep"),
        P("ep"),
        P("ep", "tp"),
        P("ep", "tp"),
        P("ep", "tp"),
        P("tp", None),
        P("ep"),
        P("ep", None),
        P("ep", None, "tp"),
        P("ep", "tp", None),
        P("ep", None),
    )
    out_specs = (
        P("ep", None),
        P("ep", None),
        P("ep"),
        P("ep"),
        P("ep"),
        P("ep", "tp"),
        P("ep", "tp"),
        P("ep", "tp"),
        P("tp", None),
        P("ep"),
        P("ep", None),
        P("ep", None, "tp"),
        P("ep", "tp", None),
    )
    return jax.shard_map(shards, mesh=mesh, in_specs=in_specs, out_specs=out_specs, check_vma=False)
```

```python
import functools
import math

import jax
import jax.numpy as jnp
from jax import lax
from jax.experimental import pallas as pl
from jax.experimental.pallas import tpu as pltpu
from jax.sharding import PartitionSpec as P

HEAD_SIZE = 128
TOP = 8
PAIR = 64
LANES = 128

EPSILON = 1e-06
THETA = 1000000.0
F32 = jnp.float32
BF16 = jnp.bfloat16


def norm_rows(value_rows, norm_gain):
    return (
        value_rows
        * lax.rsqrt(jnp.mean(value_rows * value_rows, axis=-1, keepdims=True) + EPSILON)
        * norm_gain
    )


def norm_back(value_rows, norm_gain, upstream):
    scaling = lax.rsqrt(jnp.mean(value_rows * value_rows, axis=-1, keepdims=True) + EPSILON)
    normal = value_rows * scaling
    weighted = upstream * norm_gain
    inward = scaling * (weighted - normal * jnp.mean(weighted * normal, axis=-1, keepdims=True))
    return (inward, upstream * normal)


def rope_tables(positions, head_size):
    halfway = head_size // 2
    inverse = THETA ** (-(jnp.arange(halfway, dtype=jnp.float32) * 2.0) / head_size)
    angles = positions.astype(jnp.float32)[:, None] * inverse[None, :]
    return (jnp.cos(angles)[:, None, :], jnp.sin(angles)[:, None, :])


def rotate(value_rows, cosine, sine_table):
    halfway = value_rows.shape[-1] // 2
    first_half = value_rows[..., :halfway]
    second_half = value_rows[..., halfway:]
    return jnp.concatenate(
        [
            first_half * cosine - second_half * sine_table,
            second_half * cosine + first_half * sine_table,
        ],
        axis=-1,
    )


def rotate_back(upstream, cosine, sine_table):
    halfway = upstream.shape[-1] // 2
    first_half = upstream[..., :halfway]
    second_half = upstream[..., halfway:]
    return jnp.concatenate(
        [
            first_half * cosine + second_half * sine_table,
            second_half * cosine - first_half * sine_table,
        ],
        axis=-1,
    )


SWAPPED = 8


def swap(value, axis, mask):
    count = lax.axis_size(axis)
    return lax.ppermute(value, axis, [(i, i ^ mask) for i in range(count)])


def join(*values):
    return lax.optimization_barrier(values)


ORDER = (0, 2, 4, 6, 1, 3, 5, 7)


def plus(*values):
    total = values[0].astype(F32)
    for v in values[1:]:
        total = total + v.astype(F32)
    return total.astype(BF16)


def absolute():
    return lax.axis_size("ep") > SWAPPED


def gather_hops(value):
    if absolute():
        return [lax.all_gather(value, "ep", axis=0, tiled=True)]
    return [swap(value, "ep", m) for m in ORDER[1:4]]


def gather_near(value, hops):
    if absolute():
        return hops[0][: hops[0].shape[0] // 2]
    return jnp.concatenate([value] + hops, axis=0)


def gather_core(near, hops):
    if absolute():
        return hops[0][hops[0].shape[0] // 2 :]
    return swap(near, "ep", 1)


def scatter_swap(send):
    return send if absolute() else swap(send, "ep", 1)


def scatter_sums(keep, come):
    if absolute():
        return [jnp.concatenate([keep, come], axis=0)]
    rows = keep.shape[0] // 4
    return [
        plus(keep[i * rows : (i + 1) * rows], come[i * rows : (i + 1) * rows]) for i in range(4)
    ]


def scatter_hops(sums):
    if absolute():
        return [lax.psum_scatter(sums[0], "ep", scatter_dimension=0, tiled=True)]
    return [swap(v, "ep", m) for v, m in zip(sums[1:], ORDER[1:4])]


def scatter_total(sums, hops):
    return hops[0] if absolute() else plus(sums[0], *hops)


def chunk_of(value, index):
    rows = value.shape[0] // lax.axis_size("tp")
    return lax.dynamic_slice_in_dim(value, index * rows, rows, 0)


def reduce_hops(value):
    mine = lax.axis_index("tp")
    return [swap(chunk_of(value, mine ^ m), "tp", m) for m in range(1, lax.axis_size("tp"))]


def reduce_total(value, hops):
    return plus(chunk_of(value, lax.axis_index("tp")), *hops)


def spread_hops(chunk):
    return [swap(chunk, "tp", m) for m in range(1, lax.axis_size("tp"))]


def spread_total(chunk, hops):
    mine = lax.axis_index("tp")
    rows = chunk.shape[0]
    result = jnp.zeros(((len(hops) + 1) * rows,) + chunk.shape[1:], chunk.dtype)
    for m, piece in enumerate([chunk] + hops):
        result = lax.dynamic_update_slice_in_dim(result, piece, (mine ^ m) * rows, 0)
    return result


def pick_blocks(value, axis):
    count = lax.axis_size("ep")
    if count > SWAPPED:
        return value
    mine = lax.axis_index("ep")
    size = value.shape[axis] // count
    return jnp.concatenate(
        [lax.dynamic_slice_in_dim(value, (mine ^ m) * size, size, axis) for m in ORDER],
        axis=axis,
    )


def put_blocks(value, axis):
    count = lax.axis_size("ep")
    if count > SWAPPED:
        return value
    mine = lax.axis_index("ep")
    size = value.shape[axis] // count
    place = lambda m: (m // 2 + (m % 2) * (count // 2)) * size
    return jnp.concatenate(
        [lax.dynamic_slice_in_dim(value, place(mine ^ b), size, axis) for b in range(count)],
        axis=axis,
    )


def expert_kernel(
    base_ref, x_ref, g_ref, ids_ref, router_ref, wgu_ref, wd_ref, *rest
):
    dx_ref, joined_ref, hidden_ref = rest[-3:]
    rows = x_ref.shape[0]
    features = x_ref.shape[1]
    expert_count = router_ref.shape[1]
    hidden_count = wd_ref.shape[0]
    extra = dx_ref.shape[1] - features
    base = base_ref[0]
    local = base_ref.shape[0] - 1
    x = x_ref[...]
    logits = jnp.dot(x, router_ref[...], preferred_element_type=F32)
    lane = lax.broadcasted_iota(jnp.int32, (rows, expert_count), 1)
    named = ids_ref[:, 0:1] == lane
    for k in range(1, TOP):
        named = named | (ids_ref[:, k : k + 1] == lane)
    exponent = jnp.exp(logits - jnp.max(logits, axis=1, keepdims=True))
    router = exponent / jnp.sum(exponent, axis=1, keepdims=True)
    chosen = jnp.where(named, router, 0.0)
    gates = chosen / jnp.sum(chosen, axis=1, keepdims=True)
    gate = [
        jnp.sum(jnp.where(lane == base + j, gates, 0.0), axis=1, keepdims=True)
        for j in range(local)
    ]
    left = lax.broadcasted_iota(jnp.int32, (rows, LANES), 1) < PAIR
    per_expert = hidden_count // local // PAIR
    gate_sum = [jnp.zeros((rows, LANES), F32) for _ in range(local)]
    group = 3

    def products(q):
        wide = group * LANES
        act = jnp.dot(
            x, wgu_ref[:, 2 * q * wide : 2 * (q + 1) * wide], preferred_element_type=F32
        )
        back = lax.dot_general(
            g_ref[...],
            wd_ref[q * wide : (q + 1) * wide, :],
            (((1,), (1,)), ((), ())),
            preferred_element_type=F32,
        )
        return act, back

    def elementwise(q, act, back):
        for i in range(group):
            p = q * group + i
            one, two = 2 * p // per_expert, (2 * p + 1) // per_expert
            first = act[:, 2 * i * LANES : (2 * i + 1) * LANES]
            second = act[:, (2 * i + 1) * LANES : (2 * i + 2) * LANES]
            g = jnp.where(left, first, pltpu.roll(second, PAIR, 1))
            u = jnp.where(left, pltpu.roll(first, PAIR, 1), second)
            gh = back[:, i * LANES : (i + 1) * LANES]
            if one == two:
                scale = jnp.broadcast_to(gate[one], (rows, LANES))
            else:
                scale = jnp.where(left, gate[one], gate[two])
            sig = lax.logistic(g)
            silu = g * sig
            hid = silu * u
            product = hid * gh
            if one == two:
                gate_sum[one] += product
            else:
                gate_sum[one] += jnp.where(left, product, 0.0)
                gate_sum[two] += jnp.where(left, 0.0, product)
            hidden_ref[:, p * LANES : (p + 1) * LANES] = (hid * scale).astype(BF16)
            gs = gh * scale
            dg = gs * u * sig * (1.0 + g * (1.0 - sig))
            du = gs * silu
            joined_ref[:, 2 * p * LANES : (2 * p + 1) * LANES] = jnp.where(
                left, dg, pltpu.roll(du, PAIR, 1)
            ).astype(BF16)
            joined_ref[:, (2 * p + 1) * LANES : (2 * p + 2) * LANES] = jnp.where(
                left, pltpu.roll(dg, PAIR, 1), du
            ).astype(BF16)

    count = hidden_count // LANES // group
    waiting = []
    for q in range(count):
        waiting.append((q, *products(q)))
        if q:
            elementwise(*waiting.pop(0))
    elementwise(*waiting.pop(0))
    dx = lax.dot_general(
        joined_ref[...], wgu_ref[...], (((1,), (1,)), ((), ())), preferred_element_type=F32
    )
    dx_ref[:, :features] = dx.astype(BF16)
    wide = lax.broadcasted_iota(jnp.int32, (rows, extra), 1)
    tail = jnp.zeros((rows, extra), F32)
    for j in range(local):
        total = jnp.sum(gate_sum[j], axis=1, keepdims=True)
        high = total.astype(BF16).astype(F32)
        tail = jnp.where(wide == base + j, high, tail)
        tail = jnp.where(wide == expert_count + base + j, total - high, tail)
    dx_ref[:, features:] = tail.astype(BF16)


def run_experts(x, g, ids, router, wgu, wd, local, piece, pieces, earlier=None):
    tokens, features = x.shape
    tile = 256
    steps = tokens // tile
    expert_count = router.shape[1]
    extra = -(-2 * expert_count // LANES) * LANES
    base = jnp.full((local + 1,), lax.axis_index("ep") * local, jnp.int32)
    whole = lambda v: pl.BlockSpec(v.shape, lambda i, s: (0, 0), pipeline_mode=pl.Buffered(1))
    by_rows = lambda width, skip=0: pl.BlockSpec((tile, width), lambda i, s: (i + skip, 0))
    in_specs = [
        by_rows(features),
        by_rows(features),
        by_rows(TOP),
        whole(router),
        whole(wgu),
        whole(wd),
    ]
    operands = [base, x, g, ids, router, wgu, wd]
    aliases = {}
    if earlier:
        in_specs += [pl.BlockSpec(memory_space=pl.ANY)] * 2
        operands += list(earlier)
        aliases = {7: 1, 8: 2}
    return pl.pallas_call(
        expert_kernel,
        grid_spec=pltpu.PrefetchScalarGridSpec(
            num_scalar_prefetch=1,
            grid=(steps,),
            in_specs=in_specs,
            out_specs=[
                by_rows(features + extra),
                by_rows(wgu.shape[1], piece * steps),
                by_rows(wd.shape[0], piece * steps),
            ],
        ),
        out_shape=[
            jax.ShapeDtypeStruct((tokens, features + extra), BF16),
            jax.ShapeDtypeStruct((pieces * tokens, wgu.shape[1]), BF16),
            jax.ShapeDtypeStruct((pieces * tokens, wd.shape[0]), BF16),
        ],
        input_output_aliases=aliases,
        compiler_params=pltpu.CompilerParams(vmem_limit_bytes=36 * 1024 * 1024),
        cost_estimate=pl.CostEstimate(
            flops=2 * tokens * features * (2 * wgu.shape[1] + wd.shape[0]),
            bytes_accessed=2 * tokens * features * 3 + 2 * features * 2 * wgu.shape[1],
            transcendentals=tokens * wd.shape[0],
        ),
    )(*operands)


def rows_product(pieces, whole):
    rows = pieces[0].shape[0]
    total = None
    for i, v in enumerate(pieces):
        part = lax.dot_general(
            v[...],
            whole[i * rows : (i + 1) * rows, :],
            (((0,), (0,)), ((), ())),
            preferred_element_type=F32,
        )
        total = part if total is None else total + part
    return total


def gate_up_kernel(*refs):
    *pieces, joined_ref, result_ref = refs
    total = rows_product(pieces, joined_ref)
    width = result_ref.shape[2]
    for e in range(result_ref.shape[0]):
        result_ref[e] = total[:, e * width : (e + 1) * width]


def gate_up_product(pieces, joined, shape):
    rows, features = pieces[0].shape
    tile = 256
    return pl.pallas_call(
        gate_up_kernel,
        grid=(features // tile,),
        in_specs=[pl.BlockSpec((rows, tile), lambda i: (0, i)) for _ in pieces]
        + [pl.BlockSpec(joined.shape, lambda i: (0, 0), pipeline_mode=pl.Buffered(1))],
        out_specs=pl.BlockSpec((shape[0], tile, shape[2]), lambda i: (0, i, 0)),
        out_shape=jax.ShapeDtypeStruct(shape, F32),
        compiler_params=pltpu.CompilerParams(vmem_limit_bytes=56 * 1024 * 1024),
        cost_estimate=pl.CostEstimate(
            flops=2 * joined.shape[0] * features * joined.shape[1],
            bytes_accessed=2 * joined.shape[0] * features + 2 * joined.size + 4 * math.prod(shape),
            transcendentals=0,
        ),
    )(*pieces, joined)


def down_kernel(hidden_ref, *refs):
    *pieces, result_ref = refs
    rows = pieces[0].shape[0]
    total = None
    for i, v in enumerate(pieces):
        part = lax.dot_general(
            hidden_ref[i * rows : (i + 1) * rows, :],
            v[...],
            (((0,), (0,)), ((), ())),
            preferred_element_type=F32,
        )
        total = part if total is None else total + part
    result_ref[...] = total


def down_product(hidden, pieces):
    rows, features = pieces[0].shape
    tile = 256
    whole = pl.BlockSpec((rows, features), lambda i: (0, 0), pipeline_mode=pl.Buffered(1))
    return pl.pallas_call(
        down_kernel,
        grid=(hidden.shape[1] // tile,),
        in_specs=[pl.BlockSpec((hidden.shape[0], tile), lambda i: (0, i))] + [whole] * len(pieces),
        out_specs=pl.BlockSpec((tile, features), lambda i: (i, 0)),
        out_shape=jax.ShapeDtypeStruct((hidden.shape[1], features), F32),
        compiler_params=pltpu.CompilerParams(vmem_limit_bytes=56 * 1024 * 1024),
        cost_estimate=pl.CostEstimate(
            flops=2 * hidden.size * features,
            bytes_accessed=2 * hidden.size
            + 2 * hidden.shape[0] * features
            + 4 * hidden.shape[1] * features,
            transcendentals=0,
        ),
    )(hidden, *pieces)


def shards(
    hidden_in,
    expert_ids,
    attention_gain,
    query_gain,
    key_gain,
    query_weight,
    key_matrix,
    value_matrix,
    output_weight,
    expert_gain,
    router_weight,
    gate_up_weight,
    down_weight,
    output_grad,
):
    tokens, features = hidden_in.shape
    owners = lax.axis_size("ep")
    local_experts = gate_up_weight.shape[0]
    expert_count = local_experts * owners
    everyone = lambda v: lax.all_gather(v, "ep", axis=0, tiled=True)

    rows_a = tokens // 2
    halves = lambda v: (v[:rows_a], v[rows_a:])

    weights = jnp.concatenate([query_weight, key_matrix, value_matrix], axis=1)
    hops = gather_hops(weights)
    head_share = query_gain.shape[0]
    head_gains = jnp.pad(
        jnp.stack([query_gain, key_gain], axis=1),
        ((0, router_weight.shape[0] - head_share), (0, 0)),
    )
    packed = everyone(
        jnp.concatenate(
            [router_weight, attention_gain[:, None], expert_gain[:, None], head_gains], axis=1
        )
    )
    router_full = packed[:, :expert_count]
    attn_gain_full = packed[:, expert_count].astype(F32)
    mlp_gain_full = packed[:, expert_count + 1].astype(F32)
    head_gains = (
        packed[:, expert_count + 2 :]
        .reshape(owners, -1, 2)[:, :head_share]
        .reshape(HEAD_SIZE, 2)
        .astype(F32)
    )
    query_gain_full = head_gains[:, 0]
    key_gain_full = head_gains[:, 1]
    wgu = gate_up_weight.transpose(1, 0, 2).reshape(features, -1)
    wd = down_weight.reshape(-1, features)
    hidden_f = hidden_in.astype(F32)
    normed_low = norm_rows(hidden_f, attn_gain_full).astype(BF16)
    normed_rel = pick_blocks(normed_low, 1)
    positions = jnp.arange(tokens, dtype=jnp.int32)
    cosine, sine_table = rope_tables(positions, HEAD_SIZE)
    hops, normed_rel, wgu, cosine, sine_table, router_full, output_grad = join(
        hops, normed_rel, wgu, cosine, sine_table, router_full, output_grad
    )

    near = gather_near(weights, hops)
    weights_rel = [near, gather_core(near, hops)]
    grad_halves = halves(output_grad)
    grad_hops = [gather_hops(v) for v in grad_halves]
    query_width = query_weight.shape[1]
    key_width = key_matrix.shape[1]
    query_heads = query_width // HEAD_SIZE
    key_heads = key_width // HEAD_SIZE
    heads_per_group = query_heads // key_heads
    split = features // 2
    raw = jnp.dot(normed_rel[:, :split], weights_rel[0], preferred_element_type=F32) + jnp.dot(
        normed_rel[:, split:], weights_rel[1], preferred_element_type=F32
    )
    query_raw = raw[:, :query_width].reshape(tokens, query_heads, HEAD_SIZE)
    key_raw = raw[:, query_width : query_width + key_width].reshape(tokens, key_heads, HEAD_SIZE)
    value_low = raw[:, query_width + key_width :].astype(BF16)
    query_low = rotate(norm_rows(query_raw, query_gain_full), cosine, sine_table).astype(BF16)
    all_keys = rotate(norm_rows(key_raw, key_gain_full), cosine, sine_table).astype(BF16)
    all_values = value_low.reshape(tokens, key_heads, HEAD_SIZE)
    allowed = jnp.arange(tokens)[None, :] <= jnp.arange(tokens)[:, None]
    grouped_queries = query_low.reshape(tokens, key_heads, heads_per_group, HEAD_SIZE)

    def score_block():
        raw_scores = jnp.einsum(
            "ikgd,jkd->kgij", grouped_queries, all_keys, preferred_element_type=F32
        ) / math.sqrt(HEAD_SIZE)
        return jnp.where(allowed, raw_scores, -jnp.inf)

    scores = score_block()
    row_max = jnp.max(scores, axis=-1, keepdims=True)
    exps = jnp.exp(scores - row_max)
    row_total = jnp.sum(exps, axis=-1, keepdims=True)
    probs = exps / row_total
    log_total = row_max + jnp.log(row_total)
    attention_output = (
        jnp.einsum("kgij,jkd->ikgd", probs.astype(BF16), all_values, preferred_element_type=F32)
        .astype(BF16)
        .reshape(tokens, query_heads * HEAD_SIZE)
    )
    head_parts = [
        jnp.dot(v, output_weight, preferred_element_type=F32).astype(BF16)
        for v in halves(attention_output)
    ]
    head_parts, grad_hops[0] = join(head_parts, grad_hops[0])

    grad_near = [gather_near(grad_halves[0], grad_hops[0])]
    grad_core = [gather_core(grad_near[0], grad_hops[0])]
    ids_hops = gather_hops(expert_ids)
    hops = reduce_hops(head_parts[0])
    hops, ids_hops = join(hops, ids_hops)

    ids_near = gather_near(expert_ids, ids_hops)
    ids_core = gather_core(ids_near, ids_hops)
    chunk = reduce_total(head_parts[0], hops)
    hops_b, hops, grad_core[0], grad_hops[1], ids_core = join(
        reduce_hops(head_parts[1]), spread_hops(chunk), grad_core[0], grad_hops[1], ids_core
    )

    attended = [spread_total(chunk, hops)]
    chunk = reduce_total(head_parts[1], hops_b)
    hops = spread_hops(chunk)
    grad_near.append(gather_near(grad_halves[1], grad_hops[1]))
    grad_core.append(gather_core(grad_near[1], grad_hops[1]))
    resid_halves = [hidden_f[:rows_a] + attended[0].astype(F32)]
    routed_halves = [norm_rows(resid_halves[0], mlp_gain_full).astype(BF16)]
    hops_a, hops, grad_core[1] = join(gather_hops(routed_halves[0]), hops, grad_core[1])

    attended.append(spread_total(chunk, hops))
    resid_halves.append(hidden_f[rows_a:] + attended[1].astype(F32))
    routed_halves.append(norm_rows(resid_halves[1], mlp_gain_full).astype(BF16))
    near_a = gather_near(routed_halves[0], hops_a)
    core_a = gather_core(near_a, hops_a)
    hops_b = gather_hops(routed_halves[1])
    grad_pieces = [grad_near[0], grad_core[0], grad_near[1], grad_core[1]]
    piece_rows = near_a.shape[0]
    ids_pieces = [
        v.reshape(-1, 2, rows_a, TOP)[:, h].reshape(piece_rows, TOP)
        for h in range(2)
        for v in (ids_near, ids_core)
    ]

    def experts(piece, x, kept=None):
        return run_experts(
            x,
            grad_pieces[piece],
            ids_pieces[piece],
            router_full,
            wgu,
            wd,
            local_experts,
            piece,
            4,
            kept,
        )

    keep_a, *kept = experts(0, near_a)
    send_a, *kept = experts(1, core_a, kept)
    hops_b, send_a, kept = join(hops_b, send_a, kept)

    near_b = gather_near(routed_halves[1], hops_b)
    core_b = gather_core(near_b, hops_b)
    come = scatter_swap(send_a)
    keep_b, *kept = experts(2, near_b, kept)
    come, core_b, keep_b, kept = join(come, core_b, keep_b, kept)

    sums_a = scatter_sums(keep_a, come)
    hops_a = scatter_hops(sums_a)
    send_b, *kept = experts(3, core_b, kept)
    hops_a, send_b, kept = join(hops_a, send_b, kept)
    joined, hidden = kept
    routed_pieces = [near_a, core_a, near_b, core_b]
    resid = jnp.concatenate(resid_halves, axis=0)
    routed_low = jnp.concatenate(routed_halves, axis=0)
    logits = jnp.dot(routed_low, router_full, preferred_element_type=F32)
    logit_max = jnp.max(logits, axis=-1, keepdims=True)
    exponent = jnp.exp(logits - logit_max)
    router = exponent / jnp.sum(exponent, axis=-1, keepdims=True)
    every_expert = jnp.arange(expert_count, dtype=jnp.int32)
    named = jnp.any(expert_ids[:, :, None] == every_expert[None, None, :], axis=1)
    chosen = jnp.where(named, router, 0.0)
    chosen_total = jnp.sum(chosen, axis=1, keepdims=True)
    gates = chosen / chosen_total

    come = scatter_swap(send_b)
    total_a = scatter_total(sums_a, hops_a)
    hops = reduce_hops(total_a)
    mixture_parts = [
        jnp.dot(
            hidden[i * piece_rows : (i + 1) * piece_rows], wd, preferred_element_type=F32
        ).astype(BF16)
        for i in (1, 3, 0, 2)
    ]
    come, hops, mixture_parts = join(come, hops, mixture_parts)

    sums_b = scatter_sums(keep_b, come)
    hops_b = scatter_hops(sums_b)
    chunk = reduce_total(total_a, hops)
    hops_a = spread_hops(chunk)
    mixture_come = [scatter_swap(v) for v in mixture_parts[:2]]
    hops_b, hops_a, mixture_come = join(hops_b, hops_a, mixture_come)

    returned = [spread_total(chunk, hops_a)]
    total_b = scatter_total(sums_b, hops_b)
    hops = reduce_hops(total_b)
    mixture_sums = [scatter_sums(k, c) for k, c in zip(mixture_parts[2:], mixture_come)]
    mixture_hops = [scatter_hops(v) for v in mixture_sums]
    (hops,) = join(hops)
    chunk = reduce_total(total_b, hops)
    hops, mixture_hops[0] = join(spread_hops(chunk), mixture_hops[0])

    returned.append(spread_total(chunk, hops))
    returned = jnp.concatenate(returned, axis=0)
    grad_out = output_grad.astype(F32)
    tail = returned[:, features:].astype(F32)
    grad_gates = tail[:, :expert_count] + tail[:, expert_count : 2 * expert_count]
    grad_gates = jnp.where(named, grad_gates, 0.0)
    grad_router = jnp.where(
        named,
        (grad_gates - jnp.sum(grad_gates * gates, axis=1, keepdims=True)) / chosen_total,
        0.0,
    )
    grad_logits = (
        router * (grad_router - jnp.sum(router * grad_router, axis=1, keepdims=True))
    ).astype(BF16)
    router_grad = jnp.dot(routed_low.T, grad_logits, preferred_element_type=F32)
    grad_routed = returned[:, :features].astype(F32) + jnp.dot(
        grad_logits, router_full.T, preferred_element_type=F32
    )
    grad_resid_norm, mlp_terms = norm_back(resid, mlp_gain_full, grad_routed)
    mlp_gain_grad = jnp.sum(mlp_terms, axis=0)
    grad_resid = grad_out + grad_resid_norm
    grad_attended = grad_resid.astype(BF16)
    mixed_rel = pick_blocks(attention_output, 1)
    output_local = lax.dot_general(
        mixed_rel, grad_attended, (((0,), (0,)), ((), ())), preferred_element_type=F32
    ).astype(BF16)
    output_half = output_local.shape[0] // 2
    output_local, grad_attended, mixture_hops[1] = join(
        output_local, grad_attended, mixture_hops[1]
    )

    come = scatter_swap(output_local[output_half:])
    mixture = jnp.concatenate(
        [scatter_total(v, h) for v, h in zip(mixture_sums, mixture_hops)], axis=0
    )
    grad_mixed = (
        jnp.dot(grad_attended, output_weight.T, preferred_element_type=F32)
        .astype(BF16)
        .reshape(tokens, key_heads, heads_per_group, HEAD_SIZE)
    )
    grad_mixed, come = join(grad_mixed, come)

    output_sums = scatter_sums(output_local[:output_half], come)
    output_hops = scatter_hops(output_sums)
    mixture_hops = reduce_hops(mixture)
    probs_again = jnp.exp(score_block() - log_total)
    grad_probs = jnp.einsum("ikgd,jkd->kgij", grad_mixed, all_values, preferred_element_type=F32)
    grad_values = jnp.einsum(
        "kgij,ikgd->jkd", probs_again.astype(BF16), grad_mixed, preferred_element_type=F32
    )
    grad_scores = (
        probs_again * (grad_probs - jnp.sum(probs_again * grad_probs, axis=-1, keepdims=True))
    ).astype(BF16)
    grad_queries = jnp.einsum(
        "kgij,jkd->ikgd", grad_scores, all_keys, preferred_element_type=F32
    ) / math.sqrt(HEAD_SIZE)
    grad_keys = jnp.einsum(
        "kgij,ikgd->jkd", grad_scores, grouped_queries, preferred_element_type=F32
    ) / math.sqrt(HEAD_SIZE)
    grad_query_rot = rotate_back(
        grad_queries.reshape(tokens, query_heads, HEAD_SIZE), cosine, sine_table
    )
    grad_query_raw, query_terms = norm_back(query_raw, query_gain_full, grad_query_rot)
    grad_key_rot = rotate_back(grad_keys, cosine, sine_table)
    grad_key_raw, key_terms = norm_back(key_raw, key_gain_full, grad_key_rot)
    grad_raw = jnp.concatenate(
        [
            grad_query_raw.reshape(tokens, -1).astype(BF16),
            grad_key_raw.reshape(tokens, -1).astype(BF16),
            grad_values.reshape(tokens, -1).astype(BF16),
        ],
        axis=1,
    )
    over_columns = (((1,), (1,)), ((), ()))
    feature_part = jnp.concatenate(
        [
            lax.dot_general(grad_raw, w, over_columns, preferred_element_type=F32).astype(BF16)
            for w in weights_rel
        ]
        + [jnp.sum(query_terms, axis=1).astype(BF16), jnp.sum(key_terms, axis=1).astype(BF16)],
        axis=1,
    )
    by_feature = jnp.concatenate([router_grad, mlp_gain_grad[:, None]], axis=1).astype(BF16)
    by_feature = jnp.pad(by_feature, ((0, 0), (0, -by_feature.shape[1] % LANES)))
    weights_grad = jnp.concatenate(
        [
            lax.dot_general(
                normed_rel, grad_raw, (((0,), (0,)), ((), ())), preferred_element_type=F32
            ).astype(BF16),
            pick_blocks(by_feature, 0),
        ],
        axis=1,
    )
    feature_part, weights_grad, output_hops, mixture_hops = join(
        feature_part, weights_grad, output_hops, mixture_hops
    )

    come = scatter_swap(weights_grad[split:])
    hops = reduce_hops(feature_part)
    output_share = scatter_total(output_sums, output_hops)
    output_hops = gather_hops(output_share)
    mixture_chunk = reduce_total(mixture, mixture_hops)
    come, hops = join(come, hops)

    weights_sums = scatter_sums(weights_grad[:split], come)
    weights_hops = scatter_hops(weights_sums)
    chunk = reduce_total(feature_part, hops)
    hops = spread_hops(chunk)
    last_joined, last_hidden, chunk = join(joined, hidden, chunk)
    down_grad = down_product(last_hidden, grad_pieces).reshape(down_weight.shape)
    hops, output_hops, down_grad = join(hops, output_hops, down_grad)

    near = gather_near(output_share, output_hops)
    output_weight_grad = put_blocks(
        jnp.concatenate([near, gather_core(near, output_hops)], axis=0), 0
    ).astype(F32)
    mixture_hops = spread_hops(mixture_chunk)
    total = spread_total(chunk, hops)
    grad_normed = put_blocks(total[:, :features], 1).astype(F32)
    head_grads = jnp.sum(total[:, features:].astype(F32), axis=0)
    grad_input_norm, attn_terms = norm_back(hidden_f, attn_gain_full, grad_normed)
    input_grad = grad_resid + grad_input_norm
    late = jnp.concatenate([jnp.sum(attn_terms, axis=0), head_grads])
    weights_hops, late, last_joined = join(weights_hops, late, last_joined)
    late = lax.psum(late, "ep")
    weights_rows = scatter_total(weights_sums, weights_hops).astype(F32)
    early = weights_rows[:, query_width + 2 * key_width :]
    gate_up_grad = gate_up_product(routed_pieces, last_joined, gate_up_weight.shape)
    mixture = spread_total(mixture_chunk, mixture_hops)
    block_out = (resid + mixture.astype(F32)).astype(BF16)
    mine = lax.axis_index("ep")
    own = lambda start, size: lax.dynamic_slice_in_dim(
        late, start + mine * (size // owners), size // owners, 0
    )
    return (
        block_out,
        input_grad,
        own(0, features),
        own(features, HEAD_SIZE),
        own(features + HEAD_SIZE, HEAD_SIZE),
        weights_rows[:, :query_width],
        weights_rows[:, query_width : query_width + key_width],
        weights_rows[:, query_width + key_width : query_width + 2 * key_width],
        output_weight_grad,
        early[:, expert_count],
        early[:, :expert_count],
        gate_up_grad,
        down_grad,
    )


def solution(mesh):
    in_specs = (
        P("ep", None),
        P("ep", None),
        P("ep"),
        P("ep"),
        P("ep"),
        P("ep", "tp"),
        P("ep", "tp"),
        P("ep", "tp"),
        P("tp", None),
        P("ep"),
        P("ep", None),
        P("ep", None, "tp"),
        P("ep", "tp", None),
        P("ep", None),
    )
    out_specs = (
        P("ep", None),
        P("ep", None),
        P("ep"),
        P("ep"),
        P("ep"),
        P("ep", "tp"),
        P("ep", "tp"),
        P("ep", "tp"),
        P("tp", None),
        P("ep"),
        P("ep", None),
        P("ep", None, "tp"),
        P("ep", "tp", None),
    )
    return jax.shard_map(shards, mesh=mesh, in_specs=in_specs, out_specs=out_specs, check_vma=False)
```

```python
import functools
import math

import jax
import jax.numpy as jnp
from jax import lax
from jax.experimental import pallas as pl
from jax.experimental.pallas import tpu as pltpu
from jax.sharding import PartitionSpec as P

HEAD_SIZE = 128
TOP = 8
PAIR = 64
LANES = 128

EPSILON = 1e-06
THETA = 1000000.0
F32 = jnp.float32
BF16 = jnp.bfloat16


def norm_rows(value_rows, norm_gain):
    return (
        value_rows
        * lax.rsqrt(jnp.mean(value_rows * value_rows, axis=-1, keepdims=True) + EPSILON)
        * norm_gain
    )


def norm_back(value_rows, norm_gain, upstream):
    scaling = lax.rsqrt(jnp.mean(value_rows * value_rows, axis=-1, keepdims=True) + EPSILON)
    normal = value_rows * scaling
    weighted = upstream * norm_gain
    inward = scaling * (weighted - normal * jnp.mean(weighted * normal, axis=-1, keepdims=True))
    return (inward, upstream * normal)


def rope_tables(positions, head_size):
    halfway = head_size // 2
    inverse = THETA ** (-(jnp.arange(halfway, dtype=jnp.float32) * 2.0) / head_size)
    angles = positions.astype(jnp.float32)[:, None] * inverse[None, :]
    cosine, sine = jnp.cos(angles), jnp.sin(angles)
    return (
        jnp.concatenate([cosine, cosine], axis=1),
        jnp.concatenate([-sine, sine], axis=1),
    )


SWAPPED = 8


def swap(value, axis, mask):
    count = lax.axis_size(axis)
    return lax.ppermute(value, axis, [(i, i ^ mask) for i in range(count)])


def join(*values):
    return lax.optimization_barrier(values)


ORDER = (0, 2, 4, 6, 1, 3, 5, 7)


def plus(*values):
    total = values[0].astype(F32)
    for v in values[1:]:
        total = total + v.astype(F32)
    return total.astype(values[0].dtype)


def absolute():
    return lax.axis_size("ep") > SWAPPED


def gather_hops(value):
    if absolute():
        return [lax.all_gather(value, "ep", axis=0, tiled=True)]
    return [swap(value, "ep", m) for m in ORDER[1:4]]


def gather_near(value, hops):
    if absolute():
        return hops[0][: hops[0].shape[0] // 2]
    return jnp.concatenate([value] + hops, axis=0)


def gather_core(near, hops):
    if absolute():
        return hops[0][hops[0].shape[0] // 2 :]
    return swap(near, "ep", 1)


def scatter_swap(send):
    return send if absolute() else swap(send, "ep", 1)


def scatter_sums(keep, come):
    if absolute():
        return [jnp.concatenate([keep, come], axis=0)]
    rows = keep.shape[0] // 4
    return [
        plus(keep[i * rows : (i + 1) * rows], come[i * rows : (i + 1) * rows]) for i in range(4)
    ]


def scatter_hops(sums):
    if absolute():
        return [lax.psum_scatter(sums[0], "ep", scatter_dimension=0, tiled=True)]
    return [swap(v, "ep", m) for v, m in zip(sums[1:], ORDER[1:4])]


def scatter_total(sums, hops):
    return hops[0] if absolute() else plus(sums[0], *hops)


def chunk_of(value, index):
    rows = value.shape[0] // lax.axis_size("tp")
    return lax.dynamic_slice_in_dim(value, index * rows, rows, 0)


def reduce_hops(value):
    mine = lax.axis_index("tp")
    return [swap(chunk_of(value, mine ^ m), "tp", m) for m in range(1, lax.axis_size("tp"))]


def reduce_total(value, hops):
    return plus(chunk_of(value, lax.axis_index("tp")), *hops)


def spread_hops(chunk):
    return [swap(chunk, "tp", m) for m in range(1, lax.axis_size("tp"))]


def spread_total(chunk, hops):
    mine = lax.axis_index("tp")
    rows = chunk.shape[0]
    result = jnp.zeros(((len(hops) + 1) * rows,) + chunk.shape[1:], chunk.dtype)
    for m, piece in enumerate([chunk] + hops):
        result = lax.dynamic_update_slice_in_dim(result, piece, (mine ^ m) * rows, 0)
    return result


def places():
    if absolute():
        return [jnp.int32(b) for b in range(lax.axis_size("ep"))]
    return [lax.axis_index("ep") ^ m for m in ORDER]


def pick_blocks(value, axis):
    count = lax.axis_size("ep")
    if count > SWAPPED:
        return value
    mine = lax.axis_index("ep")
    size = value.shape[axis] // count
    return jnp.concatenate(
        [lax.dynamic_slice_in_dim(value, (mine ^ m) * size, size, axis) for m in ORDER],
        axis=axis,
    )


def put_blocks(value, axis):
    count = lax.axis_size("ep")
    if count > SWAPPED:
        return value
    mine = lax.axis_index("ep")
    size = value.shape[axis] // count
    place = lambda m: (m // 2 + (m % 2) * (count // 2)) * size
    return jnp.concatenate(
        [lax.dynamic_slice_in_dim(value, place(mine ^ b), size, axis) for b in range(count)],
        axis=axis,
    )


def expert_kernel(
    local, place_ref, x_ref, g0_ref, g1_ref, ids0_ref, ids1_ref, router_ref, wgu_ref, wd_ref,
    dx_ref, joined_ref, hidden_ref,
):
    rows = x_ref.shape[0]
    features = x_ref.shape[1]
    expert_count = router_ref.shape[1]
    hidden_count = wd_ref.shape[0]
    extra = dx_ref.shape[1] - features
    base = place_ref[0]
    x = x_ref[...]
    upstream = jnp.concatenate([g0_ref[...], g1_ref[...]], axis=0)
    ids = jnp.concatenate([ids0_ref[...], ids1_ref[...]], axis=0)
    logits = jnp.dot(x, router_ref[...], preferred_element_type=F32)
    lane = lax.broadcasted_iota(jnp.int32, (rows, expert_count), 1)
    named = ids[:, 0:1] == lane
    for k in range(1, TOP):
        named = named | (ids[:, k : k + 1] == lane)
    exponent = jnp.exp(logits - jnp.max(logits, axis=1, keepdims=True))
    router = exponent / jnp.sum(exponent, axis=1, keepdims=True)
    chosen = jnp.where(named, router, 0.0)
    gates = chosen / jnp.sum(chosen, axis=1, keepdims=True)
    gate = [
        jnp.sum(jnp.where(lane == base + j, gates, 0.0), axis=1, keepdims=True)
        for j in range(local)
    ]
    left = lax.broadcasted_iota(jnp.int32, (rows, LANES), 1) < PAIR
    per_expert = hidden_count // local // PAIR
    gate_sum = [jnp.zeros((rows, LANES), F32) for _ in range(local)]
    group = 3

    def products(q):
        wide = group * LANES
        act = jnp.dot(
            x, wgu_ref[:, 2 * q * wide : 2 * (q + 1) * wide], preferred_element_type=F32
        )
        back = lax.dot_general(
            upstream,
            wd_ref[q * wide : (q + 1) * wide, :],
            (((1,), (1,)), ((), ())),
            preferred_element_type=F32,
        )
        return act, back

    def elementwise(q, act, back):
        for i in range(group):
            p = q * group + i
            one, two = 2 * p // per_expert, (2 * p + 1) // per_expert
            first = act[:, 2 * i * LANES : (2 * i + 1) * LANES]
            second = act[:, (2 * i + 1) * LANES : (2 * i + 2) * LANES]
            g = jnp.where(left, first, pltpu.roll(second, PAIR, 1))
            u = jnp.where(left, pltpu.roll(first, PAIR, 1), second)
            gh = back[:, i * LANES : (i + 1) * LANES]
            if one == two:
                scale = jnp.broadcast_to(gate[one], (rows, LANES))
            else:
                scale = jnp.where(left, gate[one], gate[two])
            sig = lax.logistic(g)
            silu = g * sig
            hid = silu * u
            product = hid * gh
            if one == two:
                gate_sum[one] += product
            else:
                gate_sum[one] += jnp.where(left, product, 0.0)
                gate_sum[two] += jnp.where(left, 0.0, product)
            hidden_ref[:, p * LANES : (p + 1) * LANES] = (hid * scale).astype(BF16)
            gs = gh * scale
            dg = gs * u * sig * (1.0 + g * (1.0 - sig))
            du = gs * silu
            joined_ref[:, 2 * p * LANES : (2 * p + 1) * LANES] = jnp.where(
                left, dg, pltpu.roll(du, PAIR, 1)
            ).astype(BF16)
            joined_ref[:, (2 * p + 1) * LANES : (2 * p + 2) * LANES] = jnp.where(
                left, pltpu.roll(dg, PAIR, 1), du
            ).astype(BF16)

    count = hidden_count // LANES // group
    waiting = []
    for q in range(count):
        waiting.append((q, *products(q)))
        if q:
            elementwise(*waiting.pop(0))
    elementwise(*waiting.pop(0))
    dx = lax.dot_general(
        joined_ref[...], wgu_ref[...], (((1,), (1,)), ((), ())), preferred_element_type=F32
    )
    dx_ref[:, :features] = dx.astype(BF16)
    wide = lax.broadcasted_iota(jnp.int32, (rows, extra), 1)
    tail = jnp.zeros((rows, extra), F32)
    for j in range(local):
        total = jnp.sum(gate_sum[j], axis=1, keepdims=True)
        high = total.astype(BF16).astype(F32)
        tail = jnp.where(wide == base + j, high, tail)
        tail = jnp.where(wide == expert_count + base + j, total - high, tail)
    dx_ref[:, features:] = tail.astype(BF16)


def run_experts(x, g, ids, where, router, wgu, wd, local):
    tokens, features = x.shape
    tile = 256
    block = tokens // len(where)
    steps = tokens // tile
    expert_count = router.shape[1]
    extra = -(-2 * expert_count // LANES) * LANES
    place = jnp.stack([lax.axis_index("ep") * local] + list(where)).astype(jnp.int32)
    found = lambda width, j: pl.BlockSpec((block, width), lambda i, s: (s[1 + 2 * i + j], 0))
    whole = lambda v: pl.BlockSpec(v.shape, lambda i, s: (0, 0), pipeline_mode=pl.Buffered(1))
    by_rows = lambda width: pl.BlockSpec((tile, width), lambda i, s: (i, 0))
    in_specs = [
        by_rows(features),
        found(features, 0),
        found(features, 1),
        found(TOP, 0),
        found(TOP, 1),
        whole(router),
        whole(wgu),
        whole(wd),
    ]
    operands = [place, x, g, g, ids, ids, router, wgu, wd]
    return pl.pallas_call(
        functools.partial(expert_kernel, local),
        grid_spec=pltpu.PrefetchScalarGridSpec(
            num_scalar_prefetch=1,
            grid=(steps,),
            in_specs=in_specs,
            out_specs=[
                by_rows(features + extra),
                by_rows(wgu.shape[1]),
                by_rows(wd.shape[0]),
            ],
        ),
        out_shape=[
            jax.ShapeDtypeStruct((tokens, features + extra), BF16),
            jax.ShapeDtypeStruct((tokens, wgu.shape[1]), BF16),
            jax.ShapeDtypeStruct((tokens, wd.shape[0]), BF16),
        ],
        compiler_params=pltpu.CompilerParams(vmem_limit_bytes=32 * 1024 * 1024),
        cost_estimate=pl.CostEstimate(
            flops=2 * tokens * features * (2 * wgu.shape[1] + wd.shape[0]),
            bytes_accessed=2 * tokens * features * 3 + 2 * features * 2 * wgu.shape[1],
            transcendentals=tokens * wd.shape[0],
        ),
    )(*operands)


def gate_up_kernel(*refs):
    *operands, result_ref = refs
    count = len(operands) // 2
    total = None
    for x_ref, joined_ref in zip(operands[:count], operands[count:]):
        part = lax.dot_general(
            x_ref[...], joined_ref[...], (((0,), (0,)), ((), ())), preferred_element_type=F32
        )
        total = part if total is None else total + part
    width = result_ref.shape[2]
    for e in range(result_ref.shape[0]):
        result_ref[e] = total[:, e * width : (e + 1) * width]


def gate_up_product(pieces, joined, shape):
    rows, features = pieces[0].shape
    width = joined[0].shape[1]
    tile = 256
    whole = pl.BlockSpec((rows, width), lambda i: (0, 0), pipeline_mode=pl.Buffered(1))
    return pl.pallas_call(
        gate_up_kernel,
        grid=(features // tile,),
        in_specs=[pl.BlockSpec((rows, tile), lambda i: (0, i)) for _ in pieces]
        + [whole for _ in joined],
        out_specs=pl.BlockSpec((shape[0], tile, shape[2]), lambda i: (0, i, 0)),
        out_shape=jax.ShapeDtypeStruct(shape, F32),
        compiler_params=pltpu.CompilerParams(vmem_limit_bytes=56 * 1024 * 1024),
        cost_estimate=pl.CostEstimate(
            flops=2 * len(pieces) * rows * features * width,
            bytes_accessed=2 * len(pieces) * rows * (features + width) + 4 * math.prod(shape),
            transcendentals=0,
        ),
    )(*pieces, *joined)


def down_kernel(place_ref, *refs):
    *pieces, g_ref, result_ref, sorted_ref = refs
    blocks = place_ref.shape[0] // len(pieces)
    block = pieces[0].shape[0] // blocks
    for i, hidden_ref in enumerate(pieces):
        for k in range(blocks):
            start = pl.multiple_of(place_ref[i * blocks + k] * block, block)
            sorted_ref[pl.ds(start, block), :] = hidden_ref[k * block : (k + 1) * block, :]
    result_ref[...] = lax.dot_general(
        sorted_ref[...], g_ref[...], (((0,), (0,)), ((), ())), preferred_element_type=F32
    )


def down_product(hidden, g, where):
    rows, features = g.shape
    width = hidden[0].shape[1]
    tile = 256
    return pl.pallas_call(
        down_kernel,
        grid_spec=pltpu.PrefetchScalarGridSpec(
            num_scalar_prefetch=1,
            grid=(width // tile,),
            in_specs=[pl.BlockSpec((v.shape[0], tile), lambda i, s: (0, i)) for v in hidden]
            + [pl.BlockSpec((rows, features), lambda i, s: (0, 0), pipeline_mode=pl.Buffered(1))],
            out_specs=pl.BlockSpec((tile, features), lambda i, s: (i, 0)),
            scratch_shapes=[pltpu.VMEM((rows, tile), BF16)],
        ),
        out_shape=jax.ShapeDtypeStruct((width, features), F32),
        compiler_params=pltpu.CompilerParams(vmem_limit_bytes=57 * 1024 * 1024),
        cost_estimate=pl.CostEstimate(
            flops=2 * rows * width * features,
            bytes_accessed=2 * rows * (width + features) + 4 * width * features,
            transcendentals=0,
        ),
    )(jnp.stack(where).astype(jnp.int32), *hidden, g)


def mixture_kernel(
    place_ref, upper0_ref, upper1_ref, lower0_ref, lower1_ref, wd_ref, result_ref
):
    early = pl.program_id(0) < pl.num_programs(0) // 2
    rows = jnp.concatenate(
        [
            jnp.where(early, upper0_ref[...], upper1_ref[...]),
            jnp.where(early, lower0_ref[...], lower1_ref[...]),
        ],
        axis=0,
    )
    result_ref[...] = jnp.dot(rows, wd_ref[...], preferred_element_type=F32).astype(BF16)


def mixture_product(hidden, wd, where):
    count = len(where)
    block = 2 * hidden[0].shape[0] // count
    width, features = wd.shape
    first = pl.BlockSpec((block, width), lambda i, s: (jnp.minimum(i, count // 2 - 1), 0))
    second = pl.BlockSpec((block, width), lambda i, s: (jnp.maximum(i - count // 2, 0), 0))
    return pl.pallas_call(
        mixture_kernel,
        grid_spec=pltpu.PrefetchScalarGridSpec(
            num_scalar_prefetch=1,
            grid=(count,),
            in_specs=[first, second, first, second]
            + [pl.BlockSpec((width, features), lambda i, s: (0, 0))],
            out_specs=pl.BlockSpec((2 * block, features), lambda i, s: (s[i], 0)),
        ),
        out_shape=jax.ShapeDtypeStruct((2 * block * count, features), BF16),
        compiler_params=pltpu.CompilerParams(vmem_limit_bytes=24 * 1024 * 1024),
        cost_estimate=pl.CostEstimate(
            flops=4 * block * count * width * features,
            bytes_accessed=4 * block * count * (width + features) + 2 * width * features,
            transcendentals=0,
        ),
    )(jnp.stack(where).astype(jnp.int32), *hidden, wd)


def rotated(value, cosine, sine):
    return value * cosine + pltpu.roll(value, HEAD_SIZE // 2, 1) * sine


def inverse_rms(value):
    return lax.rsqrt(jnp.mean(value * value, axis=1, keepdims=True) + EPSILON)


def head_columns(h):
    return slice(h * HEAD_SIZE, (h + 1) * HEAD_SIZE)


def against(left, right):
    return lax.dot_general(left, right, (((1,), (1,)), ((), ())), preferred_element_type=F32)


def over_rows(left, right):
    return lax.dot_general(left, right, (((0,), (0,)), ((), ())), preferred_element_type=F32)


def causal(rows):
    return lax.broadcasted_iota(jnp.int32, (rows, rows), 1) <= lax.broadcasted_iota(
        jnp.int32, (rows, rows), 0
    )


def attention_kernel(
    key_heads,
    x_ref,
    near_ref,
    core_ref,
    gains_ref,
    cosine_ref,
    sine_ref,
    wo_ref,
    raw_ref,
    low_ref,
    mixed_ref,
    lse_ref,
    upper_ref,
    lower_ref,
):
    rows = x_ref.shape[0]
    split = near_ref.shape[0]
    query_heads = mixed_ref.shape[1] // HEAD_SIZE
    heads = query_heads + key_heads
    raw = jnp.dot(x_ref[:, :split], near_ref[...], preferred_element_type=F32) + jnp.dot(
        x_ref[:, split:], core_ref[...], preferred_element_type=F32
    )
    raw_ref[...] = raw[:, : heads * HEAD_SIZE]
    low_ref[:, heads * HEAD_SIZE :] = raw[:, heads * HEAD_SIZE :].astype(BF16)
    for h in range(heads):
        u = raw[:, head_columns(h)]
        gain = gains_ref[0:1, :] if h < query_heads else gains_ref[1:2, :]
        low_ref[:, head_columns(h)] = rotated(
            u * inverse_rms(u) * gain, cosine_ref[...], sine_ref[...]
        ).astype(BF16)
    allowed = causal(rows)
    for h in range(query_heads):
        k = query_heads + h * key_heads // query_heads
        scores = against(low_ref[:, head_columns(h)], low_ref[:, head_columns(k)]) / math.sqrt(
            HEAD_SIZE
        )
        scores = jnp.where(allowed, scores, -jnp.inf)
        row_max = jnp.max(scores, axis=1, keepdims=True)
        exps = jnp.exp(scores - row_max)
        total = jnp.sum(exps, axis=1, keepdims=True)
        lse_ref[:, h : h + 1] = row_max + jnp.log(total)
        mixed_ref[:, head_columns(h)] = jnp.dot(
            (exps * (1.0 / total)).astype(BF16),
            low_ref[:, head_columns(k + key_heads)],
            preferred_element_type=F32,
        ).astype(BF16)
    part = jnp.dot(mixed_ref[...], wo_ref[...], preferred_element_type=F32)
    upper_ref[...] = part[: rows // 2].astype(BF16)
    lower_ref[...] = part[rows // 2 :].astype(BF16)


def attention(x, near, core, gains, cosine, sine, wo, key_heads):
    rows = x.shape[0]
    width = near.shape[1]
    query_width, features = wo.shape
    shapes = [
        ((rows, query_width + key_heads * HEAD_SIZE), F32),
        ((rows, width), BF16),
        ((rows, query_width), BF16),
        ((rows, query_width // HEAD_SIZE), F32),
        ((rows // 2, features), BF16),
        ((rows // 2, features), BF16),
    ]
    return pl.pallas_call(
        functools.partial(attention_kernel, key_heads),
        out_shape=[jax.ShapeDtypeStruct(*v) for v in shapes],
        compiler_params=pltpu.CompilerParams(vmem_limit_bytes=32 * 1024 * 1024),
        cost_estimate=pl.CostEstimate(
            flops=2 * rows * features * (width + query_width) + 4 * rows * rows * query_width,
            bytes_accessed=2 * features * (width + query_width) + 8 * rows * width,
            transcendentals=rows * rows * query_width // HEAD_SIZE,
        ),
    )(x, near, core, gains, cosine, sine, wo)


def attention_back_kernel(
    key_heads,
    upstream_ref,
    wo_ref,
    raw_ref,
    low_ref,
    lse_ref,
    gains_ref,
    cosine_ref,
    sine_ref,
    x_ref,
    near_ref,
    core_ref,
    beside_ref,
    feature_ref,
    keep_ref,
    send_ref,
    mixed_grad_ref,
    raw_grad_ref,
):
    rows = upstream_ref.shape[0]
    split = near_ref.shape[0]
    width = near_ref.shape[1]
    query_heads = mixed_grad_ref.shape[1] // HEAD_SIZE
    group = query_heads // key_heads
    root = math.sqrt(HEAD_SIZE)
    mixed_grad_ref[...] = against(upstream_ref[...], wo_ref[...]).astype(BF16)
    allowed = causal(rows)
    cosine = cosine_ref[...]
    sine = sine_ref[...]

    def norm_back(h, grad, gain):
        u = raw_ref[:, head_columns(h)]
        scale = inverse_rms(u)
        normal = u * scale
        turned = grad * cosine - pltpu.roll(grad, HEAD_SIZE // 2, 1) * sine
        weighted = turned * gain
        inward = scale * (weighted - normal * jnp.mean(weighted * normal, axis=1, keepdims=True))
        raw_grad_ref[:, head_columns(h)] = inward.astype(BF16)
        return turned * normal

    query_terms = jnp.zeros((rows, HEAD_SIZE), F32)
    key_terms = jnp.zeros((rows, HEAD_SIZE), F32)
    for k in range(key_heads):
        keys = low_ref[:, head_columns(query_heads + k)]
        values = low_ref[:, head_columns(query_heads + key_heads + k)]
        key_grad = jnp.zeros((rows, HEAD_SIZE), F32)
        value_grad = jnp.zeros((rows, HEAD_SIZE), F32)
        for h in range(k * group, (k + 1) * group):
            queries = low_ref[:, head_columns(h)]
            mixed_grad = mixed_grad_ref[:, head_columns(h)]
            scores = against(queries, keys) / root
            probs = jnp.where(allowed, jnp.exp(scores - lse_ref[:, h : h + 1]), 0.0)
            probs_grad = against(mixed_grad, values)
            value_grad += over_rows(probs.astype(BF16), mixed_grad)
            inner = jnp.sum(probs * probs_grad, axis=1, keepdims=True)
            scores_grad = (probs * (probs_grad - inner)).astype(BF16)
            query_grad = jnp.dot(scores_grad, keys, preferred_element_type=F32) / root
            key_grad += over_rows(scores_grad, queries)
            query_terms += norm_back(h, query_grad, gains_ref[0:1, :])
        key_terms += norm_back(query_heads + k, key_grad / root, gains_ref[1:2, :])
        raw_grad_ref[:, head_columns(query_heads + key_heads + k)] = value_grad.astype(BF16)
    raw_grad = raw_grad_ref[...]
    feature_ref[:, :split] = against(raw_grad, near_ref[...]).astype(BF16)
    feature_ref[:, split : 2 * split] = against(raw_grad, core_ref[...]).astype(BF16)
    feature_ref[:, 2 * split : 2 * split + HEAD_SIZE] = query_terms.astype(BF16)
    feature_ref[:, 2 * split + HEAD_SIZE :] = key_terms.astype(BF16)
    keep_ref[:, :width] = over_rows(x_ref[:, :split], raw_grad).astype(BF16)
    send_ref[:, :width] = over_rows(x_ref[:, split:], raw_grad).astype(BF16)
    keep_ref[:, width:] = beside_ref[:split]
    send_ref[:, width:] = beside_ref[split:]


def attention_back(upstream, wo, raw, low, lse, gains, cosine, sine, x, near, core, beside, key_heads):
    rows, features = upstream.shape
    query_width = wo.shape[0]
    split, width = near.shape
    whole = width + beside.shape[1]
    shapes = [
        ((rows, features + 2 * HEAD_SIZE), BF16),
        ((split, whole), BF16),
        ((split, whole), BF16),
    ]
    return pl.pallas_call(
        functools.partial(attention_back_kernel, key_heads),
        out_shape=[jax.ShapeDtypeStruct(*v) for v in shapes],
        scratch_shapes=[pltpu.VMEM((rows, query_width), BF16), pltpu.VMEM((rows, width), BF16)],
        compiler_params=pltpu.CompilerParams(vmem_limit_bytes=40 * 1024 * 1024),
        cost_estimate=pl.CostEstimate(
            flops=2 * rows * features * (2 * width + query_width) + 10 * rows * rows * query_width,
            bytes_accessed=2 * features * (3 * width + query_width) + 8 * rows * width,
            transcendentals=rows * rows * query_width // HEAD_SIZE,
        ),
    )(upstream, wo, raw, low, lse, gains, cosine, sine, x, near, core, beside)


def shards(
    hidden_in,
    expert_ids,
    attention_gain,
    query_gain,
    key_gain,
    query_weight,
    key_matrix,
    value_matrix,
    output_weight,
    expert_gain,
    router_weight,
    gate_up_weight,
    down_weight,
    output_grad,
):
    tokens, features = hidden_in.shape
    owners = lax.axis_size("ep")
    local_experts = gate_up_weight.shape[0]
    expert_count = local_experts * owners
    rows_a = tokens // 2
    halves = lambda v: (v[:rows_a], v[rows_a:])

    head_share = query_gain.shape[0]
    small_rows = max(tokens, router_weight.shape[0])
    padded = lambda v: jnp.pad(v.astype(BF16), ((0, small_rows - v.shape[0]), (0, 0)))
    by_feature = jnp.concatenate(
        [router_weight, attention_gain[:, None], expert_gain[:, None]], axis=1
    )
    small = jnp.concatenate(
        [
            padded(by_feature),
            padded(jnp.stack([query_gain, key_gain], axis=1)),
            padded(expert_ids),
        ],
        axis=1,
    )
    small_hops = gather_hops(small)
    weights = jnp.concatenate([query_weight, key_matrix, value_matrix], axis=1)
    hops = gather_hops(weights)
    near = gather_near(small, small_hops)
    small = put_blocks(jnp.concatenate([near, gather_core(near, small_hops)], axis=0), 0)
    small = small.reshape(owners, small_rows, -1)
    packed = small[:, : router_weight.shape[0], : expert_count + 2].reshape(features, -1)
    router_full = packed[:, :expert_count]
    attn_gain_full = packed[:, expert_count].astype(F32)
    mlp_gain_full = packed[:, expert_count + 1].astype(F32)
    head_gains = (
        small[:, :head_share, expert_count + 2 : expert_count + 4]
        .reshape(HEAD_SIZE, 2)
        .astype(F32)
    )
    gains = head_gains.T
    ids_all = small[:, :tokens, expert_count + 4 :].reshape(-1, TOP).astype(jnp.int32)
    wd = down_weight.reshape(-1, features)
    hidden_f = hidden_in.astype(F32)
    normed_low = norm_rows(hidden_f, attn_gain_full).astype(BF16)
    normed_rel = pick_blocks(normed_low, 1)
    positions = jnp.arange(tokens, dtype=jnp.int32)
    cosine, sine_table = rope_tables(positions, HEAD_SIZE)
    (
        hops,
        normed_rel,
        cosine,
        sine_table,
        gains,
        packed,
        ids_all,
        output_all,
        gate_up_low,
    ) = join(
        hops,
        normed_rel,
        cosine,
        sine_table,
        gains,
        packed,
        ids_all,
        output_grad,
        gate_up_weight,
    )

    near = gather_near(weights, hops)
    weights_rel = [near, gather_core(near, hops)]
    output_all = lax.all_gather(output_all, "ep", axis=0, tiled=True)
    query_width = query_weight.shape[1]
    key_width = key_matrix.shape[1]
    key_heads = key_width // HEAD_SIZE
    split = features // 2
    raw, low, attention_output, lse, *head_parts = attention(
        normed_rel, *weights_rel, gains, cosine, sine_table, output_weight, key_heads
    )
    (head_parts,) = join(head_parts)

    hops = reduce_hops(head_parts[0])
    wgu = gate_up_low.transpose(1, 0, 2).reshape(features, -1)
    hops, wgu = join(hops, wgu)

    chunk = reduce_total(head_parts[0], hops)
    hops, hops_b = join(spread_hops(chunk), reduce_hops(head_parts[1]))

    attended = [spread_total(chunk, hops)]
    chunk = reduce_total(head_parts[1], hops_b)
    hops = spread_hops(chunk)
    resid_halves = [hidden_f[:rows_a] + attended[0].astype(F32)]
    routed_halves = [norm_rows(resid_halves[0], mlp_gain_full).astype(BF16)]
    hops_a, hops = join(gather_hops(routed_halves[0]), hops)

    attended.append(spread_total(chunk, hops))
    resid_halves.append(hidden_f[rows_a:] + attended[1].astype(F32))
    routed_halves.append(norm_rows(resid_halves[1], mlp_gain_full).astype(BF16))
    near_a = gather_near(routed_halves[0], hops_a)
    core_a = gather_core(near_a, hops_a)
    hops_b = gather_hops(routed_halves[1])
    lined = places()
    where = [2 * b + h for h in range(2) for b in lined]

    def experts(piece, x):
        rows = slice(piece * owners // 2, (piece + 1) * owners // 2)
        return run_experts(
            x, output_all, ids_all, where[rows], router_full, wgu, wd, local_experts
        )

    keep_a, joined_0, hidden_0 = experts(0, near_a)
    send_a, joined_1, hidden_1 = experts(1, core_a)
    hops_b, send_a, keep_a = join(hops_b, send_a, keep_a)

    near_b = gather_near(routed_halves[1], hops_b)
    core_b = gather_core(near_b, hops_b)
    come = scatter_swap(send_a)
    keep_b, joined_2, hidden_2 = experts(2, near_b)
    come, core_b, keep_b = join(come, core_b, keep_b)

    sums_a = scatter_sums(keep_a, come)
    hops_a = scatter_hops(sums_a)
    send_b, joined_3, hidden_3 = experts(3, core_b)
    hops_a, send_b = join(hops_a, send_b)
    joined = [joined_0, joined_1, joined_2, joined_3]
    hidden = [hidden_0, hidden_1, hidden_2, hidden_3]
    routed_pieces = [near_a, core_a, near_b, core_b]
    resid = jnp.concatenate(resid_halves, axis=0)
    routed_low = jnp.concatenate(routed_halves, axis=0)
    logits = jnp.dot(routed_low, router_full, preferred_element_type=F32)
    logit_max = jnp.max(logits, axis=-1, keepdims=True)
    exponent = jnp.exp(logits - logit_max)
    router = exponent / jnp.sum(exponent, axis=-1, keepdims=True)
    every_expert = jnp.arange(expert_count, dtype=jnp.int32)
    named = jnp.any(expert_ids[:, :, None] == every_expert[None, None, :], axis=1)
    chosen = jnp.where(named, router, 0.0)
    chosen_total = jnp.sum(chosen, axis=1, keepdims=True)
    gates = chosen / chosen_total

    come = scatter_swap(send_b)
    total_a = scatter_total(sums_a, hops_a)
    hops = reduce_hops(total_a)
    mixture_parts = mixture_product(hidden, wd, lined)
    come, hops, mixture_parts = join(come, hops, mixture_parts)

    sums_b = scatter_sums(keep_b, come)
    hops_b = scatter_hops(sums_b)
    chunk = reduce_total(total_a, hops)
    hops_a = spread_hops(chunk)
    hops_b, hops_a, mixture_parts = join(hops_b, hops_a, mixture_parts)

    mixture = lax.psum_scatter(mixture_parts, "ep", scatter_dimension=0, tiled=True)
    returned = [spread_total(chunk, hops_a)]
    total_b = scatter_total(sums_b, hops_b)
    hops = reduce_hops(total_b)
    (hops,) = join(hops)
    chunk = reduce_total(total_b, hops)
    (hops,) = join(spread_hops(chunk))

    returned.append(spread_total(chunk, hops))
    returned = jnp.concatenate(returned, axis=0)
    grad_out = output_grad.astype(F32)
    tail = returned[:, features:].astype(F32)
    grad_gates = tail[:, :expert_count] + tail[:, expert_count : 2 * expert_count]
    grad_gates = jnp.where(named, grad_gates, 0.0)
    grad_router = jnp.where(
        named,
        (grad_gates - jnp.sum(grad_gates * gates, axis=1, keepdims=True)) / chosen_total,
        0.0,
    )
    grad_logits = (
        router * (grad_router - jnp.sum(router * grad_router, axis=1, keepdims=True))
    ).astype(BF16)
    router_grad = jnp.dot(routed_low.T, grad_logits, preferred_element_type=F32)
    grad_routed = returned[:, :features].astype(F32) + jnp.dot(
        grad_logits, router_full.T, preferred_element_type=F32
    )
    grad_resid_norm, mlp_terms = norm_back(resid, mlp_gain_full, grad_routed)
    mlp_gain_grad = jnp.sum(mlp_terms, axis=0)
    grad_resid = grad_out + grad_resid_norm
    grad_attended = grad_resid.astype(BF16)
    mixed_rel = pick_blocks(attention_output, 1)
    output_local = lax.dot_general(
        mixed_rel, grad_attended, (((0,), (0,)), ((), ())), preferred_element_type=F32
    ).astype(BF16)
    output_half = output_local.shape[0] // 2
    output_local, grad_attended = join(output_local, grad_attended)

    come = scatter_swap(output_local[output_half:])
    by_feature = jnp.concatenate([router_grad, mlp_gain_grad[:, None]], axis=1).astype(BF16)
    by_feature = jnp.pad(by_feature, ((0, 0), (0, -by_feature.shape[1] % LANES)))
    by_feature = pick_blocks(by_feature, 0)
    by_feature, come = join(by_feature, come)

    output_sums = scatter_sums(output_local[:output_half], come)
    output_hops = scatter_hops(output_sums)
    feature_part, weights_keep, weights_send = attention_back(
        grad_attended,
        output_weight,
        raw,
        low,
        lse,
        gains,
        cosine,
        sine_table,
        normed_rel,
        *weights_rel,
        by_feature,
        key_heads,
    )
    feature_part, weights_keep, weights_send, output_hops, last_joined, last_hidden, mixture = (
        join(feature_part, weights_keep, weights_send, output_hops, joined, hidden, mixture)
    )
    mixture = lax.psum(mixture, "tp")

    come = scatter_swap(weights_send)
    hops = reduce_hops(feature_part)
    output_share = scatter_total(output_sums, output_hops)
    output_hops = gather_hops(output_share)
    down_grad = down_product(last_hidden, output_all, where).reshape(down_weight.shape)
    come, hops, down_grad, last_joined = join(come, hops, down_grad, last_joined)

    weights_sums = scatter_sums(weights_keep, come)
    weights_hops = scatter_hops(weights_sums)
    chunk = reduce_total(feature_part, hops)
    hops = spread_hops(chunk)
    gate_up_grad = gate_up_product(routed_pieces, last_joined, gate_up_weight.shape)
    hops, output_hops, gate_up_grad = join(hops, output_hops, gate_up_grad)

    near = gather_near(output_share, output_hops)
    output_core = gather_core(near, output_hops)
    total = spread_total(chunk, hops)
    grad_normed = put_blocks(total[:, :features], 1).astype(F32)
    head_grads = jnp.sum(total[:, features:].astype(F32), axis=0)
    grad_input_norm, attn_terms = norm_back(hidden_f, attn_gain_full, grad_normed)
    input_grad = grad_resid + grad_input_norm
    late = jnp.concatenate(
        [
            jnp.sum(attn_terms, axis=0).reshape(owners, -1),
            head_grads[:HEAD_SIZE].reshape(owners, -1),
            head_grads[HEAD_SIZE:].reshape(owners, -1),
        ],
        axis=1,
    )
    late = pick_blocks(late, 0)
    late_come, output_core, input_grad = join(
        scatter_swap(late[owners // 2 :]), output_core, input_grad
    )
    late_sums = scatter_sums(late[: owners // 2], late_come)
    late_hops = scatter_hops(late_sums)
    output_weight_grad = put_blocks(
        jnp.concatenate([near, output_core], axis=0), 0
    ).astype(F32)
    late_hops, weights_hops, output_weight_grad = join(
        late_hops, weights_hops, output_weight_grad
    )
    late, mixture = join(scatter_total(late_sums, late_hops)[0], mixture)
    weights_rows = scatter_total(weights_sums, weights_hops).astype(F32)
    block_out = (resid + mixture.astype(F32)).astype(BF16)
    early = weights_rows[:, query_width + 2 * key_width :]
    return (
        block_out,
        input_grad,
        late[: features // owners],
        late[features // owners : features // owners + head_share],
        late[features // owners + head_share :],
        weights_rows[:, :query_width],
        weights_rows[:, query_width : query_width + key_width],
        weights_rows[:, query_width + key_width : query_width + 2 * key_width],
        output_weight_grad,
        early[:, expert_count],
        early[:, :expert_count],
        gate_up_grad,
        down_grad,
    )


def solution(mesh):
    in_specs = (
        P("ep", None),
        P("ep", None),
        P("ep"),
        P("ep"),
        P("ep"),
        P("ep", "tp"),
        P("ep", "tp"),
        P("ep", "tp"),
        P("tp", None),
        P("ep"),
        P("ep", None),
        P("ep", None, "tp"),
        P("ep", "tp", None),
        P("ep", None),
    )
    out_specs = (
        P("ep", None),
        P("ep", None),
        P("ep"),
        P("ep"),
        P("ep"),
        P("ep", "tp"),
        P("ep", "tp"),
        P("ep", "tp"),
        P("tp", None),
        P("ep"),
        P("ep", None),
        P("ep", None, "tp"),
        P("ep", "tp", None),
    )
    return jax.shard_map(shards, mesh=mesh, in_specs=in_specs, out_specs=out_specs, check_vma=False)
```

```python
import functools
import math

import jax
import jax.numpy as jnp
from jax import lax
from jax.experimental import pallas as pl
from jax.experimental.pallas import tpu as pltpu
from jax.sharding import PartitionSpec as P

HEAD_SIZE = 128
TOP = 8
PAIR = 64
LANES = 128

EPSILON = 1e-06
THETA = 1000000.0
F32 = jnp.float32
BF16 = jnp.bfloat16
SMALL = pl.CostEstimate(flops=0, bytes_accessed=1024, transcendentals=0)


def norm_rows(value_rows, norm_gain):
    return (
        value_rows
        * lax.rsqrt(jnp.mean(value_rows * value_rows, axis=-1, keepdims=True) + EPSILON)
        * norm_gain
    )


def rope_tables(positions, head_size):
    halfway = head_size // 2
    inverse = THETA ** (-(jnp.arange(halfway, dtype=jnp.float32) * 2.0) / head_size)
    angles = positions.astype(jnp.float32)[:, None] * inverse[None, :]
    cosine, sine = jnp.cos(angles), jnp.sin(angles)
    return (
        jnp.concatenate([cosine, cosine], axis=1),
        jnp.concatenate([-sine, sine], axis=1),
    )


SWAPPED = 8


def swap(value, axis, mask):
    count = lax.axis_size(axis)
    return lax.ppermute(value, axis, [(i, i ^ mask) for i in range(count)])


def join(*values):
    return lax.optimization_barrier(values)


ORDER = (0, 2, 4, 6, 1, 3, 5, 7)


def plus(*values):
    total = values[0].astype(F32)
    for v in values[1:]:
        total = total + v.astype(F32)
    return total.astype(values[0].dtype)


def absolute():
    return lax.axis_size("ep") > SWAPPED


def in_hbm(*values):
    return [pltpu.with_memory_space_constraint(v, pltpu.HBM) for v in values]


def stack_kernel(*refs):
    *pieces, result_ref = refs
    rows = pieces[0].shape[0]
    for i, piece in enumerate(pieces):
        result_ref[i * rows : (i + 1) * rows, :] = piece[...]


def stack_rows(pieces):
    rows = pieces[0].shape[0]
    return pl.pallas_call(
        stack_kernel,
        out_shape=jax.ShapeDtypeStruct(
            (len(pieces) * rows,) + pieces[0].shape[1:], pieces[0].dtype
        ),
        compiler_params=pltpu.CompilerParams(vmem_limit_bytes=16 * 1024 * 1024),
        cost_estimate=SMALL,
    )(*pieces)


def gather_hops(value):
    if absolute():
        return [lax.all_gather(value, "ep", axis=0, tiled=True)]
    return [swap(value, "ep", m) for m in ORDER[1:4]]


def gather_near(value, hops):
    if absolute():
        return hops[0][: hops[0].shape[0] // 2]
    return stack_rows([value] + hops)


def gather_core(near, hops):
    if absolute():
        return hops[0][hops[0].shape[0] // 2 :]
    return swap(near, "ep", 1)


def scatter_swap(send):
    return send if absolute() else swap(send, "ep", 1)


def scatter_sums(keep, come):
    if absolute():
        return [jnp.concatenate([keep, come], axis=0)]
    rows = keep.shape[0] // 4
    return [
        plus(keep[i * rows : (i + 1) * rows], come[i * rows : (i + 1) * rows]) for i in range(4)
    ]


def scatter_hops(sums):
    if absolute():
        return [lax.psum_scatter(sums[0], "ep", scatter_dimension=0, tiled=True)]
    return [swap(v, "ep", m) for v, m in zip(sums[1:], ORDER[1:4])]


def scatter_total(sums, hops):
    return hops[0] if absolute() else plus(sums[0], *hops)


def chunk_of(value, index):
    rows = value.shape[0] // lax.axis_size("tp")
    return lax.dynamic_slice_in_dim(value, index * rows, rows, 0)


def reduce_hops(value):
    mine = lax.axis_index("tp")
    return [swap(chunk_of(value, mine ^ m), "tp", m) for m in range(1, lax.axis_size("tp"))]


def reduce_total(value, hops):
    return plus(chunk_of(value, lax.axis_index("tp")), *hops)


def spread_hops(chunk):
    return [swap(chunk, "tp", m) for m in range(1, lax.axis_size("tp"))]


def spread_total(chunk, hops):
    mine = lax.axis_index("tp")
    rows = chunk.shape[0]
    result = jnp.zeros(((len(hops) + 1) * rows,) + chunk.shape[1:], chunk.dtype)
    for m, piece in enumerate([chunk] + hops):
        result = lax.dynamic_update_slice_in_dim(result, piece, (mine ^ m) * rows, 0)
    return result


def places():
    if absolute():
        return [jnp.int32(b) for b in range(lax.axis_size("ep"))]
    return [lax.axis_index("ep") ^ m for m in ORDER]


def pick_blocks(value, axis):
    count = lax.axis_size("ep")
    if count > SWAPPED:
        return value
    mine = lax.axis_index("ep")
    size = value.shape[axis] // count
    return jnp.concatenate(
        [lax.dynamic_slice_in_dim(value, (mine ^ m) * size, size, axis) for m in ORDER],
        axis=axis,
    )


def put_blocks(value, axis):
    count = lax.axis_size("ep")
    if count > SWAPPED:
        return value
    mine = lax.axis_index("ep")
    size = value.shape[axis] // count
    place = lambda m: (m // 2 + (m % 2) * (count // 2)) * size
    return jnp.concatenate(
        [lax.dynamic_slice_in_dim(value, place(mine ^ b), size, axis) for b in range(count)],
        axis=axis,
    )


def expert_kernel(
    local, place_ref, x_ref, g0_ref, g1_ref, ids0_ref, ids1_ref, router_ref, wgu_ref, wd_ref,
    dx_ref, joined_ref, hidden_ref,
):
    rows = x_ref.shape[0]
    features = x_ref.shape[1]
    expert_count = router_ref.shape[1]
    hidden_count = wd_ref.shape[0]
    extra = dx_ref.shape[1] - features
    base = place_ref[0]
    x = x_ref[...]
    upstream = jnp.concatenate([g0_ref[...], g1_ref[...]], axis=0)
    ids = jnp.concatenate([ids0_ref[...], ids1_ref[...]], axis=0)
    logits = jnp.dot(x, router_ref[...], preferred_element_type=F32)
    lane = lax.broadcasted_iota(jnp.int32, (rows, expert_count), 1)
    named = ids[:, 0:1] == lane
    for k in range(1, TOP):
        named = named | (ids[:, k : k + 1] == lane)
    exponent = jnp.exp(logits - jnp.max(logits, axis=1, keepdims=True))
    router = exponent / jnp.sum(exponent, axis=1, keepdims=True)
    chosen = jnp.where(named, router, 0.0)
    gates = chosen / jnp.sum(chosen, axis=1, keepdims=True)
    gate = [
        jnp.sum(jnp.where(lane == base + j, gates, 0.0), axis=1, keepdims=True)
        for j in range(local)
    ]
    left = lax.broadcasted_iota(jnp.int32, (rows, LANES), 1) < PAIR
    per_expert = hidden_count // local // PAIR
    gate_sum = [jnp.zeros((rows, LANES), F32) for _ in range(local)]
    group = 3

    def products(q):
        wide = group * LANES
        act = jnp.dot(
            x, wgu_ref[:, 2 * q * wide : 2 * (q + 1) * wide], preferred_element_type=F32
        )
        back = lax.dot_general(
            upstream,
            wd_ref[q * wide : (q + 1) * wide, :],
            (((1,), (1,)), ((), ())),
            preferred_element_type=F32,
        )
        return act, back

    def elementwise(q, act, back):
        for i in range(group):
            p = q * group + i
            one, two = 2 * p // per_expert, (2 * p + 1) // per_expert
            first = act[:, 2 * i * LANES : (2 * i + 1) * LANES]
            second = act[:, (2 * i + 1) * LANES : (2 * i + 2) * LANES]
            g = jnp.where(left, first, pltpu.roll(second, PAIR, 1))
            u = jnp.where(left, pltpu.roll(first, PAIR, 1), second)
            gh = back[:, i * LANES : (i + 1) * LANES]
            if one == two:
                scale = jnp.broadcast_to(gate[one], (rows, LANES))
            else:
                scale = jnp.where(left, gate[one], gate[two])
            sig = lax.logistic(g)
            silu = g * sig
            hid = silu * u
            product = hid * gh
            if one == two:
                gate_sum[one] += product
            else:
                gate_sum[one] += jnp.where(left, product, 0.0)
                gate_sum[two] += jnp.where(left, 0.0, product)
            hidden_ref[:, p * LANES : (p + 1) * LANES] = (hid * scale).astype(BF16)
            gs = gh * scale
            dg = gs * u * sig * (1.0 + g * (1.0 - sig))
            du = gs * silu
            joined_ref[:, 2 * p * LANES : (2 * p + 1) * LANES] = jnp.where(
                left, dg, pltpu.roll(du, PAIR, 1)
            ).astype(BF16)
            joined_ref[:, (2 * p + 1) * LANES : (2 * p + 2) * LANES] = jnp.where(
                left, pltpu.roll(dg, PAIR, 1), du
            ).astype(BF16)

    count = hidden_count // LANES // group
    waiting = []
    for q in range(count):
        waiting.append((q, *products(q)))
        if q:
            elementwise(*waiting.pop(0))
    elementwise(*waiting.pop(0))
    dx = lax.dot_general(
        joined_ref[...], wgu_ref[...], (((1,), (1,)), ((), ())), preferred_element_type=F32
    )
    dx_ref[:, :features] = dx.astype(BF16)
    wide = lax.broadcasted_iota(jnp.int32, (rows, extra), 1)
    tail = jnp.zeros((rows, extra), F32)
    for j in range(local):
        total = jnp.sum(gate_sum[j], axis=1, keepdims=True)
        high = total.astype(BF16).astype(F32)
        tail = jnp.where(wide == base + j, high, tail)
        tail = jnp.where(wide == expert_count + base + j, total - high, tail)
    dx_ref[:, features:] = tail.astype(BF16)


def run_experts(x, g, ids, where, router, wgu, wd, local):
    tokens, features = x.shape
    tile = 256
    block = tokens // len(where)
    steps = tokens // tile
    expert_count = router.shape[1]
    extra = -(-2 * expert_count // LANES) * LANES
    place = jnp.stack([lax.axis_index("ep") * local] + list(where)).astype(jnp.int32)
    found = lambda width, j: pl.BlockSpec((block, width), lambda i, s: (s[1 + 2 * i + j], 0))
    resident = pl.BlockSpec(memory_space=pltpu.VMEM)
    by_rows = lambda width: pl.BlockSpec((tile, width), lambda i, s: (i, 0))
    in_specs = [
        by_rows(features),
        found(features, 0),
        found(features, 1),
        found(TOP, 0),
        found(TOP, 1),
        resident,
        resident,
        resident,
    ]
    (g,) = in_hbm(g)
    operands = [place, x, g, g, ids, ids, router, wgu, wd]
    return pl.pallas_call(
        functools.partial(expert_kernel, local),
        grid_spec=pltpu.PrefetchScalarGridSpec(
            num_scalar_prefetch=1,
            grid=(steps,),
            in_specs=in_specs,
            out_specs=[
                by_rows(features + extra),
                by_rows(wgu.shape[1]),
                by_rows(wd.shape[0]),
            ],
        ),
        out_shape=[
            jax.ShapeDtypeStruct((tokens, features + extra), BF16),
            jax.ShapeDtypeStruct((tokens, wgu.shape[1]), BF16),
            jax.ShapeDtypeStruct((tokens, wd.shape[0]), BF16),
        ],
        compiler_params=pltpu.CompilerParams(vmem_limit_bytes=24 * 1024 * 1024),
        cost_estimate=SMALL,
    )(*operands)


def gate_up_kernel(*refs):
    *operands, result_ref = refs
    count = len(operands) // 2
    total = None
    for x_ref, joined_ref in zip(operands[:count], operands[count:]):
        part = lax.dot_general(
            x_ref[...], joined_ref[...], (((0,), (0,)), ((), ())), preferred_element_type=F32
        )
        total = part if total is None else total + part
    width = result_ref.shape[2]
    for e in range(result_ref.shape[0]):
        result_ref[e] = total[:, e * width : (e + 1) * width]


def gate_up_product(pieces, joined, shape):
    rows, features = pieces[0].shape
    width = joined[0].shape[1]
    tile = 256
    whole = pl.BlockSpec((rows, width), lambda i: (0, 0), pipeline_mode=pl.Buffered(1))
    return pl.pallas_call(
        gate_up_kernel,
        grid=(features // tile,),
        in_specs=[pl.BlockSpec((rows, tile), lambda i: (0, i)) for _ in pieces]
        + [whole for _ in joined],
        out_specs=pl.BlockSpec((shape[0], tile, shape[2]), lambda i: (0, i, 0)),
        out_shape=jax.ShapeDtypeStruct(shape, F32),
        compiler_params=pltpu.CompilerParams(vmem_limit_bytes=56 * 1024 * 1024),
        cost_estimate=SMALL,
    )(*in_hbm(*pieces, *joined))


def down_kernel(place_ref, *refs):
    *pieces, g_ref, result_ref, sorted_ref = refs
    blocks = place_ref.shape[0] // len(pieces)
    block = pieces[0].shape[0] // blocks
    for i, hidden_ref in enumerate(pieces):
        for k in range(blocks):
            start = pl.multiple_of(place_ref[i * blocks + k] * block, block)
            sorted_ref[pl.ds(start, block), :] = hidden_ref[k * block : (k + 1) * block, :]
    result_ref[...] = lax.dot_general(
        sorted_ref[...], g_ref[...], (((0,), (0,)), ((), ())), preferred_element_type=F32
    )


def down_product(hidden, g, where):
    rows, features = g.shape
    width = hidden[0].shape[1]
    tile = 256
    return pl.pallas_call(
        down_kernel,
        grid_spec=pltpu.PrefetchScalarGridSpec(
            num_scalar_prefetch=1,
            grid=(width // tile,),
            in_specs=[pl.BlockSpec((v.shape[0], tile), lambda i, s: (0, i)) for v in hidden]
            + [pl.BlockSpec((rows, features), lambda i, s: (0, 0), pipeline_mode=pl.Buffered(1))],
            out_specs=pl.BlockSpec((tile, features), lambda i, s: (i, 0)),
            scratch_shapes=[pltpu.VMEM((rows, tile), BF16)],
        ),
        out_shape=jax.ShapeDtypeStruct((width, features), F32),
        compiler_params=pltpu.CompilerParams(vmem_limit_bytes=57 * 1024 * 1024),
        cost_estimate=SMALL,
    )(jnp.stack(where).astype(jnp.int32), *in_hbm(*hidden, g))


def mixture_kernel(
    place_ref, upper0_ref, upper1_ref, lower0_ref, lower1_ref, wd_ref, result_ref
):
    early = pl.program_id(0) < pl.num_programs(0) // 2
    rows = jnp.concatenate(
        [
            jnp.where(early, upper0_ref[...], upper1_ref[...]),
            jnp.where(early, lower0_ref[...], lower1_ref[...]),
        ],
        axis=0,
    )
    result_ref[...] = jnp.dot(rows, wd_ref[...], preferred_element_type=F32).astype(BF16)


def mixture_product(hidden, wd, where):
    count = len(where)
    block = 2 * hidden[0].shape[0] // count
    width, features = wd.shape
    first = pl.BlockSpec((block, width), lambda i, s: (jnp.minimum(i, count // 2 - 1), 0))
    second = pl.BlockSpec((block, width), lambda i, s: (jnp.maximum(i - count // 2, 0), 0))
    return pl.pallas_call(
        mixture_kernel,
        grid_spec=pltpu.PrefetchScalarGridSpec(
            num_scalar_prefetch=1,
            grid=(count,),
            in_specs=[first, second, first, second]
            + [pl.BlockSpec((width, features), lambda i, s: (0, 0))],
            out_specs=pl.BlockSpec((2 * block, features), lambda i, s: (s[i], 0)),
        ),
        out_shape=jax.ShapeDtypeStruct((2 * block * count, features), BF16),
        compiler_params=pltpu.CompilerParams(vmem_limit_bytes=24 * 1024 * 1024),
        cost_estimate=SMALL,
    )(jnp.stack(where).astype(jnp.int32), *in_hbm(*hidden, wd))


def rotated(value, cosine, sine):
    return value * cosine + pltpu.roll(value, HEAD_SIZE // 2, 1) * sine


def inverse_rms(value):
    return lax.rsqrt(jnp.mean(value * value, axis=1, keepdims=True) + EPSILON)


def head_columns(h):
    return slice(h * HEAD_SIZE, (h + 1) * HEAD_SIZE)


def against(left, right):
    return lax.dot_general(left, right, (((1,), (1,)), ((), ())), preferred_element_type=F32)


def over_rows(left, right):
    return lax.dot_general(left, right, (((0,), (0,)), ((), ())), preferred_element_type=F32)


def causal(rows):
    return lax.broadcasted_iota(jnp.int32, (rows, rows), 1) <= lax.broadcasted_iota(
        jnp.int32, (rows, rows), 0
    )


def attention_kernel(
    key_heads,
    x_ref,
    near_ref,
    core_ref,
    near_kv_ref,
    core_kv_ref,
    gains_ref,
    cosine_ref,
    sine_ref,
    wo_ref,
    raw_ref,
    low_ref,
    mixed_ref,
    lse_ref,
    upper_ref,
    lower_ref,
):
    rows = x_ref.shape[0]
    split = near_ref.shape[0]
    query_heads = mixed_ref.shape[1] // HEAD_SIZE
    heads = query_heads + key_heads
    queries = query_heads * HEAD_SIZE
    raw_ref[:, :queries] = jnp.dot(
        x_ref[:, :split], near_ref[...], preferred_element_type=F32
    ) + jnp.dot(x_ref[:, split:], core_ref[...], preferred_element_type=F32)
    wide = 2 * key_heads * HEAD_SIZE
    raw = jnp.dot(
        x_ref[:, :split], near_kv_ref[:, :wide], preferred_element_type=F32
    ) + jnp.dot(x_ref[:, split:], core_kv_ref[:, :wide], preferred_element_type=F32)
    raw_ref[:, queries:] = raw[:, : key_heads * HEAD_SIZE]
    low_ref[:, heads * HEAD_SIZE :] = raw[:, key_heads * HEAD_SIZE :].astype(BF16)
    for h in range(heads):
        u = raw_ref[:, head_columns(h)]
        gain = gains_ref[0:1, :] if h < query_heads else gains_ref[1:2, :]
        low_ref[:, head_columns(h)] = rotated(
            u * inverse_rms(u) * gain, cosine_ref[...], sine_ref[...]
        ).astype(BF16)
    allowed = causal(rows)
    for h in range(query_heads):
        k = query_heads + h * key_heads // query_heads
        scores = against(low_ref[:, head_columns(h)], low_ref[:, head_columns(k)]) / math.sqrt(
            HEAD_SIZE
        )
        scores = jnp.where(allowed, scores, -jnp.inf)
        row_max = jnp.max(scores, axis=1, keepdims=True)
        exps = jnp.exp(scores - row_max)
        total = jnp.sum(exps, axis=1, keepdims=True)
        lse_ref[:, h : h + 1] = row_max + jnp.log(total)
        mixed_ref[:, head_columns(h)] = jnp.dot(
            (exps * (1.0 / total)).astype(BF16),
            low_ref[:, head_columns(k + key_heads)],
            preferred_element_type=F32,
        ).astype(BF16)
    part = jnp.dot(mixed_ref[...], wo_ref[...], preferred_element_type=F32)
    upper_ref[...] = part[: rows // 2].astype(BF16)
    lower_ref[...] = part[rows // 2 :].astype(BF16)


def attention(x, near, core, near_kv, core_kv, gains, cosine, sine, wo, key_heads):
    rows = x.shape[0]
    query_width, features = wo.shape
    width = query_width + 2 * key_heads * HEAD_SIZE
    shapes = [
        ((rows, query_width + key_heads * HEAD_SIZE), F32),
        ((rows, width), BF16),
        ((rows, query_width), BF16),
        ((rows, query_width // HEAD_SIZE), F32),
        ((rows // 2, features), BF16),
        ((rows // 2, features), BF16),
    ]
    return pl.pallas_call(
        functools.partial(attention_kernel, key_heads),
        out_shape=[jax.ShapeDtypeStruct(*v) for v in shapes],
        compiler_params=pltpu.CompilerParams(vmem_limit_bytes=32 * 1024 * 1024),
        cost_estimate=SMALL,
    )(x, near, core, near_kv, core_kv, gains, cosine, sine, wo)


def attention_back_kernel(
    key_heads,
    place_ref,
    upstream_ref,
    wo_ref,
    raw_ref,
    low_ref,
    lse_ref,
    gains_ref,
    cosine_ref,
    sine_ref,
    x_ref,
    near_ref,
    core_ref,
    near_kv_ref,
    core_kv_ref,
    beside_ref,
    feature_ref,
    weights_ref,
    mixed_grad_ref,
    raw_grad_ref,
):
    rows = upstream_ref.shape[0]
    split = near_ref.shape[0]
    width = raw_grad_ref.shape[1]
    queries_width = near_ref.shape[1]
    query_heads = mixed_grad_ref.shape[1] // HEAD_SIZE
    group = query_heads // key_heads
    root = math.sqrt(HEAD_SIZE)
    mixed_grad_ref[...] = against(upstream_ref[...], wo_ref[...]).astype(BF16)
    allowed = causal(rows)
    cosine = cosine_ref[...]
    sine = sine_ref[...]

    def norm_back(h, grad, gain):
        u = raw_ref[:, head_columns(h)]
        scale = inverse_rms(u)
        normal = u * scale
        turned = grad * cosine - pltpu.roll(grad, HEAD_SIZE // 2, 1) * sine
        weighted = turned * gain
        inward = scale * (weighted - normal * jnp.mean(weighted * normal, axis=1, keepdims=True))
        raw_grad_ref[:, head_columns(h)] = inward.astype(BF16)
        return turned * normal

    query_terms = jnp.zeros((rows, HEAD_SIZE), F32)
    key_terms = jnp.zeros((rows, HEAD_SIZE), F32)
    for k in range(key_heads):
        keys = low_ref[:, head_columns(query_heads + k)]
        values = low_ref[:, head_columns(query_heads + key_heads + k)]
        key_grad = jnp.zeros((rows, HEAD_SIZE), F32)
        value_grad = jnp.zeros((rows, HEAD_SIZE), F32)
        for h in range(k * group, (k + 1) * group):
            queries = low_ref[:, head_columns(h)]
            mixed_grad = mixed_grad_ref[:, head_columns(h)]
            scores = against(queries, keys) / root
            probs = jnp.where(allowed, jnp.exp(scores - lse_ref[:, h : h + 1]), 0.0)
            probs_grad = against(mixed_grad, values)
            value_grad += over_rows(probs.astype(BF16), mixed_grad)
            inner = jnp.sum(probs * probs_grad, axis=1, keepdims=True)
            scores_grad = (probs * (probs_grad - inner)).astype(BF16)
            query_grad = jnp.dot(scores_grad, keys, preferred_element_type=F32) / root
            key_grad += over_rows(scores_grad, queries)
            query_terms += norm_back(h, query_grad, gains_ref[0:1, :])
        key_terms += norm_back(query_heads + k, key_grad / root, gains_ref[1:2, :])
        raw_grad_ref[:, head_columns(query_heads + key_heads + k)] = value_grad.astype(BF16)
    raw_grad = raw_grad_ref[...]
    for part, (query_ref, kv_ref) in enumerate(
        ((near_ref, near_kv_ref), (core_ref, core_kv_ref))
    ):
        feature_ref[:, part * split : (part + 1) * split] = (
            against(raw_grad[:, :queries_width], query_ref[...])
            + against(raw_grad[:, queries_width:], kv_ref[:, : width - queries_width])
        ).astype(BF16)
    feature_ref[:, 2 * split : 2 * split + HEAD_SIZE] = query_terms.astype(BF16)
    feature_ref[:, 2 * split + HEAD_SIZE :] = key_terms.astype(BF16)
    count = place_ref.shape[0]
    block = 2 * split // count
    for j in range(count):
        at = pl.ds(pl.multiple_of(place_ref[j] * block, block), block)
        if block % LANES == 0:
            columns = x_ref[:, j * block : (j + 1) * block]
            weights_ref[at, :width] = over_rows(columns, raw_grad).astype(BF16)
    if block % LANES:
        weights_ref[:, :width] = over_rows(x_ref[...], raw_grad).astype(BF16)
    weights_ref[:, width:] = beside_ref[...]


def in_vmem(count):
    return [pl.BlockSpec()] * count


def in_smem():
    return [pl.BlockSpec(memory_space=pltpu.SMEM)]


def attention_back(
    where, upstream, wo, raw, low, lse, gains, cosine, sine, x, weights, beside, key_heads
):
    rows, features = upstream.shape
    query_width = wo.shape[0]
    split = weights[0].shape[0]
    width = low.shape[1]
    whole = width + beside.shape[1]
    shapes = [
        ((rows, features + 2 * HEAD_SIZE), BF16),
        ((features, whole), BF16),
    ]
    operands = [upstream, wo, raw, low, lse, gains, cosine, sine, x, *weights, beside]
    return pl.pallas_call(
        functools.partial(attention_back_kernel, key_heads),
        in_specs=in_smem() + in_vmem(len(operands)),
        out_specs=in_vmem(2),
        out_shape=[jax.ShapeDtypeStruct(*v) for v in shapes],
        scratch_shapes=[pltpu.VMEM((rows, query_width), BF16), pltpu.VMEM((rows, width), BF16)],
        compiler_params=pltpu.CompilerParams(vmem_limit_bytes=40 * 1024 * 1024),
        cost_estimate=SMALL,
    )(jnp.stack(where).astype(jnp.int32), *in_hbm(*operands))


def chunk_places():
    return jnp.stack(
        [lax.axis_index("tp") ^ m for m in range(lax.axis_size("tp"))]
    ).astype(jnp.int32)


def rows_at(index, size):
    return pl.ds(pl.multiple_of(index * size, size), size)


def resid_kernel(place_ref, *refs):
    *pieces, hidden_ref, gain_ref, resid_ref, routed_ref = refs
    rows = pieces[0].shape[0]
    for m, piece in enumerate(pieces):
        at = rows_at(place_ref[m], rows)
        resid = hidden_ref[at, :].astype(F32) + piece[...].astype(F32)
        resid_ref[at, :] = resid
        routed_ref[at, :] = (resid * inverse_rms(resid) * gain_ref[...]).astype(BF16)


def resid_and_routed(pieces, hidden, gain):
    return pl.pallas_call(
        resid_kernel,
        in_specs=in_smem() + in_vmem(len(pieces) + 2),
        out_specs=in_vmem(2),
        out_shape=[
            jax.ShapeDtypeStruct(hidden.shape, F32),
            jax.ShapeDtypeStruct(hidden.shape, BF16),
        ],
        compiler_params=pltpu.CompilerParams(vmem_limit_bytes=16 * 1024 * 1024),
        cost_estimate=SMALL,
    )(chunk_places(), *pieces, hidden, gain)


def resid_back_kernel(parts, place_ref, column_ref, *refs):
    pieces = refs[: 2 * parts]
    (
        resid_a_ref,
        resid_b_ref,
        routed_a_ref,
        routed_b_ref,
        ids_ref,
        router_ref,
        gain_ref,
        upstream_ref,
        mixed_ref,
        grad_ref,
        low_ref,
        beside_ref,
        keep_ref,
        send_ref,
        returned_ref,
        wide_ref,
    ) = refs[2 * parts :]
    rows, features = upstream_ref.shape
    expert_count = router_ref.shape[1]
    chunk = pieces[0].shape[0]
    for h in range(2):
        for m in range(parts):
            returned_ref[rows_at(place_ref[m] + h * parts, chunk), :] = pieces[h * parts + m][...]
    routed = jnp.concatenate([routed_a_ref[...], routed_b_ref[...]], axis=0)
    resid = jnp.concatenate([resid_a_ref[...], resid_b_ref[...]], axis=0)
    logits = jnp.dot(routed, router_ref[...], preferred_element_type=F32)
    lane = lax.broadcasted_iota(jnp.int32, (rows, expert_count), 1)
    named = ids_ref[:, 0:1] == lane
    for k in range(1, TOP):
        named = named | (ids_ref[:, k : k + 1] == lane)
    exponent = jnp.exp(logits - jnp.max(logits, axis=1, keepdims=True))
    router = exponent / jnp.sum(exponent, axis=1, keepdims=True)
    chosen = jnp.where(named, router, 0.0)
    total = jnp.sum(chosen, axis=1, keepdims=True)
    gates = chosen / total
    tail = returned_ref[:, features:].astype(F32)
    tail = tail + pltpu.roll(tail, tail.shape[1] - expert_count, 1)
    grad_gates = jnp.where(named, tail[:, :expert_count], 0.0)
    inner = jnp.sum(grad_gates * gates, axis=1, keepdims=True)
    grad_router = jnp.where(named, (grad_gates - inner) / total, 0.0)
    inner = jnp.sum(router * grad_router, axis=1, keepdims=True)
    grad_logits = (router * (grad_router - inner)).astype(BF16)
    grad_routed = returned_ref[:, :features].astype(F32) + against(grad_logits, router_ref[...])
    scale = inverse_rms(resid)
    normal = resid * scale
    weighted = grad_routed * gain_ref[...]
    inner = jnp.mean(weighted * normal, axis=1, keepdims=True)
    grad = upstream_ref[...].astype(F32) + scale * (weighted - normal * inner)
    grad_ref[...] = grad
    low_ref[...] = grad.astype(BF16)
    half = column_ref.shape[0] // 2
    for j in range(half):
        for k, out_ref in ((j, keep_ref), (half + j, send_ref)):
            columns = pl.ds(pl.multiple_of(column_ref[k] * LANES, LANES), LANES)
            out_ref[j * LANES : (j + 1) * LANES, :] = over_rows(
                mixed_ref[:, columns], low_ref[...]
            ).astype(BF16)
    wide_ref[...] = jnp.zeros(wide_ref.shape, BF16)
    wide_ref[:, :expert_count] = grad_logits
    one = lax.broadcasted_iota(jnp.int32, wide_ref.shape, 1) == expert_count
    beside_ref[...] = (
        over_rows(routed, wide_ref[...])
        + over_rows((grad_routed * normal).astype(BF16), one.astype(F32).astype(BF16))
    ).astype(BF16)


def resid_back(pieces, resid, routed, ids, router, gain, upstream, mixed, columns):
    parts = len(pieces) // 2
    rows, features = upstream.shape
    expert_count = router.shape[1]
    wide = -(-(expert_count + 1) // LANES) * LANES
    half = mixed.shape[1] // 2
    shapes = [
        ((rows, features), F32),
        ((rows, features), BF16),
        ((features, wide), BF16),
        ((half, features), BF16),
        ((half, features), BF16),
    ]
    operands = [*pieces, *in_hbm(*resid, *routed, ids, router, gain, upstream, mixed)]
    return pl.pallas_call(
        functools.partial(resid_back_kernel, parts),
        in_specs=in_smem() * 2 + in_vmem(len(operands)),
        out_specs=in_vmem(len(shapes)),
        out_shape=[jax.ShapeDtypeStruct(*v) for v in shapes],
        scratch_shapes=[
            pltpu.VMEM((rows, pieces[0].shape[1]), BF16),
            pltpu.VMEM((rows, wide), BF16),
        ],
        compiler_params=pltpu.CompilerParams(vmem_limit_bytes=40 * 1024 * 1024),
        cost_estimate=SMALL,
    )(chunk_places(), jnp.stack(columns).astype(jnp.int32), *operands)


def input_kernel(ordered, place_ref, block_ref, *refs):
    *pieces, hidden_ref, resid_grad_ref, gain_ref, result_ref, late_ref, total_ref = refs
    features = hidden_ref.shape[1]
    rows = pieces[0].shape[0]
    count = block_ref.shape[0]
    block = features // count
    for m, piece in enumerate(pieces):
        total_ref[rows_at(place_ref[m], rows), :] = piece[...]
    hidden = hidden_ref[...].astype(F32)
    scale = inverse_rms(hidden)
    columns = [
        slice(j * block, (j + 1) * block)
        if ordered
        else pl.ds(pl.multiple_of(block_ref[j] * block, block), block)
        for j in range(count)
    ]
    inner = jnp.zeros((hidden.shape[0], 1), F32)
    for j in range(count):
        normal = hidden_ref[:, columns[j]].astype(F32) * scale
        grad = total_ref[:, j * block : (j + 1) * block].astype(F32)
        terms = grad * normal
        inner += jnp.sum(terms * gain_ref[:, columns[j]], axis=1, keepdims=True)
        late_ref[j : j + 1, :block] = jnp.sum(terms, axis=0, keepdims=True)
    inner = inner * (1.0 / features)
    for j in range(count):
        normal = hidden_ref[:, columns[j]].astype(F32) * scale
        weighted = total_ref[:, j * block : (j + 1) * block].astype(F32) * gain_ref[:, columns[j]]
        result_ref[:, columns[j]] = resid_grad_ref[:, columns[j]] + scale * (
            weighted - normal * inner
        )
    heads = jnp.sum(total_ref[:, features:].astype(F32), axis=0, keepdims=True)
    late_ref[:, block:] = jnp.broadcast_to(heads, (count, heads.shape[1]))


def input_gradient(pieces, hidden, resid_grad, gain, where):
    rows, features = hidden.shape
    count = len(where)
    extra = pieces[0].shape[1] - features
    return pl.pallas_call(
        functools.partial(input_kernel, absolute()),
        in_specs=in_smem() * 2 + in_vmem(len(pieces) + 3),
        out_specs=in_vmem(2),
        out_shape=[
            jax.ShapeDtypeStruct((rows, features), F32),
            jax.ShapeDtypeStruct((count, features // count + extra), F32),
        ],
        scratch_shapes=[pltpu.VMEM((rows, pieces[0].shape[1]), BF16)],
        compiler_params=pltpu.CompilerParams(vmem_limit_bytes=24 * 1024 * 1024),
        cost_estimate=SMALL,
    )(chunk_places(), jnp.stack(where).astype(jnp.int32), *pieces, *in_hbm(hidden, resid_grad, gain))


def widen_kernel(place_ref, near_ref, core_ref, result_ref):
    early = pl.program_id(0) < pl.num_programs(0) // 2
    result_ref[...] = jnp.where(early, near_ref[...], core_ref[...]).astype(F32)


def widen_blocks(near, core, where):
    count = len(where)
    features = near.shape[1]
    block = 2 * near.shape[0] // count
    half = count // 2
    first = pl.BlockSpec((block, features), lambda i, s: (jnp.minimum(i, half - 1), 0))
    second = pl.BlockSpec((block, features), lambda i, s: (jnp.maximum(i - half, 0), 0))
    return pl.pallas_call(
        widen_kernel,
        grid_spec=pltpu.PrefetchScalarGridSpec(
            num_scalar_prefetch=1,
            grid=(count,),
            in_specs=[first, second],
            out_specs=pl.BlockSpec((block, features), lambda i, s: (s[i], 0)),
        ),
        out_shape=jax.ShapeDtypeStruct((block * count, features), F32),
        compiler_params=pltpu.CompilerParams(vmem_limit_bytes=24 * 1024 * 1024),
        cost_estimate=SMALL,
    )(jnp.stack(where).astype(jnp.int32), near, core)


def shards(
    hidden_in,
    expert_ids,
    attention_gain,
    query_gain,
    key_gain,
    query_weight,
    key_matrix,
    value_matrix,
    output_weight,
    expert_gain,
    router_weight,
    gate_up_weight,
    down_weight,
    output_grad,
):
    tokens, features = hidden_in.shape
    owners = lax.axis_size("ep")
    local_experts = gate_up_weight.shape[0]
    expert_count = local_experts * owners
    rows_a = tokens // 2

    head_share = query_gain.shape[0]
    share = router_weight.shape[0]
    small_rows = max(tokens, share)
    padded = lambda v: jnp.pad(v.astype(BF16), ((0, small_rows - v.shape[0]), (0, 0)))
    small = jnp.concatenate(
        [
            padded(router_weight),
            padded(jnp.stack([attention_gain, expert_gain], axis=1)),
            padded(jnp.stack([query_gain, key_gain], axis=1)),
            padded(expert_ids),
        ],
        axis=1,
    )
    small_width = small.shape[1]
    small = jnp.pad(small, ((0, 0), (0, -small_width % LANES)))
    packed = jnp.concatenate([key_matrix, value_matrix], axis=1)
    packed_width = packed.shape[1]
    together = small_rows == share
    if together:
        packed = jnp.concatenate([packed, small], axis=1)
    packed_hops = gather_hops(packed)
    hops = gather_hops(query_weight)
    packed_near = gather_near(packed, packed_hops)
    packed_core = gather_core(packed_near, packed_hops)
    if together:
        small = jnp.concatenate(
            [packed_near[:, packed_width:], packed_core[:, packed_width:]], axis=0
        )
    else:
        small = lax.all_gather(small, "ep", axis=0, tiled=True)
    small = put_blocks(small, 0).reshape(owners, small_rows, -1)
    by_feature = small[:, :share, : expert_count + 2].reshape(features, -1)
    router_full = by_feature[:, :expert_count]
    attn_gain_full = by_feature[:, expert_count].astype(F32)[None, :]
    mlp_gain_full = by_feature[:, expert_count + 1].astype(F32)[None, :]
    gains = (
        small[:, :head_share, expert_count + 2 : expert_count + 4]
        .reshape(HEAD_SIZE, 2)
        .astype(F32)
        .T
    )
    ids_all = small[:, :tokens, expert_count + 4 : small_width].reshape(-1, TOP).astype(jnp.int32)
    wd = down_weight.reshape(-1, features)
    normed_low = norm_rows(hidden_in.astype(F32), attn_gain_full).astype(BF16)
    normed_rel = pick_blocks(normed_low, 1)
    positions = jnp.arange(tokens, dtype=jnp.int32)
    cosine, sine_table = rope_tables(positions, HEAD_SIZE)
    (
        hops,
        packed_core,
        normed_rel,
        cosine,
        sine_table,
        gains,
        router_full,
        attn_gain_full,
        mlp_gain_full,
        ids_all,
        output_all,
        gate_up_low,
    ) = join(
        hops,
        packed_core,
        normed_rel,
        cosine,
        sine_table,
        gains,
        router_full,
        attn_gain_full,
        mlp_gain_full,
        ids_all,
        output_grad,
        gate_up_weight,
    )

    near = gather_near(query_weight, hops)
    weights_rel = [near, gather_core(near, hops), packed_near, packed_core]
    output_all = lax.all_gather(output_all, "ep", axis=0, tiled=True)
    query_width = query_weight.shape[1]
    key_width = key_matrix.shape[1]
    key_heads = key_width // HEAD_SIZE
    raw, low, attention_output, lse, *head_parts = attention(
        normed_rel, *weights_rel, gains, cosine, sine_table, output_weight, key_heads
    )
    (head_parts,) = join(head_parts)

    hops = reduce_hops(head_parts[0])
    wgu = gate_up_low.transpose(1, 0, 2).reshape(features, -1)
    hops, wgu = join(hops, wgu)

    chunk = reduce_total(head_parts[0], hops)
    hops, hops_b = join(spread_hops(chunk), reduce_hops(head_parts[1]))

    resid_a, routed_a = resid_and_routed([chunk] + hops, hidden_in[:rows_a], mlp_gain_full)
    chunk = reduce_total(head_parts[1], hops_b)
    hops_a, hops = join(gather_hops(routed_a), spread_hops(chunk))

    resid_b, routed_b = resid_and_routed([chunk] + hops, hidden_in[rows_a:], mlp_gain_full)
    near_a = gather_near(routed_a, hops_a)
    core_a = gather_core(near_a, hops_a)
    hops_b = gather_hops(routed_b)
    lined = places()
    where = [2 * b + h for h in range(2) for b in lined]

    def experts(piece, x):
        rows = slice(piece * owners // 2, (piece + 1) * owners // 2)
        return run_experts(
            x, output_all, ids_all, where[rows], router_full, wgu, wd, local_experts
        )

    keep_a, joined_0, hidden_0 = experts(0, near_a)
    send_a, joined_1, hidden_1 = experts(1, core_a)
    hops_b, send_a, keep_a = join(hops_b, send_a, keep_a)

    near_b = gather_near(routed_b, hops_b)
    core_b = gather_core(near_b, hops_b)
    come = scatter_swap(send_a)
    keep_b, joined_2, hidden_2 = experts(2, near_b)
    come, core_b, keep_b = join(come, core_b, keep_b)

    sums_a = scatter_sums(keep_a, come)
    hops_a = scatter_hops(sums_a)
    send_b, joined_3, hidden_3 = experts(3, core_b)
    hops_a, send_b = join(hops_a, send_b)
    joined = [joined_0, joined_1, joined_2, joined_3]
    hidden = [hidden_0, hidden_1, hidden_2, hidden_3]
    routed_pieces = [near_a, core_a, near_b, core_b]

    come = scatter_swap(send_b)
    total_a = scatter_total(sums_a, hops_a)
    hops = reduce_hops(total_a)
    mixture_parts = mixture_product(hidden, wd, lined)
    come, hops, mixture_parts = join(come, hops, mixture_parts)

    mixture = lax.psum_scatter(mixture_parts, "ep", scatter_dimension=0, tiled=True)
    sums_b = scatter_sums(keep_b, come)
    hops_b = scatter_hops(sums_b)
    chunk_a = reduce_total(total_a, hops)
    gate_up_grad = gate_up_product(routed_pieces, joined, gate_up_weight.shape)
    spread_a, hops_b, gate_up_grad, hidden = join(
        spread_hops(chunk_a), hops_b, gate_up_grad, hidden
    )

    total_b = scatter_total(sums_b, hops_b)
    (hops,) = join(reduce_hops(total_b))
    chunk_b = reduce_total(total_b, hops)
    (spread_b,) = join(spread_hops(chunk_b))

    columns = (
        [jnp.int32(b) for b in range(attention_output.shape[1] // LANES)] if absolute() else lined
    )
    grad_resid, grad_attended, by_feature, output_keep, output_send = resid_back(
        [chunk_a, *spread_a, chunk_b, *spread_b],
        [resid_a, resid_b],
        [routed_a, routed_b],
        expert_ids,
        router_full,
        mlp_gain_full,
        output_grad,
        attention_output,
        columns,
    )

    feature_part, weights_grad = attention_back(
        lined,
        grad_attended,
        output_weight,
        raw,
        low,
        lse,
        gains,
        cosine,
        sine_table,
        normed_rel,
        weights_rel,
        by_feature,
        key_heads,
    )
    come, feature_part, weights_grad = join(
        scatter_swap(output_send), feature_part, weights_grad
    )

    weights_rows = lax.psum_scatter(weights_grad, "ep", scatter_dimension=0, tiled=True)
    hops = reduce_hops(feature_part)
    output_sums = scatter_sums(output_keep, come)
    output_hops = scatter_hops(output_sums)
    down_grad = down_product(hidden, output_all, where).reshape(down_weight.shape)
    hops, output_hops, down_grad, mixture = join(hops, output_hops, down_grad, mixture)

    chunk = reduce_total(feature_part, hops)
    output_share = scatter_total(output_sums, output_hops)
    hops, output_hops, mixture = join(
        spread_hops(chunk), gather_hops(output_share), mixture
    )

    mixture_hops = reduce_hops(mixture)
    near = gather_near(output_share, output_hops)
    output_core = gather_core(near, output_hops)
    input_grad, late = input_gradient(
        [chunk, *hops], hidden_in, grad_resid, attn_gain_full, lined
    )
    late_come = scatter_swap(late[owners // 2 :])
    output_core, late_come, mixture_hops = join(output_core, late_come, mixture_hops)

    mixture_chunk = reduce_total(mixture, mixture_hops)
    mixture_hops = spread_hops(mixture_chunk)
    late_sums = scatter_sums(late[: owners // 2], late_come)
    late_hops = scatter_hops(late_sums)
    output_weight_grad = widen_blocks(near, output_core, lined)
    late_hops, output_weight_grad, weights_rows, mixture_hops = join(
        late_hops, output_weight_grad, weights_rows, mixture_hops
    )
    weights_rows = weights_rows.astype(F32)
    late = scatter_total(late_sums, late_hops)[0]
    head_grads = lax.dynamic_slice_in_dim(
        late[share:].reshape(2, HEAD_SIZE), lax.axis_index("ep") * head_share, head_share, 1
    )
    early = weights_rows[:, query_width + 2 * key_width :]
    mixture = spread_total(mixture_chunk, mixture_hops)
    block_out = (jnp.concatenate([resid_a, resid_b], axis=0) + mixture.astype(F32)).astype(BF16)
    return (
        block_out,
        input_grad,
        late[:share],
        head_grads[0],
        head_grads[1],
        weights_rows[:, :query_width],
        weights_rows[:, query_width : query_width + key_width],
        weights_rows[:, query_width + key_width : query_width + 2 * key_width],
        output_weight_grad,
        early[:, expert_count],
        early[:, :expert_count],
        gate_up_grad,
        down_grad,
    )


def solution(mesh):
    in_specs = (
        P("ep", None),
        P("ep", None),
        P("ep"),
        P("ep"),
        P("ep"),
        P("ep", "tp"),
        P("ep", "tp"),
        P("ep", "tp"),
        P("tp", None),
        P("ep"),
        P("ep", None),
        P("ep", None, "tp"),
        P("ep", "tp", None),
        P("ep", None),
    )
    out_specs = (
        P("ep", None),
        P("ep", None),
        P("ep"),
        P("ep"),
        P("ep"),
        P("ep", "tp"),
        P("ep", "tp"),
        P("ep", "tp"),
        P("tp", None),
        P("ep"),
        P("ep", None),
        P("ep", None, "tp"),
        P("ep", "tp", None),
    )
    return jax.shard_map(shards, mesh=mesh, in_specs=in_specs, out_specs=out_specs, check_vma=False)
```

```python
import functools
import math

import jax
import jax.numpy as jnp
from jax import lax
from jax.experimental import pallas as pl
from jax.experimental.pallas import tpu as pltpu
from jax.sharding import PartitionSpec as P

HEAD_SIZE = 128
TOP = 8
PAIR = 64
LANES = 128

EPSILON = 1e-06
THETA = 1000000.0
F32 = jnp.float32
BF16 = jnp.bfloat16
SMALL = pl.CostEstimate(flops=0, bytes_accessed=1024, transcendentals=0)


def norm_rows(value_rows, norm_gain):
    return (
        value_rows
        * lax.rsqrt(jnp.mean(value_rows * value_rows, axis=-1, keepdims=True) + EPSILON)
        * norm_gain
    )


def rope_tables(positions, head_size):
    halfway = head_size // 2
    inverse = THETA ** (-(jnp.arange(halfway, dtype=jnp.float32) * 2.0) / head_size)
    angles = positions.astype(jnp.float32)[:, None] * inverse[None, :]
    cosine, sine = jnp.cos(angles), jnp.sin(angles)
    return (
        jnp.concatenate([cosine, cosine], axis=1),
        jnp.concatenate([-sine, sine], axis=1),
    )


SWAPPED = 8


def swap(value, axis, mask):
    count = lax.axis_size(axis)
    return lax.ppermute(value, axis, [(i, i ^ mask) for i in range(count)])


def join(*values):
    return lax.optimization_barrier(values)


ORDER = (0, 2, 4, 6, 1, 3, 5, 7)


def plus(*values):
    total = values[0].astype(F32)
    for v in values[1:]:
        total = total + v.astype(F32)
    return total.astype(values[0].dtype)


def absolute():
    return lax.axis_size("ep") > SWAPPED


def in_hbm(*values):
    return [pltpu.with_memory_space_constraint(v, pltpu.HBM) for v in values]


def stack_kernel(*refs):
    *pieces, result_ref = refs
    rows = pieces[0].shape[0]
    for i, piece in enumerate(pieces):
        result_ref[i * rows : (i + 1) * rows, :] = piece[...]


def stack_rows(pieces):
    rows = pieces[0].shape[0]
    return pl.pallas_call(
        stack_kernel,
        out_shape=jax.ShapeDtypeStruct(
            (len(pieces) * rows,) + pieces[0].shape[1:], pieces[0].dtype
        ),
        compiler_params=pltpu.CompilerParams(vmem_limit_bytes=8 * 1024 * 1024),
        cost_estimate=SMALL,
    )(*pieces)


def gather_hops(value):
    if absolute():
        return [lax.all_gather(value, "ep", axis=0, tiled=True)]
    return [swap(value, "ep", m) for m in ORDER[1:4]]


def gather_near(value, hops):
    if absolute():
        return hops[0][: hops[0].shape[0] // 2]
    return stack_rows([value] + hops)


def gather_core(near, hops):
    if absolute():
        return hops[0][hops[0].shape[0] // 2 :]
    return swap(near, "ep", 1)


def scatter_swap(send):
    return send if absolute() else swap(send, "ep", 1)


def scatter_sums(keep, come):
    if absolute():
        return [jnp.concatenate([keep, come], axis=0)]
    rows = keep.shape[0] // 4
    return [
        plus(keep[i * rows : (i + 1) * rows], come[i * rows : (i + 1) * rows]) for i in range(4)
    ]


def scatter_hops(sums):
    if absolute():
        return [lax.psum_scatter(sums[0], "ep", scatter_dimension=0, tiled=True)]
    return [swap(v, "ep", m) for v, m in zip(sums[1:], ORDER[1:4])]


def scatter_total(sums, hops):
    return hops[0] if absolute() else plus(sums[0], *hops)


def chunk_of(value, index):
    rows = value.shape[0] // lax.axis_size("tp")
    return lax.dynamic_slice_in_dim(value, index * rows, rows, 0)


def reduce_hops(value):
    mine = lax.axis_index("tp")
    return [swap(chunk_of(value, mine ^ m), "tp", m) for m in range(1, lax.axis_size("tp"))]


def reduce_total(value, hops):
    return plus(chunk_of(value, lax.axis_index("tp")), *hops)


def spread_hops(chunk):
    return [swap(chunk, "tp", m) for m in range(1, lax.axis_size("tp"))]


def spread_total(chunk, hops):
    mine = lax.axis_index("tp")
    rows = chunk.shape[0]
    result = jnp.zeros(((len(hops) + 1) * rows,) + chunk.shape[1:], chunk.dtype)
    for m, piece in enumerate([chunk] + hops):
        result = lax.dynamic_update_slice_in_dim(result, piece, (mine ^ m) * rows, 0)
    return result


def places():
    if absolute():
        return [jnp.int32(b) for b in range(lax.axis_size("ep"))]
    return [lax.axis_index("ep") ^ m for m in ORDER]


def pick_blocks(value, axis):
    count = lax.axis_size("ep")
    if count > SWAPPED:
        return value
    mine = lax.axis_index("ep")
    size = value.shape[axis] // count
    return jnp.concatenate(
        [lax.dynamic_slice_in_dim(value, (mine ^ m) * size, size, axis) for m in ORDER],
        axis=axis,
    )


def put_blocks(value, axis):
    count = lax.axis_size("ep")
    if count > SWAPPED:
        return value
    mine = lax.axis_index("ep")
    size = value.shape[axis] // count
    place = lambda m: (m // 2 + (m % 2) * (count // 2)) * size
    return jnp.concatenate(
        [lax.dynamic_slice_in_dim(value, place(mine ^ b), size, axis) for b in range(count)],
        axis=axis,
    )


def expert_kernel(
    local, place_ref, x_ref, g0_ref, g1_ref, ids0_ref, ids1_ref, router_ref, wgu_ref, wd_ref,
    dx_ref, joined_ref, hidden_ref,
):
    rows = x_ref.shape[0]
    features = x_ref.shape[1]
    expert_count = router_ref.shape[1]
    hidden_count = wd_ref.shape[0]
    extra = dx_ref.shape[1] - features
    base = place_ref[0]
    x = x_ref[...]
    upstream = jnp.concatenate([g0_ref[...], g1_ref[...]], axis=0)
    ids = jnp.concatenate([ids0_ref[...], ids1_ref[...]], axis=0)
    logits = jnp.dot(x, router_ref[...], preferred_element_type=F32)
    lane = lax.broadcasted_iota(jnp.int32, (rows, expert_count), 1)
    named = ids[:, 0:1] == lane
    for k in range(1, TOP):
        named = named | (ids[:, k : k + 1] == lane)
    exponent = jnp.exp(logits - jnp.max(logits, axis=1, keepdims=True))
    router = exponent / jnp.sum(exponent, axis=1, keepdims=True)
    chosen = jnp.where(named, router, 0.0)
    gates = chosen / jnp.sum(chosen, axis=1, keepdims=True)
    gate = [
        jnp.sum(jnp.where(lane == base + j, gates, 0.0), axis=1, keepdims=True)
        for j in range(local)
    ]
    left = lax.broadcasted_iota(jnp.int32, (rows, LANES), 1) < PAIR
    per_expert = hidden_count // local // PAIR
    gate_sum = [jnp.zeros((rows, LANES), F32) for _ in range(local)]
    group = 3

    def products(q):
        wide = group * LANES
        act = jnp.dot(
            x, wgu_ref[:, 2 * q * wide : 2 * (q + 1) * wide], preferred_element_type=F32
        )
        back = lax.dot_general(
            upstream,
            wd_ref[q * wide : (q + 1) * wide, :],
            (((1,), (1,)), ((), ())),
            preferred_element_type=F32,
        )
        return act, back

    def elementwise(q, act, back):
        for i in range(group):
            p = q * group + i
            one, two = 2 * p // per_expert, (2 * p + 1) // per_expert
            first = act[:, 2 * i * LANES : (2 * i + 1) * LANES]
            second = act[:, (2 * i + 1) * LANES : (2 * i + 2) * LANES]
            g = jnp.where(left, first, pltpu.roll(second, PAIR, 1))
            u = jnp.where(left, pltpu.roll(first, PAIR, 1), second)
            gh = back[:, i * LANES : (i + 1) * LANES]
            if one == two:
                scale = jnp.broadcast_to(gate[one], (rows, LANES))
            else:
                scale = jnp.where(left, gate[one], gate[two])
            sig = lax.logistic(g)
            silu = g * sig
            hid = silu * u
            product = hid * gh
            if one == two:
                gate_sum[one] += product
            else:
                gate_sum[one] += jnp.where(left, product, 0.0)
                gate_sum[two] += jnp.where(left, 0.0, product)
            hidden_ref[:, p * LANES : (p + 1) * LANES] = (hid * scale).astype(BF16)
            gs = gh * scale
            dg = gs * u * sig * (1.0 + g * (1.0 - sig))
            du = gs * silu
            joined_ref[:, 2 * p * LANES : (2 * p + 1) * LANES] = jnp.where(
                left, dg, pltpu.roll(du, PAIR, 1)
            ).astype(BF16)
            joined_ref[:, (2 * p + 1) * LANES : (2 * p + 2) * LANES] = jnp.where(
                left, pltpu.roll(dg, PAIR, 1), du
            ).astype(BF16)

    count = hidden_count // LANES // group
    waiting = []
    for q in range(count):
        waiting.append((q, *products(q)))
        if q:
            elementwise(*waiting.pop(0))
    elementwise(*waiting.pop(0))
    dx = lax.dot_general(
        joined_ref[...], wgu_ref[...], (((1,), (1,)), ((), ())), preferred_element_type=F32
    )
    dx_ref[:, :features] = dx.astype(BF16)
    wide = lax.broadcasted_iota(jnp.int32, (rows, extra), 1)
    tail = jnp.zeros((rows, extra), F32)
    for j in range(local):
        total = jnp.sum(gate_sum[j], axis=1, keepdims=True)
        high = total.astype(BF16).astype(F32)
        tail = jnp.where(wide == base + j, high, tail)
        tail = jnp.where(wide == expert_count + base + j, total - high, tail)
    dx_ref[:, features:] = tail.astype(BF16)


def run_experts(x, g, ids, where, router, wgu, wd, local):
    tokens, features = x.shape
    tile = 256
    block = tokens // len(where)
    steps = tokens // tile
    expert_count = router.shape[1]
    extra = -(-2 * expert_count // LANES) * LANES
    place = jnp.stack([lax.axis_index("ep") * local] + list(where)).astype(jnp.int32)
    found = lambda width, j: pl.BlockSpec((block, width), lambda i, s: (s[1 + 2 * i + j], 0))
    resident = pl.BlockSpec(memory_space=pltpu.VMEM)
    by_rows = lambda width: pl.BlockSpec((tile, width), lambda i, s: (i, 0))
    in_specs = [
        by_rows(features),
        found(features, 0),
        found(features, 1),
        found(TOP, 0),
        found(TOP, 1),
        resident,
        resident,
        resident,
    ]
    (g,) = in_hbm(g)
    operands = [place, x, g, g, ids, ids, router, wgu, wd]
    return pl.pallas_call(
        functools.partial(expert_kernel, local),
        grid_spec=pltpu.PrefetchScalarGridSpec(
            num_scalar_prefetch=1,
            grid=(steps,),
            in_specs=in_specs,
            out_specs=[
                by_rows(features + extra),
                by_rows(wgu.shape[1]),
                by_rows(wd.shape[0]),
            ],
        ),
        out_shape=[
            jax.ShapeDtypeStruct((tokens, features + extra), BF16),
            jax.ShapeDtypeStruct((tokens, wgu.shape[1]), BF16),
            jax.ShapeDtypeStruct((tokens, wd.shape[0]), BF16),
        ],
        compiler_params=pltpu.CompilerParams(vmem_limit_bytes=20 * 1024 * 1024),
        cost_estimate=SMALL,
    )(*operands)


def gate_up_kernel(*refs):
    *operands, result_ref = refs
    count = len(operands) // 2
    total = None
    for x_ref, joined_ref in zip(operands[:count], operands[count:]):
        part = lax.dot_general(
            x_ref[...], joined_ref[...], (((0,), (0,)), ((), ())), preferred_element_type=F32
        )
        total = part if total is None else total + part
    width = result_ref.shape[2]
    for e in range(result_ref.shape[0]):
        result_ref[e] = total[:, e * width : (e + 1) * width]


def gate_up_product(pieces, joined, shape):
    rows, features = pieces[0].shape
    width = joined[0].shape[1]
    tile = 256
    whole = pl.BlockSpec((rows, width), lambda i: (0, 0), pipeline_mode=pl.Buffered(1))
    return pl.pallas_call(
        gate_up_kernel,
        grid=(features // tile,),
        in_specs=[pl.BlockSpec((rows, tile), lambda i: (0, i)) for _ in pieces]
        + [whole for _ in joined],
        out_specs=pl.BlockSpec((shape[0], tile, shape[2]), lambda i: (0, i, 0)),
        out_shape=jax.ShapeDtypeStruct(shape, F32),
        compiler_params=pltpu.CompilerParams(vmem_limit_bytes=56 * 1024 * 1024),
        cost_estimate=SMALL,
    )(*in_hbm(*pieces, *joined))


def down_kernel(place_ref, *refs):
    *pieces, g_ref, result_ref, sorted_ref = refs
    blocks = place_ref.shape[0] // len(pieces)
    block = pieces[0].shape[0] // blocks
    for i, hidden_ref in enumerate(pieces):
        for k in range(blocks):
            start = pl.multiple_of(place_ref[i * blocks + k] * block, block)
            sorted_ref[pl.ds(start, block), :] = hidden_ref[k * block : (k + 1) * block, :]
    result_ref[...] = lax.dot_general(
        sorted_ref[...], g_ref[...], (((0,), (0,)), ((), ())), preferred_element_type=F32
    )


def down_product(hidden, g, where):
    rows, features = g.shape
    width = hidden[0].shape[1]
    tile = 256
    return pl.pallas_call(
        down_kernel,
        grid_spec=pltpu.PrefetchScalarGridSpec(
            num_scalar_prefetch=1,
            grid=(width // tile,),
            in_specs=[pl.BlockSpec((v.shape[0], tile), lambda i, s: (0, i)) for v in hidden]
            + [pl.BlockSpec((rows, features), lambda i, s: (0, 0), pipeline_mode=pl.Buffered(1))],
            out_specs=pl.BlockSpec((tile, features), lambda i, s: (i, 0)),
            scratch_shapes=[pltpu.VMEM((rows, tile), BF16)],
        ),
        out_shape=jax.ShapeDtypeStruct((width, features), F32),
        compiler_params=pltpu.CompilerParams(vmem_limit_bytes=57 * 1024 * 1024),
        cost_estimate=SMALL,
    )(jnp.stack(where).astype(jnp.int32), *in_hbm(*hidden, g))


def mixture_kernel(
    place_ref, upper0_ref, upper1_ref, lower0_ref, lower1_ref, wd_ref, result_ref
):
    early = pl.program_id(0) < pl.num_programs(0) // 2
    rows = jnp.concatenate(
        [
            jnp.where(early, upper0_ref[...], upper1_ref[...]),
            jnp.where(early, lower0_ref[...], lower1_ref[...]),
        ],
        axis=0,
    )
    result_ref[...] = jnp.dot(rows, wd_ref[...], preferred_element_type=F32).astype(BF16)


def mixture_product(hidden, wd, where):
    count = len(where)
    block = 2 * hidden[0].shape[0] // count
    width, features = wd.shape
    first = pl.BlockSpec((block, width), lambda i, s: (jnp.minimum(i, count // 2 - 1), 0))
    second = pl.BlockSpec((block, width), lambda i, s: (jnp.maximum(i - count // 2, 0), 0))
    return pl.pallas_call(
        mixture_kernel,
        grid_spec=pltpu.PrefetchScalarGridSpec(
            num_scalar_prefetch=1,
            grid=(count,),
            in_specs=[first, second, first, second]
            + [pl.BlockSpec((width, features), lambda i, s: (0, 0))],
            out_specs=pl.BlockSpec((2 * block, features), lambda i, s: (s[i], 0)),
        ),
        out_shape=jax.ShapeDtypeStruct((2 * block * count, features), BF16),
        compiler_params=pltpu.CompilerParams(vmem_limit_bytes=24 * 1024 * 1024),
        cost_estimate=SMALL,
    )(jnp.stack(where).astype(jnp.int32), *in_hbm(*hidden, wd))


def rotated(value, cosine, sine):
    return value * cosine + pltpu.roll(value, HEAD_SIZE // 2, 1) * sine


def inverse_rms(value):
    return lax.rsqrt(jnp.mean(value * value, axis=1, keepdims=True) + EPSILON)


def head_columns(h):
    return slice(h * HEAD_SIZE, (h + 1) * HEAD_SIZE)


def against(left, right):
    return lax.dot_general(left, right, (((1,), (1,)), ((), ())), preferred_element_type=F32)


def over_rows(left, right):
    return lax.dot_general(left, right, (((0,), (0,)), ((), ())), preferred_element_type=F32)


def causal(rows):
    return lax.broadcasted_iota(jnp.int32, (rows, rows), 1) <= lax.broadcasted_iota(
        jnp.int32, (rows, rows), 0
    )


def attention_kernel(
    key_heads,
    x_ref,
    near_ref,
    core_ref,
    near_kv_ref,
    core_kv_ref,
    gains_ref,
    cosine_ref,
    sine_ref,
    wo_ref,
    raw_ref,
    low_ref,
    mixed_ref,
    lse_ref,
    upper_ref,
    lower_ref,
):
    rows = x_ref.shape[0]
    split = near_ref.shape[0]
    query_heads = mixed_ref.shape[1] // HEAD_SIZE
    heads = query_heads + key_heads
    queries = query_heads * HEAD_SIZE
    raw_ref[:, :queries] = jnp.dot(
        x_ref[:, :split], near_ref[...], preferred_element_type=F32
    ) + jnp.dot(x_ref[:, split:], core_ref[...], preferred_element_type=F32)
    wide = 2 * key_heads * HEAD_SIZE
    raw = jnp.dot(
        x_ref[:, :split], near_kv_ref[:, :wide], preferred_element_type=F32
    ) + jnp.dot(x_ref[:, split:], core_kv_ref[:, :wide], preferred_element_type=F32)
    raw_ref[:, queries:] = raw[:, : key_heads * HEAD_SIZE]
    low_ref[:, heads * HEAD_SIZE :] = raw[:, key_heads * HEAD_SIZE :].astype(BF16)
    for h in range(heads):
        u = raw_ref[:, head_columns(h)]
        gain = gains_ref[0:1, :] if h < query_heads else gains_ref[1:2, :]
        low_ref[:, head_columns(h)] = rotated(
            u * inverse_rms(u) * gain, cosine_ref[...], sine_ref[...]
        ).astype(BF16)
    allowed = causal(rows)
    for h in range(query_heads):
        k = query_heads + h * key_heads // query_heads
        scores = against(low_ref[:, head_columns(h)], low_ref[:, head_columns(k)]) / math.sqrt(
            HEAD_SIZE
        )
        scores = jnp.where(allowed, scores, -jnp.inf)
        row_max = jnp.max(scores, axis=1, keepdims=True)
        exps = jnp.exp(scores - row_max)
        total = jnp.sum(exps, axis=1, keepdims=True)
        lse_ref[:, h : h + 1] = row_max + jnp.log(total)
        mixed_ref[:, head_columns(h)] = jnp.dot(
            (exps * (1.0 / total)).astype(BF16),
            low_ref[:, head_columns(k + key_heads)],
            preferred_element_type=F32,
        ).astype(BF16)
    part = jnp.dot(mixed_ref[...], wo_ref[...], preferred_element_type=F32)
    upper_ref[...] = part[: rows // 2].astype(BF16)
    lower_ref[...] = part[rows // 2 :].astype(BF16)


def attention(x, near, core, near_kv, core_kv, gains, cosine, sine, wo, key_heads):
    rows = x.shape[0]
    query_width, features = wo.shape
    width = query_width + 2 * key_heads * HEAD_SIZE
    shapes = [
        ((rows, query_width + key_heads * HEAD_SIZE), F32),
        ((rows, width), BF16),
        ((rows, query_width), BF16),
        ((rows, query_width // HEAD_SIZE), F32),
        ((rows // 2, features), BF16),
        ((rows // 2, features), BF16),
    ]
    return pl.pallas_call(
        functools.partial(attention_kernel, key_heads),
        out_shape=[jax.ShapeDtypeStruct(*v) for v in shapes],
        compiler_params=pltpu.CompilerParams(vmem_limit_bytes=32 * 1024 * 1024),
        cost_estimate=SMALL,
    )(x, near, core, near_kv, core_kv, gains, cosine, sine, wo)


def attention_back_kernel(
    key_heads,
    place_ref,
    upstream_ref,
    wo_ref,
    raw_ref,
    low_ref,
    lse_ref,
    gains_ref,
    cosine_ref,
    sine_ref,
    x_ref,
    near_ref,
    core_ref,
    near_kv_ref,
    core_kv_ref,
    beside_ref,
    feature_ref,
    weights_ref,
    mixed_grad_ref,
    raw_grad_ref,
):
    rows = upstream_ref.shape[0]
    split = near_ref.shape[0]
    width = raw_grad_ref.shape[1]
    queries_width = near_ref.shape[1]
    query_heads = mixed_grad_ref.shape[1] // HEAD_SIZE
    group = query_heads // key_heads
    root = math.sqrt(HEAD_SIZE)
    mixed_grad_ref[...] = against(upstream_ref[...], wo_ref[...]).astype(BF16)
    allowed = causal(rows)
    cosine = cosine_ref[...]
    sine = sine_ref[...]

    def norm_back(h, grad, gain):
        u = raw_ref[:, head_columns(h)]
        scale = inverse_rms(u)
        normal = u * scale
        turned = grad * cosine - pltpu.roll(grad, HEAD_SIZE // 2, 1) * sine
        weighted = turned * gain
        inward = scale * (weighted - normal * jnp.mean(weighted * normal, axis=1, keepdims=True))
        raw_grad_ref[:, head_columns(h)] = inward.astype(BF16)
        return turned * normal

    query_terms = jnp.zeros((rows, HEAD_SIZE), F32)
    key_terms = jnp.zeros((rows, HEAD_SIZE), F32)
    for k in range(key_heads):
        keys = low_ref[:, head_columns(query_heads + k)]
        values = low_ref[:, head_columns(query_heads + key_heads + k)]
        key_grad = jnp.zeros((rows, HEAD_SIZE), F32)
        value_grad = jnp.zeros((rows, HEAD_SIZE), F32)
        for h in range(k * group, (k + 1) * group):
            queries = low_ref[:, head_columns(h)]
            mixed_grad = mixed_grad_ref[:, head_columns(h)]
            scores = against(queries, keys) / root
            probs = jnp.where(allowed, jnp.exp(scores - lse_ref[:, h : h + 1]), 0.0)
            probs_grad = against(mixed_grad, values)
            value_grad += over_rows(probs.astype(BF16), mixed_grad)
            inner = jnp.sum(probs * probs_grad, axis=1, keepdims=True)
            scores_grad = (probs * (probs_grad - inner)).astype(BF16)
            query_grad = jnp.dot(scores_grad, keys, preferred_element_type=F32) / root
            key_grad += over_rows(scores_grad, queries)
            query_terms += norm_back(h, query_grad, gains_ref[0:1, :])
        key_terms += norm_back(query_heads + k, key_grad / root, gains_ref[1:2, :])
        raw_grad_ref[:, head_columns(query_heads + key_heads + k)] = value_grad.astype(BF16)
    raw_grad = raw_grad_ref[...]
    for part, (query_ref, kv_ref) in enumerate(
        ((near_ref, near_kv_ref), (core_ref, core_kv_ref))
    ):
        feature_ref[:, part * split : (part + 1) * split] = (
            against(raw_grad[:, :queries_width], query_ref[...])
            + against(raw_grad[:, queries_width:], kv_ref[:, : width - queries_width])
        ).astype(BF16)
    feature_ref[:, 2 * split : 2 * split + HEAD_SIZE] = query_terms.astype(BF16)
    feature_ref[:, 2 * split + HEAD_SIZE :] = key_terms.astype(BF16)
    count = place_ref.shape[0]
    block = 2 * split // count
    for j in range(count):
        at = pl.ds(pl.multiple_of(place_ref[j] * block, block), block)
        if block % LANES == 0:
            columns = x_ref[:, j * block : (j + 1) * block]
            weights_ref[at, :width] = over_rows(columns, raw_grad).astype(BF16)
    if block % LANES:
        weights_ref[:, :width] = over_rows(x_ref[...], raw_grad).astype(BF16)
    weights_ref[:, width:] = beside_ref[...]


def in_vmem(count):
    return [pl.BlockSpec()] * count


def in_smem():
    return [pl.BlockSpec(memory_space=pltpu.SMEM)]


def attention_back(
    where, upstream, wo, raw, low, lse, gains, cosine, sine, x, weights, beside, key_heads
):
    rows, features = upstream.shape
    query_width = wo.shape[0]
    split = weights[0].shape[0]
    width = low.shape[1]
    whole = width + beside.shape[1]
    shapes = [
        ((rows, features + 2 * HEAD_SIZE), BF16),
        ((features, whole), BF16),
    ]
    operands = [upstream, wo, raw, low, lse, gains, cosine, sine, x, *weights, beside]
    return pl.pallas_call(
        functools.partial(attention_back_kernel, key_heads),
        in_specs=in_smem() + in_vmem(len(operands)),
        out_specs=in_vmem(2),
        out_shape=[jax.ShapeDtypeStruct(*v) for v in shapes],
        scratch_shapes=[pltpu.VMEM((rows, query_width), BF16), pltpu.VMEM((rows, width), BF16)],
        compiler_params=pltpu.CompilerParams(vmem_limit_bytes=40 * 1024 * 1024),
        cost_estimate=SMALL,
    )(jnp.stack(where).astype(jnp.int32), *in_hbm(*operands))


def chunk_places():
    return jnp.stack(
        [lax.axis_index("tp") ^ m for m in range(lax.axis_size("tp"))]
    ).astype(jnp.int32)


def rows_at(index, size):
    return pl.ds(pl.multiple_of(index * size, size), size)


def resid_kernel(place_ref, *refs):
    *pieces, hidden_ref, gain_ref, resid_ref, routed_ref = refs
    rows = pieces[0].shape[0]
    for m, piece in enumerate(pieces):
        at = rows_at(place_ref[m], rows)
        resid = hidden_ref[at, :].astype(F32) + piece[...].astype(F32)
        resid_ref[at, :] = resid
        routed_ref[at, :] = (resid * inverse_rms(resid) * gain_ref[...]).astype(BF16)


def resid_and_routed(pieces, hidden, gain):
    return pl.pallas_call(
        resid_kernel,
        in_specs=in_smem() + in_vmem(len(pieces) + 2),
        out_specs=in_vmem(2),
        out_shape=[
            jax.ShapeDtypeStruct(hidden.shape, F32),
            jax.ShapeDtypeStruct(hidden.shape, BF16),
        ],
        compiler_params=pltpu.CompilerParams(vmem_limit_bytes=6 * 1024 * 1024),
        cost_estimate=SMALL,
    )(chunk_places(), *pieces, hidden, gain)


def resid_back_kernel(parts, place_ref, column_ref, *refs):
    pieces = refs[: 2 * parts]
    (
        resid_a_ref,
        resid_b_ref,
        routed_a_ref,
        routed_b_ref,
        ids_ref,
        router_ref,
        gain_ref,
        upstream_ref,
        mixed_ref,
        grad_ref,
        low_ref,
        beside_ref,
        keep_ref,
        send_ref,
        returned_ref,
        wide_ref,
    ) = refs[2 * parts :]
    rows, features = upstream_ref.shape
    expert_count = router_ref.shape[1]
    chunk = pieces[0].shape[0]
    for h in range(2):
        for m in range(parts):
            returned_ref[rows_at(place_ref[m] + h * parts, chunk), :] = pieces[h * parts + m][...]
    routed = jnp.concatenate([routed_a_ref[...], routed_b_ref[...]], axis=0)
    resid = jnp.concatenate([resid_a_ref[...], resid_b_ref[...]], axis=0)
    logits = jnp.dot(routed, router_ref[...], preferred_element_type=F32)
    lane = lax.broadcasted_iota(jnp.int32, (rows, expert_count), 1)
    named = ids_ref[:, 0:1] == lane
    for k in range(1, TOP):
        named = named | (ids_ref[:, k : k + 1] == lane)
    exponent = jnp.exp(logits - jnp.max(logits, axis=1, keepdims=True))
    router = exponent / jnp.sum(exponent, axis=1, keepdims=True)
    chosen = jnp.where(named, router, 0.0)
    total = jnp.sum(chosen, axis=1, keepdims=True)
    gates = chosen / total
    tail = returned_ref[:, features:].astype(F32)
    tail = tail + pltpu.roll(tail, tail.shape[1] - expert_count, 1)
    grad_gates = jnp.where(named, tail[:, :expert_count], 0.0)
    inner = jnp.sum(grad_gates * gates, axis=1, keepdims=True)
    grad_router = jnp.where(named, (grad_gates - inner) / total, 0.0)
    inner = jnp.sum(router * grad_router, axis=1, keepdims=True)
    grad_logits = (router * (grad_router - inner)).astype(BF16)
    grad_routed = returned_ref[:, :features].astype(F32) + against(grad_logits, router_ref[...])
    scale = inverse_rms(resid)
    normal = resid * scale
    weighted = grad_routed * gain_ref[...]
    inner = jnp.mean(weighted * normal, axis=1, keepdims=True)
    grad = upstream_ref[...].astype(F32) + scale * (weighted - normal * inner)
    grad_ref[...] = grad
    low_ref[...] = grad.astype(BF16)
    half = column_ref.shape[0] // 2
    for j in range(half):
        for k, out_ref in ((j, keep_ref), (half + j, send_ref)):
            columns = pl.ds(pl.multiple_of(column_ref[k] * LANES, LANES), LANES)
            out_ref[j * LANES : (j + 1) * LANES, :] = over_rows(
                mixed_ref[:, columns], low_ref[...]
            ).astype(BF16)
    wide_ref[...] = jnp.zeros(wide_ref.shape, BF16)
    wide_ref[:, :expert_count] = grad_logits
    one = lax.broadcasted_iota(jnp.int32, wide_ref.shape, 1) == expert_count
    beside_ref[...] = (
        over_rows(routed, wide_ref[...])
        + over_rows((grad_routed * normal).astype(BF16), one.astype(F32).astype(BF16))
    ).astype(BF16)


def resid_back(pieces, resid, routed, ids, router, gain, upstream, mixed, columns):
    parts = len(pieces) // 2
    rows, features = upstream.shape
    expert_count = router.shape[1]
    wide = -(-(expert_count + 1) // LANES) * LANES
    half = mixed.shape[1] // 2
    shapes = [
        ((rows, features), F32),
        ((rows, features), BF16),
        ((features, wide), BF16),
        ((half, features), BF16),
        ((half, features), BF16),
    ]
    operands = [*pieces, *in_hbm(*resid, *routed, ids, router, gain, upstream, mixed)]
    return pl.pallas_call(
        functools.partial(resid_back_kernel, parts),
        in_specs=in_smem() * 2 + in_vmem(len(operands)),
        out_specs=in_vmem(len(shapes)),
        out_shape=[jax.ShapeDtypeStruct(*v) for v in shapes],
        scratch_shapes=[
            pltpu.VMEM((rows, pieces[0].shape[1]), BF16),
            pltpu.VMEM((rows, wide), BF16),
        ],
        compiler_params=pltpu.CompilerParams(vmem_limit_bytes=40 * 1024 * 1024),
        cost_estimate=SMALL,
    )(chunk_places(), jnp.stack(columns).astype(jnp.int32), *operands)


def input_kernel(ordered, place_ref, block_ref, *refs):
    *pieces, hidden_ref, resid_grad_ref, gain_ref, result_ref, late_ref, total_ref = refs
    features = hidden_ref.shape[1]
    rows = pieces[0].shape[0]
    count = block_ref.shape[0]
    block = features // count
    for m, piece in enumerate(pieces):
        total_ref[rows_at(place_ref[m], rows), :] = piece[...]
    hidden = hidden_ref[...].astype(F32)
    scale = inverse_rms(hidden)
    columns = [
        slice(j * block, (j + 1) * block)
        if ordered
        else pl.ds(pl.multiple_of(block_ref[j] * block, block), block)
        for j in range(count)
    ]
    inner = jnp.zeros((hidden.shape[0], 1), F32)
    for j in range(count):
        normal = hidden_ref[:, columns[j]].astype(F32) * scale
        grad = total_ref[:, j * block : (j + 1) * block].astype(F32)
        terms = grad * normal
        inner += jnp.sum(terms * gain_ref[:, columns[j]], axis=1, keepdims=True)
        late_ref[j : j + 1, :block] = jnp.sum(terms, axis=0, keepdims=True)
    inner = inner * (1.0 / features)
    for j in range(count):
        normal = hidden_ref[:, columns[j]].astype(F32) * scale
        weighted = total_ref[:, j * block : (j + 1) * block].astype(F32) * gain_ref[:, columns[j]]
        result_ref[:, columns[j]] = resid_grad_ref[:, columns[j]] + scale * (
            weighted - normal * inner
        )
    heads = jnp.sum(total_ref[:, features:].astype(F32), axis=0, keepdims=True)
    late_ref[:, block:] = jnp.broadcast_to(heads, (count, heads.shape[1]))


def input_gradient(pieces, hidden, resid_grad, gain, where):
    rows, features = hidden.shape
    count = len(where)
    extra = pieces[0].shape[1] - features
    return pl.pallas_call(
        functools.partial(input_kernel, absolute()),
        in_specs=in_smem() * 2 + in_vmem(len(pieces) + 3),
        out_specs=in_vmem(2),
        out_shape=[
            jax.ShapeDtypeStruct((rows, features), F32),
            jax.ShapeDtypeStruct((count, features // count + extra), F32),
        ],
        scratch_shapes=[pltpu.VMEM((rows, pieces[0].shape[1]), BF16)],
        compiler_params=pltpu.CompilerParams(vmem_limit_bytes=24 * 1024 * 1024),
        cost_estimate=SMALL,
    )(chunk_places(), jnp.stack(where).astype(jnp.int32), *pieces, *in_hbm(hidden, resid_grad, gain))


def widen_kernel(place_ref, near_ref, core_ref, result_ref):
    early = pl.program_id(0) < pl.num_programs(0) // 2
    result_ref[...] = jnp.where(early, near_ref[...], core_ref[...]).astype(F32)


def widen_blocks(near, core, where):
    count = len(where)
    features = near.shape[1]
    block = 2 * near.shape[0] // count
    half = count // 2
    first = pl.BlockSpec((block, features), lambda i, s: (jnp.minimum(i, half - 1), 0))
    second = pl.BlockSpec((block, features), lambda i, s: (jnp.maximum(i - half, 0), 0))
    return pl.pallas_call(
        widen_kernel,
        grid_spec=pltpu.PrefetchScalarGridSpec(
            num_scalar_prefetch=1,
            grid=(count,),
            in_specs=[first, second],
            out_specs=pl.BlockSpec((block, features), lambda i, s: (s[i], 0)),
        ),
        out_shape=jax.ShapeDtypeStruct((block * count, features), F32),
        compiler_params=pltpu.CompilerParams(vmem_limit_bytes=24 * 1024 * 1024),
        cost_estimate=SMALL,
    )(jnp.stack(where).astype(jnp.int32), near, core)


def shards(
    hidden_in,
    expert_ids,
    attention_gain,
    query_gain,
    key_gain,
    query_weight,
    key_matrix,
    value_matrix,
    output_weight,
    expert_gain,
    router_weight,
    gate_up_weight,
    down_weight,
    output_grad,
):
    tokens, features = hidden_in.shape
    owners = lax.axis_size("ep")
    local_experts = gate_up_weight.shape[0]
    expert_count = local_experts * owners
    rows_a = tokens // 2

    head_share = query_gain.shape[0]
    share = router_weight.shape[0]
    small_rows = max(tokens, share)
    padded = lambda v: jnp.pad(v.astype(BF16), ((0, small_rows - v.shape[0]), (0, 0)))
    small = jnp.concatenate(
        [
            padded(router_weight),
            padded(jnp.stack([attention_gain, expert_gain], axis=1)),
            padded(jnp.stack([query_gain, key_gain], axis=1)),
            padded(expert_ids),
        ],
        axis=1,
    )
    small_width = small.shape[1]
    small = jnp.pad(small, ((0, 0), (0, -small_width % LANES)))
    packed = jnp.concatenate([key_matrix, value_matrix], axis=1)
    packed_width = packed.shape[1]
    together = small_rows == share
    if together:
        packed = jnp.concatenate([packed, small], axis=1)
    packed_hops = gather_hops(packed)
    hops = gather_hops(query_weight)
    packed_near = gather_near(packed, packed_hops)
    packed_core = gather_core(packed_near, packed_hops)
    if together:
        small = jnp.concatenate(
            [packed_near[:, packed_width:], packed_core[:, packed_width:]], axis=0
        )
    else:
        small = lax.all_gather(small, "ep", axis=0, tiled=True)
    small = put_blocks(small, 0).reshape(owners, small_rows, -1)
    by_feature = small[:, :share, : expert_count + 2].reshape(features, -1)
    router_full = by_feature[:, :expert_count]
    attn_gain_full = by_feature[:, expert_count].astype(F32)[None, :]
    mlp_gain_full = by_feature[:, expert_count + 1].astype(F32)[None, :]
    gains = (
        small[:, :head_share, expert_count + 2 : expert_count + 4]
        .reshape(HEAD_SIZE, 2)
        .astype(F32)
        .T
    )
    ids_all = small[:, :tokens, expert_count + 4 : small_width].reshape(-1, TOP).astype(jnp.int32)
    wd = down_weight.reshape(-1, features)
    normed_low = norm_rows(hidden_in.astype(F32), attn_gain_full).astype(BF16)
    normed_rel = pick_blocks(normed_low, 1)
    positions = jnp.arange(tokens, dtype=jnp.int32)
    cosine, sine_table = rope_tables(positions, HEAD_SIZE)
    (
        hops,
        packed_core,
        normed_rel,
        cosine,
        sine_table,
        gains,
        router_full,
        attn_gain_full,
        mlp_gain_full,
        ids_all,
        output_all,
        gate_up_low,
    ) = join(
        hops,
        packed_core,
        normed_rel,
        cosine,
        sine_table,
        gains,
        router_full,
        attn_gain_full,
        mlp_gain_full,
        ids_all,
        output_grad,
        gate_up_weight,
    )

    near = gather_near(query_weight, hops)
    weights_rel = [near, gather_core(near, hops), packed_near, packed_core]
    output_all = lax.all_gather(output_all, "ep", axis=0, tiled=True)
    query_width = query_weight.shape[1]
    key_width = key_matrix.shape[1]
    key_heads = key_width // HEAD_SIZE
    raw, low, attention_output, lse, *head_parts = attention(
        normed_rel, *weights_rel, gains, cosine, sine_table, output_weight, key_heads
    )
    (head_parts,) = join(head_parts)

    hops = reduce_hops(head_parts[0])
    wgu = gate_up_low.transpose(1, 0, 2).reshape(features, -1)
    hops, wgu = join(hops, wgu)

    chunk = reduce_total(head_parts[0], hops)
    hops, hops_b = join(spread_hops(chunk), reduce_hops(head_parts[1]))

    resid_a, routed_a = resid_and_routed([chunk] + hops, hidden_in[:rows_a], mlp_gain_full)
    chunk = reduce_total(head_parts[1], hops_b)
    hops_a, hops = join(gather_hops(routed_a), spread_hops(chunk))

    resid_b, routed_b = resid_and_routed([chunk] + hops, hidden_in[rows_a:], mlp_gain_full)
    near_a = gather_near(routed_a, hops_a)
    core_a = gather_core(near_a, hops_a)
    hops_b = gather_hops(routed_b)
    lined = places()
    where = [2 * b + h for h in range(2) for b in lined]

    def experts(piece, x):
        rows = slice(piece * owners // 2, (piece + 1) * owners // 2)
        return run_experts(
            x, output_all, ids_all, where[rows], router_full, wgu, wd, local_experts
        )

    keep_a, joined_0, hidden_0 = experts(0, near_a)
    send_a, joined_1, hidden_1 = experts(1, core_a)
    hops_b, send_a, keep_a = join(hops_b, send_a, keep_a)

    near_b = gather_near(routed_b, hops_b)
    core_b = gather_core(near_b, hops_b)
    come = scatter_swap(send_a)
    keep_b, joined_2, hidden_2 = experts(2, near_b)
    come, core_b, keep_b = join(come, core_b, keep_b)

    sums_a = scatter_sums(keep_a, come)
    hops_a = scatter_hops(sums_a)
    send_b, joined_3, hidden_3 = experts(3, core_b)
    hops_a, send_b = join(hops_a, send_b)
    joined = [joined_0, joined_1, joined_2, joined_3]
    hidden = [hidden_0, hidden_1, hidden_2, hidden_3]
    routed_pieces = [near_a, core_a, near_b, core_b]

    come = scatter_swap(send_b)
    total_a = scatter_total(sums_a, hops_a)
    hops = reduce_hops(total_a)
    come, hidden = join(come, hidden)

    sums_b = scatter_sums(keep_b, come)
    hops_b = scatter_hops(sums_b)
    mixture_parts = mixture_product(hidden, wd, lined)
    chunk_a = reduce_total(total_a, hops)
    spread_a, hops_b, mixture_parts, joined = join(
        spread_hops(chunk_a), hops_b, mixture_parts, joined
    )

    mixture = lax.psum_scatter(mixture_parts, "ep", scatter_dimension=0, tiled=True)
    total_b = scatter_total(sums_b, hops_b)
    (hops,) = join(reduce_hops(total_b))
    chunk_b = reduce_total(total_b, hops)
    (spread_b,) = join(spread_hops(chunk_b))

    columns = (
        [jnp.int32(b) for b in range(attention_output.shape[1] // LANES)] if absolute() else lined
    )
    grad_resid, grad_attended, by_feature, output_keep, output_send = resid_back(
        [chunk_a, *spread_a, chunk_b, *spread_b],
        [resid_a, resid_b],
        [routed_a, routed_b],
        expert_ids,
        router_full,
        mlp_gain_full,
        output_grad,
        attention_output,
        columns,
    )

    feature_part, weights_grad = attention_back(
        lined,
        grad_attended,
        output_weight,
        raw,
        low,
        lse,
        gains,
        cosine,
        sine_table,
        normed_rel,
        weights_rel,
        by_feature,
        key_heads,
    )
    come, feature_part, weights_grad = join(
        scatter_swap(output_send), feature_part, weights_grad
    )

    weights_rows = lax.psum_scatter(weights_grad, "ep", scatter_dimension=0, tiled=True)
    hops = reduce_hops(feature_part)
    output_sums = scatter_sums(output_keep, come)
    output_hops = scatter_hops(output_sums)
    down_grad = down_product(hidden, output_all, where).reshape(down_weight.shape)
    hops, output_hops, down_grad, mixture, joined = join(
        hops, output_hops, down_grad, mixture, joined
    )

    chunk = reduce_total(feature_part, hops)
    hops = spread_hops(chunk)
    mixture_hops = reduce_hops(mixture)
    output_share = scatter_total(output_sums, output_hops)
    gate_up_grad = gate_up_product(routed_pieces, joined, gate_up_weight.shape)
    hops, gate_up_grad, output_share = join(hops, gate_up_grad, output_share)

    output_hops = gather_hops(output_share)
    input_grad, late = input_gradient(
        [chunk, *hops], hidden_in, grad_resid, attn_gain_full, lined
    )
    late_come = scatter_swap(late[owners // 2 :])
    late_come, output_hops, mixture_hops = join(late_come, output_hops, mixture_hops)

    mixture_chunk = reduce_total(mixture, mixture_hops)
    mixture_hops = spread_hops(mixture_chunk)
    near = gather_near(output_share, output_hops)
    output_core = gather_core(near, output_hops)
    late_sums = scatter_sums(late[: owners // 2], late_come)
    late_hops = scatter_hops(late_sums)
    output_weight_grad = widen_blocks(near, output_core, lined)
    late_hops, output_weight_grad, weights_rows, mixture_hops = join(
        late_hops, output_weight_grad, weights_rows, mixture_hops
    )
    weights_rows = weights_rows.astype(F32)
    late = scatter_total(late_sums, late_hops)[0]
    head_grads = lax.dynamic_slice_in_dim(
        late[share:].reshape(2, HEAD_SIZE), lax.axis_index("ep") * head_share, head_share, 1
    )
    early = weights_rows[:, query_width + 2 * key_width :]
    mixture = spread_total(mixture_chunk, mixture_hops)
    block_out = (jnp.concatenate([resid_a, resid_b], axis=0) + mixture.astype(F32)).astype(BF16)
    return (
        block_out,
        input_grad,
        late[:share],
        head_grads[0],
        head_grads[1],
        weights_rows[:, :query_width],
        weights_rows[:, query_width : query_width + key_width],
        weights_rows[:, query_width + key_width : query_width + 2 * key_width],
        output_weight_grad,
        early[:, expert_count],
        early[:, :expert_count],
        gate_up_grad,
        down_grad,
    )


def solution(mesh):
    in_specs = (
        P("ep", None),
        P("ep", None),
        P("ep"),
        P("ep"),
        P("ep"),
        P("ep", "tp"),
        P("ep", "tp"),
        P("ep", "tp"),
        P("tp", None),
        P("ep"),
        P("ep", None),
        P("ep", None, "tp"),
        P("ep", "tp", None),
        P("ep", None),
    )
    out_specs = (
        P("ep", None),
        P("ep", None),
        P("ep"),
        P("ep"),
        P("ep"),
        P("ep", "tp"),
        P("ep", "tp"),
        P("ep", "tp"),
        P("tp", None),
        P("ep"),
        P("ep", None),
        P("ep", None, "tp"),
        P("ep", "tp", None),
    )
    return jax.shard_map(shards, mesh=mesh, in_specs=in_specs, out_specs=out_specs, check_vma=False)
```

```python
import functools
import math

import jax
import jax.numpy as jnp
from jax import lax
from jax.experimental import pallas as pl
from jax.experimental.pallas import tpu as pltpu
from jax.sharding import PartitionSpec as P

HEAD_SIZE = 128
TOP = 8
PAIR = 64
LANES = 128

EPSILON = 1e-06
THETA = 1000000.0
F32 = jnp.float32
BF16 = jnp.bfloat16
SMALL = pl.CostEstimate(flops=0, bytes_accessed=1024, transcendentals=0)


def norm_rows(value_rows, norm_gain):
    return (
        value_rows
        * lax.rsqrt(jnp.mean(value_rows * value_rows, axis=-1, keepdims=True) + EPSILON)
        * norm_gain
    )


def rope_tables(positions, head_size):
    halfway = head_size // 2
    inverse = THETA ** (-(jnp.arange(halfway, dtype=jnp.float32) * 2.0) / head_size)
    angles = positions.astype(jnp.float32)[:, None] * inverse[None, :]
    cosine, sine = jnp.cos(angles), jnp.sin(angles)
    return (
        jnp.concatenate([cosine, cosine], axis=1),
        jnp.concatenate([-sine, sine], axis=1),
    )


SWAPPED = 8


def swap(value, axis, mask):
    count = lax.axis_size(axis)
    return lax.ppermute(value, axis, [(i, i ^ mask) for i in range(count)])


def join(*values):
    return lax.optimization_barrier(values)


ORDER = (0, 2, 4, 6, 1, 3, 5, 7)


def plus(*values):
    total = values[0].astype(F32)
    for v in values[1:]:
        total = total + v.astype(F32)
    return total.astype(values[0].dtype)


def absolute():
    return lax.axis_size("ep") > SWAPPED


def in_hbm(*values):
    return [pltpu.with_memory_space_constraint(v, pltpu.HBM) for v in values]


def stack_kernel(*refs):
    *pieces, result_ref = refs
    rows = pieces[0].shape[0]
    for i, piece in enumerate(pieces):
        result_ref[i * rows : (i + 1) * rows, :] = piece[...]


def stack_rows(pieces):
    rows = pieces[0].shape[0]
    return pl.pallas_call(
        stack_kernel,
        out_shape=jax.ShapeDtypeStruct(
            (len(pieces) * rows,) + pieces[0].shape[1:], pieces[0].dtype
        ),
        compiler_params=pltpu.CompilerParams(vmem_limit_bytes=8 * 1024 * 1024),
        cost_estimate=SMALL,
    )(*pieces)


def gather_hops(value):
    if absolute():
        return [lax.all_gather(value, "ep", axis=0, tiled=True)]
    return [swap(value, "ep", m) for m in ORDER[1:4]]


def gather_near(value, hops):
    if absolute():
        return hops[0][: hops[0].shape[0] // 2]
    return stack_rows([value] + hops)


def gather_core(near, hops):
    if absolute():
        return hops[0][hops[0].shape[0] // 2 :]
    return swap(near, "ep", 1)


def scatter_swap(send):
    return send if absolute() else swap(send, "ep", 1)


def scatter_sums(keep, come):
    if absolute():
        return [jnp.concatenate([keep, come], axis=0)]
    rows = keep.shape[0] // 4
    return [
        plus(keep[i * rows : (i + 1) * rows], come[i * rows : (i + 1) * rows]) for i in range(4)
    ]


def scatter_hops(sums):
    if absolute():
        return [lax.psum_scatter(sums[0], "ep", scatter_dimension=0, tiled=True)]
    return [swap(v, "ep", m) for v, m in zip(sums[1:], ORDER[1:4])]


def scatter_total(sums, hops):
    return hops[0] if absolute() else plus(sums[0], *hops)


def chunk_of(value, index):
    rows = value.shape[0] // lax.axis_size("tp")
    return lax.dynamic_slice_in_dim(value, index * rows, rows, 0)


def reduce_hops(value):
    mine = lax.axis_index("tp")
    return [swap(chunk_of(value, mine ^ m), "tp", m) for m in range(1, lax.axis_size("tp"))]


def reduce_total(value, hops):
    return plus(chunk_of(value, lax.axis_index("tp")), *hops)


def spread_hops(chunk):
    return [swap(chunk, "tp", m) for m in range(1, lax.axis_size("tp"))]


def spread_total(chunk, hops):
    mine = lax.axis_index("tp")
    rows = chunk.shape[0]
    result = jnp.zeros(((len(hops) + 1) * rows,) + chunk.shape[1:], chunk.dtype)
    for m, piece in enumerate([chunk] + hops):
        result = lax.dynamic_update_slice_in_dim(result, piece, (mine ^ m) * rows, 0)
    return result


def places():
    if absolute():
        return [jnp.int32(b) for b in range(lax.axis_size("ep"))]
    return [lax.axis_index("ep") ^ m for m in ORDER]


def pick_blocks(value, axis):
    count = lax.axis_size("ep")
    if count > SWAPPED:
        return value
    mine = lax.axis_index("ep")
    size = value.shape[axis] // count
    return jnp.concatenate(
        [lax.dynamic_slice_in_dim(value, (mine ^ m) * size, size, axis) for m in ORDER],
        axis=axis,
    )


def put_blocks(value, axis):
    count = lax.axis_size("ep")
    if count > SWAPPED:
        return value
    mine = lax.axis_index("ep")
    size = value.shape[axis] // count
    place = lambda m: (m // 2 + (m % 2) * (count // 2)) * size
    return jnp.concatenate(
        [lax.dynamic_slice_in_dim(value, place(mine ^ b), size, axis) for b in range(count)],
        axis=axis,
    )


def expert_kernel(
    local,
    place_ref,
    x_ref,
    g0_ref,
    g1_ref,
    ids0_ref,
    ids1_ref,
    router_ref,
    wgu_in_ref,
    wd_in_ref,
    dx_ref,
    joined_ref,
    hidden_ref,
    wgu_ref,
    wd_ref,
    arrived,
):
    rows = x_ref.shape[0]
    features = x_ref.shape[1]
    expert_count = router_ref.shape[1]
    hidden_count = wd_ref.shape[0]
    group = 3
    count = hidden_count // LANES // group
    copies = [
        pltpu.make_async_copy(wgu_in_ref, wgu_ref, arrived.at[0]),
        pltpu.make_async_copy(wd_in_ref, wd_ref, arrived.at[1]),
    ]

    @pl.when(pl.program_id(0) == 0)
    def _():
        for copy in copies:
            copy.start()

    extra = dx_ref.shape[1] - features
    base = place_ref[0]
    x = x_ref[...]
    upstream = jnp.concatenate([g0_ref[...], g1_ref[...]], axis=0)
    ids = jnp.concatenate([ids0_ref[...], ids1_ref[...]], axis=0)
    logits = jnp.dot(x, router_ref[...], preferred_element_type=F32)
    lane = lax.broadcasted_iota(jnp.int32, (rows, expert_count), 1)
    named = ids[:, 0:1] == lane
    for k in range(1, TOP):
        named = named | (ids[:, k : k + 1] == lane)
    exponent = jnp.exp(logits - jnp.max(logits, axis=1, keepdims=True))
    router = exponent / jnp.sum(exponent, axis=1, keepdims=True)
    chosen = jnp.where(named, router, 0.0)
    gates = chosen / jnp.sum(chosen, axis=1, keepdims=True)
    gate = [
        jnp.sum(jnp.where(lane == base + j, gates, 0.0), axis=1, keepdims=True)
        for j in range(local)
    ]
    left = lax.broadcasted_iota(jnp.int32, (rows, LANES), 1) < PAIR
    per_expert = hidden_count // local // PAIR
    gate_sum = [jnp.zeros((rows, LANES), F32) for _ in range(local)]

    @pl.when(pl.program_id(0) == 0)
    def _():
        for copy in copies:
            copy.wait()

    def products(q):
        wide = group * LANES
        act = jnp.dot(
            x, wgu_ref[:, 2 * q * wide : 2 * (q + 1) * wide], preferred_element_type=F32
        )
        back = lax.dot_general(
            upstream,
            wd_ref[q * wide : (q + 1) * wide, :],
            (((1,), (1,)), ((), ())),
            preferred_element_type=F32,
        )
        return act, back

    def elementwise(q, act, back):
        for i in range(group):
            p = q * group + i
            one, two = 2 * p // per_expert, (2 * p + 1) // per_expert
            first = act[:, 2 * i * LANES : (2 * i + 1) * LANES]
            second = act[:, (2 * i + 1) * LANES : (2 * i + 2) * LANES]
            g = jnp.where(left, first, pltpu.roll(second, PAIR, 1))
            u = jnp.where(left, pltpu.roll(first, PAIR, 1), second)
            gh = back[:, i * LANES : (i + 1) * LANES]
            if one == two:
                scale = jnp.broadcast_to(gate[one], (rows, LANES))
            else:
                scale = jnp.where(left, gate[one], gate[two])
            sig = lax.logistic(g)
            silu = g * sig
            hid = silu * u
            product = hid * gh
            if one == two:
                gate_sum[one] += product
            else:
                gate_sum[one] += jnp.where(left, product, 0.0)
                gate_sum[two] += jnp.where(left, 0.0, product)
            hidden_ref[:, p * LANES : (p + 1) * LANES] = (hid * scale).astype(BF16)
            gs = gh * scale
            dg = gs * u * sig * (1.0 + g * (1.0 - sig))
            du = gs * silu
            joined_ref[:, 2 * p * LANES : (2 * p + 1) * LANES] = jnp.where(
                left, dg, pltpu.roll(du, PAIR, 1)
            ).astype(BF16)
            joined_ref[:, (2 * p + 1) * LANES : (2 * p + 2) * LANES] = jnp.where(
                left, pltpu.roll(dg, PAIR, 1), du
            ).astype(BF16)

    waiting = []
    for q in range(count):
        waiting.append((q, *products(q)))
        if q:
            elementwise(*waiting.pop(0))
    elementwise(*waiting.pop(0))
    dx = lax.dot_general(
        joined_ref[...], wgu_ref[...], (((1,), (1,)), ((), ())), preferred_element_type=F32
    )
    dx_ref[:, :features] = dx.astype(BF16)
    wide = lax.broadcasted_iota(jnp.int32, (rows, extra), 1)
    tail = jnp.zeros((rows, extra), F32)
    for j in range(local):
        total = jnp.sum(gate_sum[j], axis=1, keepdims=True)
        high = total.astype(BF16).astype(F32)
        tail = jnp.where(wide == base + j, high, tail)
        tail = jnp.where(wide == expert_count + base + j, total - high, tail)
    dx_ref[:, features:] = tail.astype(BF16)


def run_experts(x, g, ids, where, router, wgu, wd, local):
    tokens, features = x.shape
    tile = 256
    block = tokens // len(where)
    steps = tokens // tile
    expert_count = router.shape[1]
    extra = -(-2 * expert_count // LANES) * LANES
    place = jnp.stack([lax.axis_index("ep") * local] + list(where)).astype(jnp.int32)
    found = lambda width, j: pl.BlockSpec((block, width), lambda i, s: (s[1 + 2 * i + j], 0))
    whole = pl.BlockSpec(router.shape, lambda i, s: (0, 0), pipeline_mode=pl.Buffered(1))
    anywhere = pl.BlockSpec(memory_space=pl.ANY)
    by_rows = lambda width: pl.BlockSpec((tile, width), lambda i, s: (i, 0))
    in_specs = [
        by_rows(features),
        found(features, 0),
        found(features, 1),
        found(TOP, 0),
        found(TOP, 1),
        whole,
        anywhere,
        anywhere,
    ]
    g, wgu, wd = in_hbm(g, wgu, wd)
    operands = [place, x, g, g, ids, ids, router, wgu, wd]
    return pl.pallas_call(
        functools.partial(expert_kernel, local),
        grid_spec=pltpu.PrefetchScalarGridSpec(
            num_scalar_prefetch=1,
            grid=(steps,),
            in_specs=in_specs,
            out_specs=[
                by_rows(features + extra),
                by_rows(wgu.shape[1]),
                by_rows(wd.shape[0]),
            ],
            scratch_shapes=[
                pltpu.VMEM(wgu.shape, BF16),
                pltpu.VMEM(wd.shape, BF16),
                pltpu.SemaphoreType.DMA((2,)),
            ],
        ),
        out_shape=[
            pltpu.HBM((tokens, features + extra), BF16),
            pltpu.HBM((tokens, wgu.shape[1]), BF16),
            pltpu.HBM((tokens, wd.shape[0]), BF16),
        ],
        compiler_params=pltpu.CompilerParams(vmem_limit_bytes=32 * 1024 * 1024),
        cost_estimate=SMALL,
    )(*operands)


def gate_up_kernel(*refs):
    *operands, result_ref = refs
    count = len(operands) // 2
    total = None
    for x_ref, joined_ref in zip(operands[:count], operands[count:]):
        part = lax.dot_general(
            x_ref[...], joined_ref[...], (((0,), (0,)), ((), ())), preferred_element_type=F32
        )
        total = part if total is None else total + part
    width = result_ref.shape[2]
    for e in range(result_ref.shape[0]):
        result_ref[e] = total[:, e * width : (e + 1) * width]


def gate_up_product(pieces, joined, shape):
    rows, features = pieces[0].shape
    width = joined[0].shape[1]
    tile = 256
    whole = pl.BlockSpec((rows, width), lambda i: (0, 0), pipeline_mode=pl.Buffered(1))
    return pl.pallas_call(
        gate_up_kernel,
        grid=(features // tile,),
        in_specs=[pl.BlockSpec((rows, tile), lambda i: (0, i)) for _ in pieces]
        + [whole for _ in joined],
        out_specs=pl.BlockSpec((shape[0], tile, shape[2]), lambda i: (0, i, 0)),
        out_shape=jax.ShapeDtypeStruct(shape, F32),
        compiler_params=pltpu.CompilerParams(vmem_limit_bytes=56 * 1024 * 1024),
        cost_estimate=SMALL,
    )(*in_hbm(*pieces, *joined))


def down_kernel(place_ref, *refs):
    *pieces, g_ref, result_ref, sorted_ref = refs
    blocks = place_ref.shape[0] // len(pieces)
    block = pieces[0].shape[0] // blocks
    for i, hidden_ref in enumerate(pieces):
        for k in range(blocks):
            start = pl.multiple_of(place_ref[i * blocks + k] * block, block)
            sorted_ref[pl.ds(start, block), :] = hidden_ref[k * block : (k + 1) * block, :]
    result_ref[...] = lax.dot_general(
        sorted_ref[...], g_ref[...], (((0,), (0,)), ((), ())), preferred_element_type=F32
    )


def down_product(hidden, g, where):
    rows, features = g.shape
    width = hidden[0].shape[1]
    tile = 256
    return pl.pallas_call(
        down_kernel,
        grid_spec=pltpu.PrefetchScalarGridSpec(
            num_scalar_prefetch=1,
            grid=(width // tile,),
            in_specs=[pl.BlockSpec((v.shape[0], tile), lambda i, s: (0, i)) for v in hidden]
            + [pl.BlockSpec((rows, features), lambda i, s: (0, 0), pipeline_mode=pl.Buffered(1))],
            out_specs=pl.BlockSpec((tile, features), lambda i, s: (i, 0)),
            scratch_shapes=[pltpu.VMEM((rows, tile), BF16)],
        ),
        out_shape=jax.ShapeDtypeStruct((width, features), F32),
        compiler_params=pltpu.CompilerParams(vmem_limit_bytes=57 * 1024 * 1024),
        cost_estimate=SMALL,
    )(jnp.stack(where).astype(jnp.int32), *in_hbm(*hidden, g))


def mixture_kernel(
    place_ref, upper0_ref, upper1_ref, lower0_ref, lower1_ref, wd_ref, result_ref
):
    early = pl.program_id(0) < pl.num_programs(0) // 2
    rows = jnp.concatenate(
        [
            jnp.where(early, upper0_ref[...], upper1_ref[...]),
            jnp.where(early, lower0_ref[...], lower1_ref[...]),
        ],
        axis=0,
    )
    result_ref[...] = jnp.dot(rows, wd_ref[...], preferred_element_type=F32).astype(BF16)


def mixture_product(hidden, wd, where):
    count = len(where)
    block = 2 * hidden[0].shape[0] // count
    width, features = wd.shape
    first = pl.BlockSpec((block, width), lambda i, s: (jnp.minimum(i, count // 2 - 1), 0))
    second = pl.BlockSpec((block, width), lambda i, s: (jnp.maximum(i - count // 2, 0), 0))
    return pl.pallas_call(
        mixture_kernel,
        grid_spec=pltpu.PrefetchScalarGridSpec(
            num_scalar_prefetch=1,
            grid=(count,),
            in_specs=[first, second, first, second]
            + [pl.BlockSpec((width, features), lambda i, s: (0, 0))],
            out_specs=pl.BlockSpec((2 * block, features), lambda i, s: (s[i], 0)),
        ),
        out_shape=pltpu.HBM((2 * block * count, features), BF16),
        compiler_params=pltpu.CompilerParams(vmem_limit_bytes=24 * 1024 * 1024),
        cost_estimate=SMALL,
    )(jnp.stack(where).astype(jnp.int32), *in_hbm(*hidden, wd))


def rotated(value, cosine, sine):
    return value * cosine + pltpu.roll(value, HEAD_SIZE // 2, 1) * sine


def inverse_rms(value):
    return lax.rsqrt(jnp.mean(value * value, axis=1, keepdims=True) + EPSILON)


def head_columns(h):
    return slice(h * HEAD_SIZE, (h + 1) * HEAD_SIZE)


def against(left, right):
    return lax.dot_general(left, right, (((1,), (1,)), ((), ())), preferred_element_type=F32)


def over_rows(left, right):
    return lax.dot_general(left, right, (((0,), (0,)), ((), ())), preferred_element_type=F32)


def causal(rows):
    return lax.broadcasted_iota(jnp.int32, (rows, rows), 1) <= lax.broadcasted_iota(
        jnp.int32, (rows, rows), 0
    )


def attention_kernel(
    key_heads,
    x_ref,
    near_ref,
    core_ref,
    near_kv_ref,
    core_kv_ref,
    gains_ref,
    cosine_ref,
    sine_ref,
    wo_ref,
    raw_ref,
    low_ref,
    mixed_ref,
    lse_ref,
    upper_ref,
    lower_ref,
):
    rows = x_ref.shape[0]
    split = near_ref.shape[0]
    query_heads = mixed_ref.shape[1] // HEAD_SIZE
    heads = query_heads + key_heads
    queries = query_heads * HEAD_SIZE
    raw_ref[:, :queries] = jnp.dot(
        x_ref[:, :split], near_ref[...], preferred_element_type=F32
    ) + jnp.dot(x_ref[:, split:], core_ref[...], preferred_element_type=F32)
    wide = 2 * key_heads * HEAD_SIZE
    raw = jnp.dot(
        x_ref[:, :split], near_kv_ref[:, :wide], preferred_element_type=F32
    ) + jnp.dot(x_ref[:, split:], core_kv_ref[:, :wide], preferred_element_type=F32)
    raw_ref[:, queries:] = raw[:, : key_heads * HEAD_SIZE]
    low_ref[:, heads * HEAD_SIZE :] = raw[:, key_heads * HEAD_SIZE :].astype(BF16)
    for h in range(heads):
        u = raw_ref[:, head_columns(h)]
        gain = gains_ref[0:1, :] if h < query_heads else gains_ref[1:2, :]
        low_ref[:, head_columns(h)] = rotated(
            u * inverse_rms(u) * gain, cosine_ref[...], sine_ref[...]
        ).astype(BF16)
    allowed = causal(rows)
    for h in range(query_heads):
        k = query_heads + h * key_heads // query_heads
        scores = against(low_ref[:, head_columns(h)], low_ref[:, head_columns(k)]) / math.sqrt(
            HEAD_SIZE
        )
        scores = jnp.where(allowed, scores, -jnp.inf)
        row_max = jnp.max(scores, axis=1, keepdims=True)
        exps = jnp.exp(scores - row_max)
        total = jnp.sum(exps, axis=1, keepdims=True)
        lse_ref[:, h : h + 1] = row_max + jnp.log(total)
        mixed_ref[:, head_columns(h)] = jnp.dot(
            (exps * (1.0 / total)).astype(BF16),
            low_ref[:, head_columns(k + key_heads)],
            preferred_element_type=F32,
        ).astype(BF16)
    part = jnp.dot(mixed_ref[...], wo_ref[...], preferred_element_type=F32)
    upper_ref[...] = part[: rows // 2].astype(BF16)
    lower_ref[...] = part[rows // 2 :].astype(BF16)


def attention(x, near, core, near_kv, core_kv, gains, cosine, sine, wo, key_heads):
    rows = x.shape[0]
    query_width, features = wo.shape
    width = query_width + 2 * key_heads * HEAD_SIZE
    shapes = [
        ((rows, query_width + key_heads * HEAD_SIZE), F32),
        ((rows, width), BF16),
        ((rows, query_width), BF16),
        ((rows, query_width // HEAD_SIZE), F32),
        ((rows // 2, features), BF16),
        ((rows // 2, features), BF16),
    ]
    return pl.pallas_call(
        functools.partial(attention_kernel, key_heads),
        out_shape=[jax.ShapeDtypeStruct(*v) for v in shapes],
        compiler_params=pltpu.CompilerParams(vmem_limit_bytes=32 * 1024 * 1024),
        cost_estimate=SMALL,
    )(x, near, core, near_kv, core_kv, gains, cosine, sine, wo)


def attention_back_kernel(
    key_heads,
    place_ref,
    upstream_ref,
    wo_ref,
    raw_ref,
    low_ref,
    lse_ref,
    gains_ref,
    cosine_ref,
    sine_ref,
    x_ref,
    near_ref,
    core_ref,
    near_kv_ref,
    core_kv_ref,
    beside_ref,
    feature_ref,
    weights_ref,
    mixed_grad_ref,
    raw_grad_ref,
):
    rows = upstream_ref.shape[0]
    split = near_ref.shape[0]
    width = raw_grad_ref.shape[1]
    queries_width = near_ref.shape[1]
    query_heads = mixed_grad_ref.shape[1] // HEAD_SIZE
    group = query_heads // key_heads
    root = math.sqrt(HEAD_SIZE)
    mixed_grad_ref[...] = against(upstream_ref[...], wo_ref[...]).astype(BF16)
    allowed = causal(rows)
    cosine = cosine_ref[...]
    sine = sine_ref[...]

    def norm_back(h, grad, gain):
        u = raw_ref[:, head_columns(h)]
        scale = inverse_rms(u)
        normal = u * scale
        turned = grad * cosine - pltpu.roll(grad, HEAD_SIZE // 2, 1) * sine
        weighted = turned * gain
        inward = scale * (weighted - normal * jnp.mean(weighted * normal, axis=1, keepdims=True))
        raw_grad_ref[:, head_columns(h)] = inward.astype(BF16)
        return turned * normal

    query_terms = jnp.zeros((rows, HEAD_SIZE), F32)
    key_terms = jnp.zeros((rows, HEAD_SIZE), F32)
    for k in range(key_heads):
        keys = low_ref[:, head_columns(query_heads + k)]
        values = low_ref[:, head_columns(query_heads + key_heads + k)]
        key_grad = jnp.zeros((rows, HEAD_SIZE), F32)
        value_grad = jnp.zeros((rows, HEAD_SIZE), F32)
        for h in range(k * group, (k + 1) * group):
            queries = low_ref[:, head_columns(h)]
            mixed_grad = mixed_grad_ref[:, head_columns(h)]
            scores = against(queries, keys) / root
            probs = jnp.where(allowed, jnp.exp(scores - lse_ref[:, h : h + 1]), 0.0)
            probs_grad = against(mixed_grad, values)
            value_grad += over_rows(probs.astype(BF16), mixed_grad)
            inner = jnp.sum(probs * probs_grad, axis=1, keepdims=True)
            scores_grad = (probs * (probs_grad - inner)).astype(BF16)
            query_grad = jnp.dot(scores_grad, keys, preferred_element_type=F32) / root
            key_grad += over_rows(scores_grad, queries)
            query_terms += norm_back(h, query_grad, gains_ref[0:1, :])
        key_terms += norm_back(query_heads + k, key_grad / root, gains_ref[1:2, :])
        raw_grad_ref[:, head_columns(query_heads + key_heads + k)] = value_grad.astype(BF16)
    raw_grad = raw_grad_ref[...]
    for part, (query_ref, kv_ref) in enumerate(
        ((near_ref, near_kv_ref), (core_ref, core_kv_ref))
    ):
        feature_ref[:, part * split : (part + 1) * split] = (
            against(raw_grad[:, :queries_width], query_ref[...])
            + against(raw_grad[:, queries_width:], kv_ref[:, : width - queries_width])
        ).astype(BF16)
    feature_ref[:, 2 * split : 2 * split + HEAD_SIZE] = query_terms.astype(BF16)
    feature_ref[:, 2 * split + HEAD_SIZE :] = key_terms.astype(BF16)
    count = place_ref.shape[0]
    block = 2 * split // count
    for j in range(count):
        at = pl.ds(pl.multiple_of(place_ref[j] * block, block), block)
        if block % LANES == 0:
            columns = x_ref[:, j * block : (j + 1) * block]
            weights_ref[at, :width] = over_rows(columns, raw_grad).astype(BF16)
    if block % LANES:
        weights_ref[:, :width] = over_rows(x_ref[...], raw_grad).astype(BF16)
    weights_ref[:, width:] = beside_ref[...]


def in_vmem(count):
    return [pl.BlockSpec()] * count


def in_smem():
    return [pl.BlockSpec(memory_space=pltpu.SMEM)]


def attention_back(
    where, upstream, wo, raw, low, lse, gains, cosine, sine, x, weights, beside, key_heads
):
    rows, features = upstream.shape
    query_width = wo.shape[0]
    split = weights[0].shape[0]
    width = low.shape[1]
    whole = width + beside.shape[1]
    shapes = [
        ((rows, features + 2 * HEAD_SIZE), BF16),
        ((features, whole), BF16),
    ]
    operands = [upstream, wo, raw, low, lse, gains, cosine, sine, x, *weights, beside]
    return pl.pallas_call(
        functools.partial(attention_back_kernel, key_heads),
        in_specs=in_smem() + in_vmem(len(operands)),
        out_specs=in_vmem(2),
        out_shape=[jax.ShapeDtypeStruct(*v) for v in shapes],
        scratch_shapes=[pltpu.VMEM((rows, query_width), BF16), pltpu.VMEM((rows, width), BF16)],
        compiler_params=pltpu.CompilerParams(vmem_limit_bytes=40 * 1024 * 1024),
        cost_estimate=SMALL,
    )(jnp.stack(where).astype(jnp.int32), *in_hbm(*operands))


def chunk_places():
    return jnp.stack(
        [lax.axis_index("tp") ^ m for m in range(lax.axis_size("tp"))]
    ).astype(jnp.int32)


def rows_at(index, size):
    return pl.ds(pl.multiple_of(index * size, size), size)


def resid_kernel(place_ref, *refs):
    *pieces, hidden_ref, gain_ref, resid_ref, routed_ref = refs
    rows = pieces[0].shape[0]
    for m, piece in enumerate(pieces):
        at = rows_at(place_ref[m], rows)
        resid = hidden_ref[at, :].astype(F32) + piece[...].astype(F32)
        resid_ref[at, :] = resid
        routed_ref[at, :] = (resid * inverse_rms(resid) * gain_ref[...]).astype(BF16)


def resid_and_routed(pieces, hidden, gain):
    return pl.pallas_call(
        resid_kernel,
        in_specs=in_smem() + in_vmem(len(pieces) + 2),
        out_specs=in_vmem(2),
        out_shape=[
            pltpu.HBM(hidden.shape, F32),
            jax.ShapeDtypeStruct(hidden.shape, BF16),
        ],
        compiler_params=pltpu.CompilerParams(vmem_limit_bytes=6 * 1024 * 1024),
        cost_estimate=SMALL,
    )(chunk_places(), *pieces, hidden, gain)


def resid_back_kernel(parts, place_ref, column_ref, *refs):
    pieces = refs[: 2 * parts]
    (
        resid_a_ref,
        resid_b_ref,
        routed_a_ref,
        routed_b_ref,
        ids_ref,
        router_ref,
        gain_ref,
        upstream_ref,
        mixed_ref,
        grad_ref,
        low_ref,
        beside_ref,
        keep_ref,
        send_ref,
        returned_ref,
        wide_ref,
    ) = refs[2 * parts :]
    rows, features = upstream_ref.shape
    expert_count = router_ref.shape[1]
    chunk = pieces[0].shape[0]
    for h in range(2):
        for m in range(parts):
            returned_ref[rows_at(place_ref[m] + h * parts, chunk), :] = pieces[h * parts + m][...]
    routed = jnp.concatenate([routed_a_ref[...], routed_b_ref[...]], axis=0)
    resid = jnp.concatenate([resid_a_ref[...], resid_b_ref[...]], axis=0)
    logits = jnp.dot(routed, router_ref[...], preferred_element_type=F32)
    lane = lax.broadcasted_iota(jnp.int32, (rows, expert_count), 1)
    named = ids_ref[:, 0:1] == lane
    for k in range(1, TOP):
        named = named | (ids_ref[:, k : k + 1] == lane)
    exponent = jnp.exp(logits - jnp.max(logits, axis=1, keepdims=True))
    router = exponent / jnp.sum(exponent, axis=1, keepdims=True)
    chosen = jnp.where(named, router, 0.0)
    total = jnp.sum(chosen, axis=1, keepdims=True)
    gates = chosen / total
    tail = returned_ref[:, features:].astype(F32)
    tail = tail + pltpu.roll(tail, tail.shape[1] - expert_count, 1)
    grad_gates = jnp.where(named, tail[:, :expert_count], 0.0)
    inner = jnp.sum(grad_gates * gates, axis=1, keepdims=True)
    grad_router = jnp.where(named, (grad_gates - inner) / total, 0.0)
    inner = jnp.sum(router * grad_router, axis=1, keepdims=True)
    grad_logits = (router * (grad_router - inner)).astype(BF16)
    grad_routed = returned_ref[:, :features].astype(F32) + against(grad_logits, router_ref[...])
    scale = inverse_rms(resid)
    normal = resid * scale
    weighted = grad_routed * gain_ref[...]
    inner = jnp.mean(weighted * normal, axis=1, keepdims=True)
    grad = upstream_ref[...].astype(F32) + scale * (weighted - normal * inner)
    grad_ref[...] = grad
    low_ref[...] = grad.astype(BF16)
    half = column_ref.shape[0] // 2
    for j in range(half):
        for k, out_ref in ((j, keep_ref), (half + j, send_ref)):
            columns = pl.ds(pl.multiple_of(column_ref[k] * LANES, LANES), LANES)
            out_ref[j * LANES : (j + 1) * LANES, :] = over_rows(
                mixed_ref[:, columns], low_ref[...]
            ).astype(BF16)
    wide_ref[...] = jnp.zeros(wide_ref.shape, BF16)
    wide_ref[:, :expert_count] = grad_logits
    one = lax.broadcasted_iota(jnp.int32, wide_ref.shape, 1) == expert_count
    beside_ref[...] = (
        over_rows(routed, wide_ref[...])
        + over_rows((grad_routed * normal).astype(BF16), one.astype(F32).astype(BF16))
    ).astype(BF16)


def resid_back(pieces, resid, routed, ids, router, gain, upstream, mixed, columns):
    parts = len(pieces) // 2
    rows, features = upstream.shape
    expert_count = router.shape[1]
    wide = -(-(expert_count + 1) // LANES) * LANES
    half = mixed.shape[1] // 2
    shapes = [
        ((rows, features), F32),
        ((rows, features), BF16),
        ((features, wide), BF16),
        ((half, features), BF16),
        ((half, features), BF16),
    ]
    operands = [*pieces, *in_hbm(*resid, *routed, ids, router, gain, upstream, mixed)]
    return pl.pallas_call(
        functools.partial(resid_back_kernel, parts),
        in_specs=in_smem() * 2 + in_vmem(len(operands)),
        out_specs=in_vmem(len(shapes)),
        out_shape=[jax.ShapeDtypeStruct(*v) for v in shapes],
        scratch_shapes=[
            pltpu.VMEM((rows, pieces[0].shape[1]), BF16),
            pltpu.VMEM((rows, wide), BF16),
        ],
        compiler_params=pltpu.CompilerParams(vmem_limit_bytes=40 * 1024 * 1024),
        cost_estimate=SMALL,
    )(chunk_places(), jnp.stack(columns).astype(jnp.int32), *operands)


def input_kernel(ordered, place_ref, block_ref, *refs):
    *pieces, hidden_ref, resid_grad_ref, gain_ref, result_ref, late_ref, total_ref = refs
    features = hidden_ref.shape[1]
    rows = pieces[0].shape[0]
    count = block_ref.shape[0]
    block = features // count
    for m, piece in enumerate(pieces):
        total_ref[rows_at(place_ref[m], rows), :] = piece[...]
    hidden = hidden_ref[...].astype(F32)
    scale = inverse_rms(hidden)
    columns = [
        slice(j * block, (j + 1) * block)
        if ordered
        else pl.ds(pl.multiple_of(block_ref[j] * block, block), block)
        for j in range(count)
    ]
    inner = jnp.zeros((hidden.shape[0], 1), F32)
    for j in range(count):
        normal = hidden_ref[:, columns[j]].astype(F32) * scale
        grad = total_ref[:, j * block : (j + 1) * block].astype(F32)
        terms = grad * normal
        inner += jnp.sum(terms * gain_ref[:, columns[j]], axis=1, keepdims=True)
        late_ref[j : j + 1, :block] = jnp.sum(terms, axis=0, keepdims=True)
    inner = inner * (1.0 / features)
    for j in range(count):
        normal = hidden_ref[:, columns[j]].astype(F32) * scale
        weighted = total_ref[:, j * block : (j + 1) * block].astype(F32) * gain_ref[:, columns[j]]
        result_ref[:, columns[j]] = resid_grad_ref[:, columns[j]] + scale * (
            weighted - normal * inner
        )
    heads = jnp.sum(total_ref[:, features:].astype(F32), axis=0, keepdims=True)
    late_ref[:, block:] = jnp.broadcast_to(heads, (count, heads.shape[1]))


def input_gradient(pieces, hidden, resid_grad, gain, where):
    rows, features = hidden.shape
    count = len(where)
    extra = pieces[0].shape[1] - features
    return pl.pallas_call(
        functools.partial(input_kernel, absolute()),
        in_specs=in_smem() * 2 + in_vmem(len(pieces) + 3),
        out_specs=in_vmem(2),
        out_shape=[
            jax.ShapeDtypeStruct((rows, features), F32),
            jax.ShapeDtypeStruct((count, features // count + extra), F32),
        ],
        scratch_shapes=[pltpu.VMEM((rows, pieces[0].shape[1]), BF16)],
        compiler_params=pltpu.CompilerParams(vmem_limit_bytes=24 * 1024 * 1024),
        cost_estimate=SMALL,
    )(chunk_places(), jnp.stack(where).astype(jnp.int32), *pieces, *in_hbm(hidden, resid_grad, gain))


def widen_kernel(place_ref, near_ref, core_ref, result_ref):
    early = pl.program_id(0) < pl.num_programs(0) // 2
    result_ref[...] = jnp.where(early, near_ref[...], core_ref[...]).astype(F32)


def widen_blocks(near, core, where):
    count = len(where)
    features = near.shape[1]
    block = 2 * near.shape[0] // count
    half = count // 2
    first = pl.BlockSpec((block, features), lambda i, s: (jnp.minimum(i, half - 1), 0))
    second = pl.BlockSpec((block, features), lambda i, s: (jnp.maximum(i - half, 0), 0))
    return pl.pallas_call(
        widen_kernel,
        grid_spec=pltpu.PrefetchScalarGridSpec(
            num_scalar_prefetch=1,
            grid=(count,),
            in_specs=[first, second],
            out_specs=pl.BlockSpec((block, features), lambda i, s: (s[i], 0)),
        ),
        out_shape=jax.ShapeDtypeStruct((block * count, features), F32),
        compiler_params=pltpu.CompilerParams(vmem_limit_bytes=24 * 1024 * 1024),
        cost_estimate=SMALL,
    )(jnp.stack(where).astype(jnp.int32), near, core)


def shards(
    hidden_in,
    expert_ids,
    attention_gain,
    query_gain,
    key_gain,
    query_weight,
    key_matrix,
    value_matrix,
    output_weight,
    expert_gain,
    router_weight,
    gate_up_weight,
    down_weight,
    output_grad,
):
    tokens, features = hidden_in.shape
    owners = lax.axis_size("ep")
    local_experts = gate_up_weight.shape[0]
    expert_count = local_experts * owners
    rows_a = tokens // 2

    head_share = query_gain.shape[0]
    share = router_weight.shape[0]
    small_rows = max(tokens, share)
    padded = lambda v: jnp.pad(v.astype(BF16), ((0, small_rows - v.shape[0]), (0, 0)))
    small = jnp.concatenate(
        [
            padded(router_weight),
            padded(jnp.stack([attention_gain, expert_gain], axis=1)),
            padded(jnp.stack([query_gain, key_gain], axis=1)),
            padded(expert_ids),
        ],
        axis=1,
    )
    small_width = small.shape[1]
    small = jnp.pad(small, ((0, 0), (0, -small_width % LANES)))
    packed = jnp.concatenate([key_matrix, value_matrix], axis=1)
    packed_width = packed.shape[1]
    together = small_rows == share
    if together:
        packed = jnp.concatenate([packed, small], axis=1)
    packed_hops = gather_hops(packed)
    hops = gather_hops(query_weight)
    packed_near = gather_near(packed, packed_hops)
    packed_core = gather_core(packed_near, packed_hops)
    if together:
        small = jnp.concatenate(
            [packed_near[:, packed_width:], packed_core[:, packed_width:]], axis=0
        )
    else:
        small = lax.all_gather(small, "ep", axis=0, tiled=True)
    small = put_blocks(small, 0).reshape(owners, small_rows, -1)
    by_feature = small[:, :share, : expert_count + 2].reshape(features, -1)
    router_full = by_feature[:, :expert_count]
    attn_gain_full = by_feature[:, expert_count].astype(F32)[None, :]
    mlp_gain_full = by_feature[:, expert_count + 1].astype(F32)[None, :]
    gains = (
        small[:, :head_share, expert_count + 2 : expert_count + 4]
        .reshape(HEAD_SIZE, 2)
        .astype(F32)
        .T
    )
    ids_all = small[:, :tokens, expert_count + 4 : small_width].reshape(-1, TOP).astype(jnp.int32)
    wd = down_weight.reshape(-1, features)
    normed_low = norm_rows(hidden_in.astype(F32), attn_gain_full).astype(BF16)
    normed_rel = pick_blocks(normed_low, 1)
    positions = jnp.arange(tokens, dtype=jnp.int32)
    cosine, sine_table = rope_tables(positions, HEAD_SIZE)
    (
        hops,
        packed_core,
        normed_rel,
        cosine,
        sine_table,
        gains,
        router_full,
        attn_gain_full,
        mlp_gain_full,
        ids_all,
        output_all,
        gate_up_low,
    ) = join(
        hops,
        packed_core,
        normed_rel,
        cosine,
        sine_table,
        gains,
        router_full,
        attn_gain_full,
        mlp_gain_full,
        ids_all,
        output_grad,
        gate_up_weight,
    )

    near = gather_near(query_weight, hops)
    weights_rel = [near, gather_core(near, hops), packed_near, packed_core]
    output_all = lax.all_gather(output_all, "ep", axis=0, tiled=True)
    query_width = query_weight.shape[1]
    key_width = key_matrix.shape[1]
    key_heads = key_width // HEAD_SIZE
    raw, low, attention_output, lse, *head_parts = attention(
        normed_rel, *weights_rel, gains, cosine, sine_table, output_weight, key_heads
    )
    (head_parts,) = join(head_parts)

    hops = reduce_hops(head_parts[0])
    wgu = gate_up_low.transpose(1, 0, 2).reshape(features, -1)
    hops, wgu = join(hops, wgu)

    chunk = reduce_total(head_parts[0], hops)
    hops, hops_b = join(spread_hops(chunk), reduce_hops(head_parts[1]))

    resid_a, routed_a = resid_and_routed([chunk] + hops, hidden_in[:rows_a], mlp_gain_full)
    chunk = reduce_total(head_parts[1], hops_b)
    hops_a, hops = join(gather_hops(routed_a), spread_hops(chunk))

    resid_b, routed_b = resid_and_routed([chunk] + hops, hidden_in[rows_a:], mlp_gain_full)
    near_a = gather_near(routed_a, hops_a)
    core_a = gather_core(near_a, hops_a)
    hops_b = gather_hops(routed_b)
    lined = places()
    where = [2 * b + h for h in range(2) for b in lined]

    def experts(piece, x):
        rows = slice(piece * owners // 2, (piece + 1) * owners // 2)
        return run_experts(
            x, output_all, ids_all, where[rows], router_full, wgu, wd, local_experts
        )

    keep_a, joined_0, hidden_0 = experts(0, near_a)
    send_a, joined_1, hidden_1 = experts(1, core_a)
    hops_b, send_a, keep_a = join(hops_b, send_a, keep_a)

    near_b = gather_near(routed_b, hops_b)
    core_b = gather_core(near_b, hops_b)
    come = scatter_swap(send_a)
    keep_b, joined_2, hidden_2 = experts(2, near_b)
    come, core_b, keep_b = join(come, core_b, keep_b)

    sums_a = scatter_sums(keep_a, come)
    hops_a = scatter_hops(sums_a)
    send_b, joined_3, hidden_3 = experts(3, core_b)
    hops_a, send_b = join(hops_a, send_b)
    joined = [joined_0, joined_1, joined_2, joined_3]
    hidden = [hidden_0, hidden_1, hidden_2, hidden_3]
    routed_pieces = [near_a, core_a, near_b, core_b]

    come = scatter_swap(send_b)
    total_a = scatter_total(sums_a, hops_a)
    hops = reduce_hops(total_a)
    come, hidden = join(come, hidden)

    sums_b = scatter_sums(keep_b, come)
    hops_b = scatter_hops(sums_b)
    mixture_parts = mixture_product(hidden, wd, lined)
    chunk_a = reduce_total(total_a, hops)
    spread_a, hops_b, mixture_parts, joined = join(
        spread_hops(chunk_a), hops_b, mixture_parts, joined
    )

    mixture = lax.psum_scatter(mixture_parts, "ep", scatter_dimension=0, tiled=True)
    total_b = scatter_total(sums_b, hops_b)
    (hops,) = join(reduce_hops(total_b))
    chunk_b = reduce_total(total_b, hops)
    (spread_b,) = join(spread_hops(chunk_b))

    columns = (
        [jnp.int32(b) for b in range(attention_output.shape[1] // LANES)] if absolute() else lined
    )
    grad_resid, grad_attended, by_feature, output_keep, output_send = resid_back(
        [chunk_a, *spread_a, chunk_b, *spread_b],
        [resid_a, resid_b],
        [routed_a, routed_b],
        expert_ids,
        router_full,
        mlp_gain_full,
        output_grad,
        attention_output,
        columns,
    )

    feature_part, weights_grad = attention_back(
        lined,
        grad_attended,
        output_weight,
        raw,
        low,
        lse,
        gains,
        cosine,
        sine_table,
        normed_rel,
        weights_rel,
        by_feature,
        key_heads,
    )
    come, feature_part, weights_grad = join(
        scatter_swap(output_send), feature_part, weights_grad
    )

    weights_rows = lax.psum_scatter(weights_grad, "ep", scatter_dimension=0, tiled=True)
    hops = reduce_hops(feature_part)
    output_sums = scatter_sums(output_keep, come)
    output_hops = scatter_hops(output_sums)
    down_grad = down_product(hidden, output_all, where).reshape(down_weight.shape)
    hops, output_hops, down_grad, mixture, joined = join(
        hops, output_hops, down_grad, mixture, joined
    )

    chunk = reduce_total(feature_part, hops)
    hops = spread_hops(chunk)
    mixture_hops = reduce_hops(mixture)
    output_share = scatter_total(output_sums, output_hops)
    gate_up_grad = gate_up_product(routed_pieces, joined, gate_up_weight.shape)
    hops, gate_up_grad, output_share = join(hops, gate_up_grad, output_share)

    output_hops = gather_hops(output_share)
    input_grad, late = input_gradient(
        [chunk, *hops], hidden_in, grad_resid, attn_gain_full, lined
    )
    late_come = scatter_swap(late[owners // 2 :])
    late_come, output_hops, mixture_hops = join(late_come, output_hops, mixture_hops)

    mixture_chunk = reduce_total(mixture, mixture_hops)
    mixture_hops = spread_hops(mixture_chunk)
    near = gather_near(output_share, output_hops)
    output_core = gather_core(near, output_hops)
    late_sums = scatter_sums(late[: owners // 2], late_come)
    late_hops = scatter_hops(late_sums)
    output_weight_grad = widen_blocks(near, output_core, lined)
    late_hops, output_weight_grad, weights_rows, mixture_hops = join(
        late_hops, output_weight_grad, weights_rows, mixture_hops
    )
    weights_rows = weights_rows.astype(F32)
    late = scatter_total(late_sums, late_hops)[0]
    head_grads = lax.dynamic_slice_in_dim(
        late[share:].reshape(2, HEAD_SIZE), lax.axis_index("ep") * head_share, head_share, 1
    )
    early = weights_rows[:, query_width + 2 * key_width :]
    mixture = spread_total(mixture_chunk, mixture_hops)
    block_out = (jnp.concatenate([resid_a, resid_b], axis=0) + mixture.astype(F32)).astype(BF16)
    return (
        block_out,
        input_grad,
        late[:share],
        head_grads[0],
        head_grads[1],
        weights_rows[:, :query_width],
        weights_rows[:, query_width : query_width + key_width],
        weights_rows[:, query_width + key_width : query_width + 2 * key_width],
        output_weight_grad,
        early[:, expert_count],
        early[:, :expert_count],
        gate_up_grad,
        down_grad,
    )


def solution(mesh):
    in_specs = (
        P("ep", None),
        P("ep", None),
        P("ep"),
        P("ep"),
        P("ep"),
        P("ep", "tp"),
        P("ep", "tp"),
        P("ep", "tp"),
        P("tp", None),
        P("ep"),
        P("ep", None),
        P("ep", None, "tp"),
        P("ep", "tp", None),
        P("ep", None),
    )
    out_specs = (
        P("ep", None),
        P("ep", None),
        P("ep"),
        P("ep"),
        P("ep"),
        P("ep", "tp"),
        P("ep", "tp"),
        P("ep", "tp"),
        P("tp", None),
        P("ep"),
        P("ep", None),
        P("ep", None, "tp"),
        P("ep", "tp", None),
    )
    return jax.shard_map(shards, mesh=mesh, in_specs=in_specs, out_specs=out_specs, check_vma=False)
```

```python
import functools
import math

import jax
import jax.numpy as jnp
from jax import lax
from jax.experimental import pallas as pl
from jax.experimental.pallas import tpu as pltpu
from jax.sharding import PartitionSpec as P

HEAD_SIZE = 128
TOP = 8
PAIR = 64
LANES = 128

EPSILON = 1e-06
THETA = 1000000.0
F32 = jnp.float32
BF16 = jnp.bfloat16
SMALL = pl.CostEstimate(flops=0, bytes_accessed=1024, transcendentals=0)


def norm_rows(value_rows, norm_gain):
    return (
        value_rows
        * lax.rsqrt(jnp.mean(value_rows * value_rows, axis=-1, keepdims=True) + EPSILON)
        * norm_gain
    )


def rope_tables(positions, head_size):
    halfway = head_size // 2
    inverse = THETA ** (-(jnp.arange(halfway, dtype=jnp.float32) * 2.0) / head_size)
    angles = positions.astype(jnp.float32)[:, None] * inverse[None, :]
    cosine, sine = jnp.cos(angles), jnp.sin(angles)
    return (
        jnp.concatenate([cosine, cosine], axis=1),
        jnp.concatenate([-sine, sine], axis=1),
    )


SWAPPED = 8


def swap(value, axis, mask):
    count = lax.axis_size(axis)
    return lax.ppermute(value, axis, [(i, i ^ mask) for i in range(count)])


def join(*values):
    return lax.optimization_barrier(values)


ORDER = (0, 2, 4, 6, 1, 3, 5, 7)


def plus(*values):
    total = values[0].astype(F32)
    for v in values[1:]:
        total = total + v.astype(F32)
    return total.astype(values[0].dtype)


def absolute():
    return lax.axis_size("ep") > SWAPPED


def in_hbm(*values):
    return [pltpu.with_memory_space_constraint(v, pltpu.HBM) for v in values]


def stack_kernel(*refs):
    *pieces, result_ref = refs
    rows = pieces[0].shape[0]
    for i, piece in enumerate(pieces):
        result_ref[i * rows : (i + 1) * rows, :] = piece[...]


def stack_rows(pieces):
    rows = pieces[0].shape[0]
    return pl.pallas_call(
        stack_kernel,
        out_shape=jax.ShapeDtypeStruct(
            (len(pieces) * rows,) + pieces[0].shape[1:], pieces[0].dtype
        ),
        compiler_params=pltpu.CompilerParams(vmem_limit_bytes=8 * 1024 * 1024),
        cost_estimate=SMALL,
    )(*pieces)


def gather_hops(value):
    if absolute():
        return [lax.all_gather(value, "ep", axis=0, tiled=True)]
    return [swap(value, "ep", m) for m in ORDER[1:4]]


def gather_near(value, hops):
    if absolute():
        return hops[0][: hops[0].shape[0] // 2]
    return stack_rows([value] + hops)


def gather_core(near, hops):
    if absolute():
        return hops[0][hops[0].shape[0] // 2 :]
    return swap(near, "ep", 1)


def scatter_swap(send):
    return send if absolute() else swap(send, "ep", 1)


def scatter_sums(keep, come):
    if absolute():
        return [jnp.concatenate([keep, come], axis=0)]
    rows = keep.shape[0] // 4
    return [
        plus(keep[i * rows : (i + 1) * rows], come[i * rows : (i + 1) * rows]) for i in range(4)
    ]


def scatter_hops(sums):
    if absolute():
        return [lax.psum_scatter(sums[0], "ep", scatter_dimension=0, tiled=True)]
    return [swap(v, "ep", m) for v, m in zip(sums[1:], ORDER[1:4])]


def scatter_total(sums, hops):
    return hops[0] if absolute() else plus(sums[0], *hops)


def chunk_of(value, index):
    rows = value.shape[0] // lax.axis_size("tp")
    return lax.dynamic_slice_in_dim(value, index * rows, rows, 0)


def reduce_hops(value):
    mine = lax.axis_index("tp")
    return [swap(chunk_of(value, mine ^ m), "tp", m) for m in range(1, lax.axis_size("tp"))]


def reduce_total(value, hops):
    return plus(chunk_of(value, lax.axis_index("tp")), *hops)


def spread_hops(chunk):
    return [swap(chunk, "tp", m) for m in range(1, lax.axis_size("tp"))]


def spread_total(chunk, hops):
    mine = lax.axis_index("tp")
    rows = chunk.shape[0]
    result = jnp.zeros(((len(hops) + 1) * rows,) + chunk.shape[1:], chunk.dtype)
    for m, piece in enumerate([chunk] + hops):
        result = lax.dynamic_update_slice_in_dim(result, piece, (mine ^ m) * rows, 0)
    return result


def places():
    if absolute():
        return [jnp.int32(b) for b in range(lax.axis_size("ep"))]
    return [lax.axis_index("ep") ^ m for m in ORDER]


def pick_blocks(value, axis):
    count = lax.axis_size("ep")
    if count > SWAPPED:
        return value
    mine = lax.axis_index("ep")
    size = value.shape[axis] // count
    return jnp.concatenate(
        [lax.dynamic_slice_in_dim(value, (mine ^ m) * size, size, axis) for m in ORDER],
        axis=axis,
    )


def put_blocks(value, axis):
    count = lax.axis_size("ep")
    if count > SWAPPED:
        return value
    mine = lax.axis_index("ep")
    size = value.shape[axis] // count
    place = lambda m: (m // 2 + (m % 2) * (count // 2)) * size
    return jnp.concatenate(
        [lax.dynamic_slice_in_dim(value, place(mine ^ b), size, axis) for b in range(count)],
        axis=axis,
    )


def expert_kernel(
    local,
    place_ref,
    x_ref,
    g0_ref,
    g1_ref,
    ids0_ref,
    ids1_ref,
    router_ref,
    wgu_in_ref,
    wd_in_ref,
    dx_ref,
    joined_ref,
    hidden_ref,
    wgu_ref,
    wd_ref,
    arrived,
):
    rows = x_ref.shape[0]
    features = x_ref.shape[1]
    expert_count = router_ref.shape[1]
    hidden_count = wd_ref.shape[0]
    group = 3
    count = hidden_count // LANES // group
    copies = [
        pltpu.make_async_copy(wgu_in_ref, wgu_ref, arrived.at[0]),
        pltpu.make_async_copy(wd_in_ref, wd_ref, arrived.at[1]),
    ]

    @pl.when(pl.program_id(0) == 0)
    def _():
        for copy in copies:
            copy.start()

    extra = dx_ref.shape[1] - features
    base = place_ref[0]
    x = x_ref[...]
    upstream = jnp.concatenate([g0_ref[...], g1_ref[...]], axis=0)
    ids = jnp.concatenate([ids0_ref[...], ids1_ref[...]], axis=0)
    logits = jnp.dot(x, router_ref[...], preferred_element_type=F32)
    lane = lax.broadcasted_iota(jnp.int32, (rows, expert_count), 1)
    named = ids[:, 0:1] == lane
    for k in range(1, TOP):
        named = named | (ids[:, k : k + 1] == lane)
    exponent = jnp.exp(logits - jnp.max(logits, axis=1, keepdims=True))
    router = exponent / jnp.sum(exponent, axis=1, keepdims=True)
    chosen = jnp.where(named, router, 0.0)
    gates = chosen / jnp.sum(chosen, axis=1, keepdims=True)
    gate = [
        jnp.sum(jnp.where(lane == base + j, gates, 0.0), axis=1, keepdims=True)
        for j in range(local)
    ]
    left = lax.broadcasted_iota(jnp.int32, (rows, LANES), 1) < PAIR
    per_expert = hidden_count // local // PAIR
    gate_sum = [jnp.zeros((rows, LANES), F32) for _ in range(local)]

    @pl.when(pl.program_id(0) == 0)
    def _():
        for copy in copies:
            copy.wait()

    def products(q):
        wide = group * LANES
        act = jnp.dot(
            x, wgu_ref[:, 2 * q * wide : 2 * (q + 1) * wide], preferred_element_type=F32
        )
        back = lax.dot_general(
            upstream,
            wd_ref[q * wide : (q + 1) * wide, :],
            (((1,), (1,)), ((), ())),
            preferred_element_type=F32,
        )
        return act, back

    def elementwise(q, act, back):
        for i in range(group):
            p = q * group + i
            one, two = 2 * p // per_expert, (2 * p + 1) // per_expert
            first = act[:, 2 * i * LANES : (2 * i + 1) * LANES]
            second = act[:, (2 * i + 1) * LANES : (2 * i + 2) * LANES]
            g = jnp.where(left, first, pltpu.roll(second, PAIR, 1))
            u = jnp.where(left, pltpu.roll(first, PAIR, 1), second)
            gh = back[:, i * LANES : (i + 1) * LANES]
            if one == two:
                scale = jnp.broadcast_to(gate[one], (rows, LANES))
            else:
                scale = jnp.where(left, gate[one], gate[two])
            sig = lax.logistic(g)
            silu = g * sig
            hid = silu * u
            product = hid * gh
            if one == two:
                gate_sum[one] += product
            else:
                gate_sum[one] += jnp.where(left, product, 0.0)
                gate_sum[two] += jnp.where(left, 0.0, product)
            hidden_ref[:, p * LANES : (p + 1) * LANES] = (hid * scale).astype(BF16)
            gs = gh * scale
            dg = gs * u * sig * (1.0 + g * (1.0 - sig))
            du = gs * silu
            joined_ref[:, 2 * p * LANES : (2 * p + 1) * LANES] = jnp.where(
                left, dg, pltpu.roll(du, PAIR, 1)
            ).astype(BF16)
            joined_ref[:, (2 * p + 1) * LANES : (2 * p + 2) * LANES] = jnp.where(
                left, pltpu.roll(dg, PAIR, 1), du
            ).astype(BF16)

    waiting = []
    for q in range(count):
        waiting.append((q, *products(q)))
        if q:
            elementwise(*waiting.pop(0))
    elementwise(*waiting.pop(0))
    dx = lax.dot_general(
        joined_ref[...], wgu_ref[...], (((1,), (1,)), ((), ())), preferred_element_type=F32
    )
    dx_ref[:, :features] = dx.astype(BF16)
    wide = lax.broadcasted_iota(jnp.int32, (rows, extra), 1)
    tail = jnp.zeros((rows, extra), F32)
    for j in range(local):
        total = jnp.sum(gate_sum[j], axis=1, keepdims=True)
        high = total.astype(BF16).astype(F32)
        tail = jnp.where(wide == base + j, high, tail)
        tail = jnp.where(wide == expert_count + base + j, total - high, tail)
    dx_ref[:, features:] = tail.astype(BF16)


def run_experts(x, g, ids, where, router, wgu, wd, local):
    tokens, features = x.shape
    tile = 256
    block = tokens // len(where)
    steps = tokens // tile
    expert_count = router.shape[1]
    extra = -(-2 * expert_count // LANES) * LANES
    place = jnp.stack([lax.axis_index("ep") * local] + list(where)).astype(jnp.int32)
    found = lambda width, j: pl.BlockSpec((block, width), lambda i, s: (s[1 + 2 * i + j], 0))
    whole = pl.BlockSpec(router.shape, lambda i, s: (0, 0), pipeline_mode=pl.Buffered(1))
    anywhere = pl.BlockSpec(memory_space=pl.ANY)
    by_rows = lambda width: pl.BlockSpec((tile, width), lambda i, s: (i, 0))
    in_specs = [
        by_rows(features),
        found(features, 0),
        found(features, 1),
        found(TOP, 0),
        found(TOP, 1),
        whole,
        anywhere,
        anywhere,
    ]
    g, wgu, wd = in_hbm(g, wgu, wd)
    operands = [place, x, g, g, ids, ids, router, wgu, wd]
    return pl.pallas_call(
        functools.partial(expert_kernel, local),
        grid_spec=pltpu.PrefetchScalarGridSpec(
            num_scalar_prefetch=1,
            grid=(steps,),
            in_specs=in_specs,
            out_specs=[
                by_rows(features + extra),
                by_rows(wgu.shape[1]),
                by_rows(wd.shape[0]),
            ],
            scratch_shapes=[
                pltpu.VMEM(wgu.shape, BF16),
                pltpu.VMEM(wd.shape, BF16),
                pltpu.SemaphoreType.DMA((2,)),
            ],
        ),
        out_shape=[
            pltpu.HBM((tokens, features + extra), BF16),
            pltpu.HBM((tokens, wgu.shape[1]), BF16),
            pltpu.HBM((tokens, wd.shape[0]), BF16),
        ],
        compiler_params=pltpu.CompilerParams(vmem_limit_bytes=32 * 1024 * 1024),
        cost_estimate=SMALL,
    )(*operands)


def gate_up_kernel(*refs):
    *operands, result_ref = refs
    count = len(operands) // 2
    total = None
    for x_ref, joined_ref in zip(operands[:count], operands[count:]):
        part = lax.dot_general(
            x_ref[...], joined_ref[...], (((0,), (0,)), ((), ())), preferred_element_type=F32
        )
        total = part if total is None else total + part
    width = result_ref.shape[2]
    for e in range(result_ref.shape[0]):
        result_ref[e] = total[:, e * width : (e + 1) * width]


def gate_up_product(pieces, joined, shape):
    rows, features = pieces[0].shape
    width = joined[0].shape[1]
    tile = 256
    whole = pl.BlockSpec((rows, width), lambda i: (0, 0), pipeline_mode=pl.Buffered(1))
    return pl.pallas_call(
        gate_up_kernel,
        grid=(features // tile,),
        in_specs=[pl.BlockSpec((rows, tile), lambda i: (0, i)) for _ in pieces]
        + [whole for _ in joined],
        out_specs=pl.BlockSpec((shape[0], tile, shape[2]), lambda i: (0, i, 0)),
        out_shape=jax.ShapeDtypeStruct(shape, F32),
        compiler_params=pltpu.CompilerParams(vmem_limit_bytes=56 * 1024 * 1024),
        cost_estimate=SMALL,
    )(*in_hbm(*pieces, *joined))


def down_kernel(place_ref, *refs):
    *pieces, g_ref, result_ref, sorted_ref = refs
    blocks = place_ref.shape[0] // len(pieces)
    block = pieces[0].shape[0] // blocks
    for i, hidden_ref in enumerate(pieces):
        for k in range(blocks):
            start = pl.multiple_of(place_ref[i * blocks + k] * block, block)
            sorted_ref[pl.ds(start, block), :] = hidden_ref[k * block : (k + 1) * block, :]
    result_ref[...] = lax.dot_general(
        sorted_ref[...], g_ref[...], (((0,), (0,)), ((), ())), preferred_element_type=F32
    )


def down_product(hidden, g, where):
    rows, features = g.shape
    width = hidden[0].shape[1]
    tile = 256
    return pl.pallas_call(
        down_kernel,
        grid_spec=pltpu.PrefetchScalarGridSpec(
            num_scalar_prefetch=1,
            grid=(width // tile,),
            in_specs=[pl.BlockSpec((v.shape[0], tile), lambda i, s: (0, i)) for v in hidden]
            + [pl.BlockSpec((rows, features), lambda i, s: (0, 0), pipeline_mode=pl.Buffered(1))],
            out_specs=pl.BlockSpec((tile, features), lambda i, s: (i, 0)),
            scratch_shapes=[pltpu.VMEM((rows, tile), BF16)],
        ),
        out_shape=jax.ShapeDtypeStruct((width, features), F32),
        compiler_params=pltpu.CompilerParams(vmem_limit_bytes=57 * 1024 * 1024),
        cost_estimate=SMALL,
    )(jnp.stack(where).astype(jnp.int32), *in_hbm(*hidden, g))


def mixture_kernel(
    place_ref, upper0_ref, upper1_ref, lower0_ref, lower1_ref, wd_ref, result_ref
):
    early = pl.program_id(0) < pl.num_programs(0) // 2
    rows = jnp.concatenate(
        [
            jnp.where(early, upper0_ref[...], upper1_ref[...]),
            jnp.where(early, lower0_ref[...], lower1_ref[...]),
        ],
        axis=0,
    )
    result_ref[...] = jnp.dot(rows, wd_ref[...], preferred_element_type=F32).astype(BF16)


def mixture_product(hidden, wd, where):
    count = len(where)
    block = 2 * hidden[0].shape[0] // count
    width, features = wd.shape
    first = pl.BlockSpec((block, width), lambda i, s: (jnp.minimum(i, count // 2 - 1), 0))
    second = pl.BlockSpec((block, width), lambda i, s: (jnp.maximum(i - count // 2, 0), 0))
    return pl.pallas_call(
        mixture_kernel,
        grid_spec=pltpu.PrefetchScalarGridSpec(
            num_scalar_prefetch=1,
            grid=(count,),
            in_specs=[first, second, first, second]
            + [pl.BlockSpec((width, features), lambda i, s: (0, 0))],
            out_specs=pl.BlockSpec((2 * block, features), lambda i, s: (s[i], 0)),
        ),
        out_shape=pltpu.HBM((2 * block * count, features), BF16),
        compiler_params=pltpu.CompilerParams(vmem_limit_bytes=24 * 1024 * 1024),
        cost_estimate=SMALL,
    )(jnp.stack(where).astype(jnp.int32), *in_hbm(*hidden, wd))


def rotated(value, cosine, sine):
    return value * cosine + pltpu.roll(value, HEAD_SIZE // 2, 1) * sine


def inverse_rms(value):
    return lax.rsqrt(jnp.mean(value * value, axis=1, keepdims=True) + EPSILON)


def head_columns(h):
    return slice(h * HEAD_SIZE, (h + 1) * HEAD_SIZE)


def against(left, right):
    return lax.dot_general(left, right, (((1,), (1,)), ((), ())), preferred_element_type=F32)


def over_rows(left, right):
    return lax.dot_general(left, right, (((0,), (0,)), ((), ())), preferred_element_type=F32)


def causal(rows):
    return lax.broadcasted_iota(jnp.int32, (rows, rows), 1) <= lax.broadcasted_iota(
        jnp.int32, (rows, rows), 0
    )


def attention_kernel(
    key_heads,
    x_ref,
    near_ref,
    core_ref,
    near_kv_ref,
    core_kv_ref,
    gains_ref,
    cosine_ref,
    sine_ref,
    wo_ref,
    raw_ref,
    low_ref,
    mixed_ref,
    lse_ref,
    upper_ref,
    lower_ref,
):
    rows = x_ref.shape[0]
    split = near_ref.shape[0]
    query_heads = mixed_ref.shape[1] // HEAD_SIZE
    heads = query_heads + key_heads
    queries = query_heads * HEAD_SIZE
    raw_ref[:, :queries] = jnp.dot(
        x_ref[:, :split], near_ref[...], preferred_element_type=F32
    ) + jnp.dot(x_ref[:, split:], core_ref[...], preferred_element_type=F32)
    wide = 2 * key_heads * HEAD_SIZE
    raw = jnp.dot(
        x_ref[:, :split], near_kv_ref[:, :wide], preferred_element_type=F32
    ) + jnp.dot(x_ref[:, split:], core_kv_ref[:, :wide], preferred_element_type=F32)
    raw_ref[:, queries:] = raw[:, : key_heads * HEAD_SIZE]
    low_ref[:, heads * HEAD_SIZE :] = raw[:, key_heads * HEAD_SIZE :].astype(BF16)
    for h in range(heads):
        u = raw_ref[:, head_columns(h)]
        gain = gains_ref[0:1, :] if h < query_heads else gains_ref[1:2, :]
        low_ref[:, head_columns(h)] = rotated(
            u * inverse_rms(u) * gain, cosine_ref[...], sine_ref[...]
        ).astype(BF16)
    allowed = causal(rows)
    for h in range(query_heads):
        k = query_heads + h * key_heads // query_heads
        scores = against(low_ref[:, head_columns(h)], low_ref[:, head_columns(k)]) / math.sqrt(
            HEAD_SIZE
        )
        scores = jnp.where(allowed, scores, -jnp.inf)
        row_max = jnp.max(scores, axis=1, keepdims=True)
        exps = jnp.exp(scores - row_max)
        total = jnp.sum(exps, axis=1, keepdims=True)
        lse_ref[:, h : h + 1] = row_max + jnp.log(total)
        mixed_ref[:, head_columns(h)] = jnp.dot(
            (exps * (1.0 / total)).astype(BF16),
            low_ref[:, head_columns(k + key_heads)],
            preferred_element_type=F32,
        ).astype(BF16)
    part = jnp.dot(mixed_ref[...], wo_ref[...], preferred_element_type=F32)
    upper_ref[...] = part[: rows // 2].astype(BF16)
    lower_ref[...] = part[rows // 2 :].astype(BF16)


def attention(x, near, core, near_kv, core_kv, gains, cosine, sine, wo, key_heads):
    rows = x.shape[0]
    query_width, features = wo.shape
    width = query_width + 2 * key_heads * HEAD_SIZE
    shapes = [
        ((rows, query_width + key_heads * HEAD_SIZE), F32),
        ((rows, width), BF16),
        ((rows, query_width), BF16),
        ((rows, query_width // HEAD_SIZE), F32),
        ((rows // 2, features), BF16),
        ((rows // 2, features), BF16),
    ]
    return pl.pallas_call(
        functools.partial(attention_kernel, key_heads),
        out_shape=[jax.ShapeDtypeStruct(*v) for v in shapes],
        compiler_params=pltpu.CompilerParams(vmem_limit_bytes=32 * 1024 * 1024),
        cost_estimate=SMALL,
    )(x, near, core, near_kv, core_kv, gains, cosine, sine, wo)


def attention_back_kernel(
    key_heads,
    place_ref,
    upstream_ref,
    wo_ref,
    raw_ref,
    low_ref,
    lse_ref,
    gains_ref,
    cosine_ref,
    sine_ref,
    x_ref,
    near_ref,
    core_ref,
    near_kv_ref,
    core_kv_ref,
    beside_ref,
    feature_ref,
    weights_ref,
    mixed_grad_ref,
    raw_grad_ref,
):
    rows = upstream_ref.shape[0]
    split = near_ref.shape[0]
    width = raw_grad_ref.shape[1]
    queries_width = near_ref.shape[1]
    query_heads = mixed_grad_ref.shape[1] // HEAD_SIZE
    group = query_heads // key_heads
    root = math.sqrt(HEAD_SIZE)
    mixed_grad_ref[...] = against(upstream_ref[...], wo_ref[...]).astype(BF16)
    allowed = causal(rows)
    cosine = cosine_ref[...]
    sine = sine_ref[...]

    def norm_back(h, grad, gain):
        u = raw_ref[:, head_columns(h)]
        scale = inverse_rms(u)
        normal = u * scale
        turned = grad * cosine - pltpu.roll(grad, HEAD_SIZE // 2, 1) * sine
        weighted = turned * gain
        inward = scale * (weighted - normal * jnp.mean(weighted * normal, axis=1, keepdims=True))
        raw_grad_ref[:, head_columns(h)] = inward.astype(BF16)
        return turned * normal

    query_terms = jnp.zeros((rows, HEAD_SIZE), F32)
    key_terms = jnp.zeros((rows, HEAD_SIZE), F32)
    for k in range(key_heads):
        keys = low_ref[:, head_columns(query_heads + k)]
        values = low_ref[:, head_columns(query_heads + key_heads + k)]
        key_grad = jnp.zeros((rows, HEAD_SIZE), F32)
        value_grad = jnp.zeros((rows, HEAD_SIZE), F32)
        for h in range(k * group, (k + 1) * group):
            queries = low_ref[:, head_columns(h)]
            mixed_grad = mixed_grad_ref[:, head_columns(h)]
            scores = against(queries, keys) / root
            probs = jnp.where(allowed, jnp.exp(scores - lse_ref[:, h : h + 1]), 0.0)
            probs_grad = against(mixed_grad, values)
            value_grad += over_rows(probs.astype(BF16), mixed_grad)
            inner = jnp.sum(probs * probs_grad, axis=1, keepdims=True)
            scores_grad = (probs * (probs_grad - inner)).astype(BF16)
            query_grad = jnp.dot(scores_grad, keys, preferred_element_type=F32) / root
            key_grad += over_rows(scores_grad, queries)
            query_terms += norm_back(h, query_grad, gains_ref[0:1, :])
        key_terms += norm_back(query_heads + k, key_grad / root, gains_ref[1:2, :])
        raw_grad_ref[:, head_columns(query_heads + key_heads + k)] = value_grad.astype(BF16)
    raw_grad = raw_grad_ref[...]
    for part, (query_ref, kv_ref) in enumerate(
        ((near_ref, near_kv_ref), (core_ref, core_kv_ref))
    ):
        feature_ref[:, part * split : (part + 1) * split] = (
            against(raw_grad[:, :queries_width], query_ref[...])
            + against(raw_grad[:, queries_width:], kv_ref[:, : width - queries_width])
        ).astype(BF16)
    feature_ref[:, 2 * split : 2 * split + HEAD_SIZE] = query_terms.astype(BF16)
    feature_ref[:, 2 * split + HEAD_SIZE :] = key_terms.astype(BF16)
    count = place_ref.shape[0]
    block = 2 * split // count
    for j in range(count):
        at = pl.ds(pl.multiple_of(place_ref[j] * block, block), block)
        if block % LANES == 0:
            columns = x_ref[:, j * block : (j + 1) * block]
            weights_ref[at, :width] = over_rows(columns, raw_grad).astype(BF16)
    if block % LANES:
        weights_ref[:, :width] = over_rows(x_ref[...], raw_grad).astype(BF16)
    weights_ref[:, width:] = beside_ref[...]


def in_vmem(count):
    return [pl.BlockSpec()] * count


def in_smem():
    return [pl.BlockSpec(memory_space=pltpu.SMEM)]


def attention_back(
    where, upstream, wo, raw, low, lse, gains, cosine, sine, x, weights, beside, key_heads
):
    rows, features = upstream.shape
    query_width = wo.shape[0]
    split = weights[0].shape[0]
    width = low.shape[1]
    whole = width + beside.shape[1]
    shapes = [
        ((rows, features + 2 * HEAD_SIZE), BF16),
        ((features, whole), BF16),
    ]
    operands = [upstream, wo, raw, low, lse, gains, cosine, sine, x, *weights, beside]
    return pl.pallas_call(
        functools.partial(attention_back_kernel, key_heads),
        in_specs=in_smem() + in_vmem(len(operands)),
        out_specs=in_vmem(2),
        out_shape=[jax.ShapeDtypeStruct(*v) for v in shapes],
        scratch_shapes=[pltpu.VMEM((rows, query_width), BF16), pltpu.VMEM((rows, width), BF16)],
        compiler_params=pltpu.CompilerParams(vmem_limit_bytes=40 * 1024 * 1024),
        cost_estimate=SMALL,
    )(jnp.stack(where).astype(jnp.int32), *in_hbm(*operands))


def chunk_places():
    return jnp.stack(
        [lax.axis_index("tp") ^ m for m in range(lax.axis_size("tp"))]
    ).astype(jnp.int32)


def rows_at(index, size):
    return pl.ds(pl.multiple_of(index * size, size), size)


def resid_kernel(place_ref, *refs):
    *pieces, hidden_ref, gain_ref, resid_ref, routed_ref = refs
    rows = pieces[0].shape[0]
    for m, piece in enumerate(pieces):
        at = rows_at(place_ref[m], rows)
        resid = hidden_ref[at, :].astype(F32) + piece[...].astype(F32)
        resid_ref[at, :] = resid
        routed_ref[at, :] = (resid * inverse_rms(resid) * gain_ref[...]).astype(BF16)


def resid_and_routed(pieces, hidden, gain):
    return pl.pallas_call(
        resid_kernel,
        in_specs=in_smem() + in_vmem(len(pieces) + 2),
        out_specs=in_vmem(2),
        out_shape=[
            pltpu.HBM(hidden.shape, F32),
            jax.ShapeDtypeStruct(hidden.shape, BF16),
        ],
        compiler_params=pltpu.CompilerParams(vmem_limit_bytes=6 * 1024 * 1024),
        cost_estimate=SMALL,
    )(chunk_places(), *pieces, hidden, gain)


def resid_back_kernel(parts, place_ref, column_ref, *refs):
    pieces = refs[: 2 * parts]
    (
        resid_a_ref,
        resid_b_ref,
        routed_a_ref,
        routed_b_ref,
        ids_ref,
        router_ref,
        gain_ref,
        upstream_ref,
        mixed_ref,
        grad_ref,
        low_ref,
        beside_ref,
        keep_ref,
        send_ref,
        returned_ref,
        wide_ref,
    ) = refs[2 * parts :]
    rows, features = upstream_ref.shape
    expert_count = router_ref.shape[1]
    chunk = pieces[0].shape[0]
    for h in range(2):
        for m in range(parts):
            returned_ref[rows_at(place_ref[m] + h * parts, chunk), :] = pieces[h * parts + m][...]
    routed = jnp.concatenate([routed_a_ref[...], routed_b_ref[...]], axis=0)
    resid = jnp.concatenate([resid_a_ref[...], resid_b_ref[...]], axis=0)
    logits = jnp.dot(routed, router_ref[...], preferred_element_type=F32)
    lane = lax.broadcasted_iota(jnp.int32, (rows, expert_count), 1)
    named = ids_ref[:, 0:1] == lane
    for k in range(1, TOP):
        named = named | (ids_ref[:, k : k + 1] == lane)
    exponent = jnp.exp(logits - jnp.max(logits, axis=1, keepdims=True))
    router = exponent / jnp.sum(exponent, axis=1, keepdims=True)
    chosen = jnp.where(named, router, 0.0)
    total = jnp.sum(chosen, axis=1, keepdims=True)
    gates = chosen / total
    tail = returned_ref[:, features:].astype(F32)
    tail = tail + pltpu.roll(tail, tail.shape[1] - expert_count, 1)
    grad_gates = jnp.where(named, tail[:, :expert_count], 0.0)
    inner = jnp.sum(grad_gates * gates, axis=1, keepdims=True)
    grad_router = jnp.where(named, (grad_gates - inner) / total, 0.0)
    inner = jnp.sum(router * grad_router, axis=1, keepdims=True)
    grad_logits = (router * (grad_router - inner)).astype(BF16)
    grad_routed = returned_ref[:, :features].astype(F32) + against(grad_logits, router_ref[...])
    scale = inverse_rms(resid)
    normal = resid * scale
    weighted = grad_routed * gain_ref[...]
    inner = jnp.mean(weighted * normal, axis=1, keepdims=True)
    grad = upstream_ref[...].astype(F32) + scale * (weighted - normal * inner)
    grad_ref[...] = grad
    low_ref[...] = grad.astype(BF16)
    half = column_ref.shape[0] // 2
    for j in range(half):
        for k, out_ref in ((j, keep_ref), (half + j, send_ref)):
            columns = pl.ds(pl.multiple_of(column_ref[k] * LANES, LANES), LANES)
            out_ref[j * LANES : (j + 1) * LANES, :] = over_rows(
                mixed_ref[:, columns], low_ref[...]
            ).astype(BF16)
    wide_ref[...] = jnp.zeros(wide_ref.shape, BF16)
    wide_ref[:, :expert_count] = grad_logits
    one = lax.broadcasted_iota(jnp.int32, wide_ref.shape, 1) == expert_count
    beside_ref[...] = (
        over_rows(routed, wide_ref[...])
        + over_rows((grad_routed * normal).astype(BF16), one.astype(F32).astype(BF16))
    ).astype(BF16)


def resid_back(pieces, resid, routed, ids, router, gain, upstream, mixed, columns):
    parts = len(pieces) // 2
    rows, features = upstream.shape
    expert_count = router.shape[1]
    wide = -(-(expert_count + 1) // LANES) * LANES
    half = mixed.shape[1] // 2
    shapes = [
        ((rows, features), F32),
        ((rows, features), BF16),
        ((features, wide), BF16),
        ((half, features), BF16),
        ((half, features), BF16),
    ]
    operands = [*pieces, *in_hbm(*resid, *routed, ids, router, gain, upstream, mixed)]
    return pl.pallas_call(
        functools.partial(resid_back_kernel, parts),
        in_specs=in_smem() * 2 + in_vmem(len(operands)),
        out_specs=in_vmem(len(shapes)),
        out_shape=[jax.ShapeDtypeStruct(*v) for v in shapes],
        scratch_shapes=[
            pltpu.VMEM((rows, pieces[0].shape[1]), BF16),
            pltpu.VMEM((rows, wide), BF16),
        ],
        compiler_params=pltpu.CompilerParams(vmem_limit_bytes=40 * 1024 * 1024),
        cost_estimate=SMALL,
    )(chunk_places(), jnp.stack(columns).astype(jnp.int32), *operands)


def input_kernel(ordered, place_ref, block_ref, *refs):
    *pieces, hidden_ref, resid_grad_ref, gain_ref, result_ref, late_ref, total_ref = refs
    features = hidden_ref.shape[1]
    rows = pieces[0].shape[0]
    count = block_ref.shape[0]
    block = features // count
    for m, piece in enumerate(pieces):
        total_ref[rows_at(place_ref[m], rows), :] = piece[...]
    hidden = hidden_ref[...].astype(F32)
    scale = inverse_rms(hidden)
    columns = [
        slice(j * block, (j + 1) * block)
        if ordered
        else pl.ds(pl.multiple_of(block_ref[j] * block, block), block)
        for j in range(count)
    ]
    inner = jnp.zeros((hidden.shape[0], 1), F32)
    for j in range(count):
        normal = hidden_ref[:, columns[j]].astype(F32) * scale
        grad = total_ref[:, j * block : (j + 1) * block].astype(F32)
        terms = grad * normal
        inner += jnp.sum(terms * gain_ref[:, columns[j]], axis=1, keepdims=True)
        late_ref[j : j + 1, :block] = jnp.sum(terms, axis=0, keepdims=True)
    inner = inner * (1.0 / features)
    for j in range(count):
        normal = hidden_ref[:, columns[j]].astype(F32) * scale
        weighted = total_ref[:, j * block : (j + 1) * block].astype(F32) * gain_ref[:, columns[j]]
        result_ref[:, columns[j]] = resid_grad_ref[:, columns[j]] + scale * (
            weighted - normal * inner
        )
    heads = jnp.sum(total_ref[:, features:].astype(F32), axis=0, keepdims=True)
    late_ref[:, block:] = jnp.broadcast_to(heads, (count, heads.shape[1]))


def input_gradient(pieces, hidden, resid_grad, gain, where):
    rows, features = hidden.shape
    count = len(where)
    extra = pieces[0].shape[1] - features
    return pl.pallas_call(
        functools.partial(input_kernel, absolute()),
        in_specs=in_smem() * 2 + in_vmem(len(pieces) + 3),
        out_specs=in_vmem(2),
        out_shape=[
            jax.ShapeDtypeStruct((rows, features), F32),
            jax.ShapeDtypeStruct((count, features // count + extra), F32),
        ],
        scratch_shapes=[pltpu.VMEM((rows, pieces[0].shape[1]), BF16)],
        compiler_params=pltpu.CompilerParams(vmem_limit_bytes=24 * 1024 * 1024),
        cost_estimate=SMALL,
    )(chunk_places(), jnp.stack(where).astype(jnp.int32), *pieces, *in_hbm(hidden, resid_grad, gain))


def widen_kernel(place_ref, near_ref, core_ref, result_ref):
    early = pl.program_id(0) < pl.num_programs(0) // 2
    result_ref[...] = jnp.where(early, near_ref[...], core_ref[...]).astype(F32)


def widen_blocks(near, core, where):
    count = len(where)
    features = near.shape[1]
    block = 2 * near.shape[0] // count
    half = count // 2
    first = pl.BlockSpec((block, features), lambda i, s: (jnp.minimum(i, half - 1), 0))
    second = pl.BlockSpec((block, features), lambda i, s: (jnp.maximum(i - half, 0), 0))
    return pl.pallas_call(
        widen_kernel,
        grid_spec=pltpu.PrefetchScalarGridSpec(
            num_scalar_prefetch=1,
            grid=(count,),
            in_specs=[first, second],
            out_specs=pl.BlockSpec((block, features), lambda i, s: (s[i], 0)),
        ),
        out_shape=jax.ShapeDtypeStruct((block * count, features), F32),
        compiler_params=pltpu.CompilerParams(vmem_limit_bytes=24 * 1024 * 1024),
        cost_estimate=SMALL,
    )(jnp.stack(where).astype(jnp.int32), near, core)


def shards(
    hidden_in,
    expert_ids,
    attention_gain,
    query_gain,
    key_gain,
    query_weight,
    key_matrix,
    value_matrix,
    output_weight,
    expert_gain,
    router_weight,
    gate_up_weight,
    down_weight,
    output_grad,
):
    tokens, features = hidden_in.shape
    owners = lax.axis_size("ep")
    local_experts = gate_up_weight.shape[0]
    expert_count = local_experts * owners
    rows_a = tokens // 2

    head_share = query_gain.shape[0]
    share = router_weight.shape[0]
    small_rows = max(tokens, share)
    padded = lambda v: jnp.pad(v.astype(BF16), ((0, small_rows - v.shape[0]), (0, 0)))
    small = jnp.concatenate(
        [
            padded(router_weight),
            padded(jnp.stack([attention_gain, expert_gain], axis=1)),
            padded(jnp.stack([query_gain, key_gain], axis=1)),
            padded(expert_ids),
        ],
        axis=1,
    )
    small_width = small.shape[1]
    small = jnp.pad(small, ((0, 0), (0, -small_width % LANES)))
    packed = jnp.concatenate([key_matrix, value_matrix], axis=1)
    packed_width = packed.shape[1]
    together = small_rows == share
    if together:
        packed = jnp.concatenate([packed, small], axis=1)
    packed_hops = gather_hops(packed)
    hops = gather_hops(query_weight)
    packed_near = gather_near(packed, packed_hops)
    packed_core = gather_core(packed_near, packed_hops)
    if together:
        small = jnp.concatenate(
            [packed_near[:, packed_width:], packed_core[:, packed_width:]], axis=0
        )
    else:
        small = lax.all_gather(small, "ep", axis=0, tiled=True)
    small = put_blocks(small, 0).reshape(owners, small_rows, -1)
    by_feature = small[:, :share, : expert_count + 2].reshape(features, -1)
    router_full = by_feature[:, :expert_count]
    attn_gain_full = by_feature[:, expert_count].astype(F32)[None, :]
    mlp_gain_full = by_feature[:, expert_count + 1].astype(F32)[None, :]
    gains = (
        small[:, :head_share, expert_count + 2 : expert_count + 4]
        .reshape(HEAD_SIZE, 2)
        .astype(F32)
        .T
    )
    ids_all = small[:, :tokens, expert_count + 4 : small_width].reshape(-1, TOP).astype(jnp.int32)
    wd = down_weight.reshape(-1, features)
    normed_low = norm_rows(hidden_in.astype(F32), attn_gain_full).astype(BF16)
    normed_rel = pick_blocks(normed_low, 1)
    positions = jnp.arange(tokens, dtype=jnp.int32)
    cosine, sine_table = rope_tables(positions, HEAD_SIZE)
    (
        hops,
        packed_core,
        normed_rel,
        cosine,
        sine_table,
        gains,
        router_full,
        attn_gain_full,
        mlp_gain_full,
        ids_all,
        output_all,
        gate_up_low,
    ) = join(
        hops,
        packed_core,
        normed_rel,
        cosine,
        sine_table,
        gains,
        router_full,
        attn_gain_full,
        mlp_gain_full,
        ids_all,
        output_grad,
        gate_up_weight,
    )

    near = gather_near(query_weight, hops)
    weights_rel = [near, gather_core(near, hops), packed_near, packed_core]
    output_all = lax.all_gather(output_all, "ep", axis=0, tiled=True)
    query_width = query_weight.shape[1]
    key_width = key_matrix.shape[1]
    key_heads = key_width // HEAD_SIZE
    raw, low, attention_output, lse, *head_parts = attention(
        normed_rel, *weights_rel, gains, cosine, sine_table, output_weight, key_heads
    )
    (head_parts,) = join(head_parts)
    head_parts = list(head_parts)

    hops = reduce_hops(head_parts[0])
    wgu = gate_up_low.transpose(1, 0, 2).reshape(features, -1)
    hops, wgu, head_parts[1] = join(hops, wgu, head_parts[1])

    chunk = reduce_total(head_parts[0], hops)
    hops_b = reduce_hops(head_parts[1])
    (hops,) = join(spread_hops(chunk))

    resid_a, routed_a = resid_and_routed([chunk] + hops, hidden_in[:rows_a], mlp_gain_full)
    chunk = reduce_total(head_parts[1], hops_b)
    hops_a, hops = join(gather_hops(routed_a), spread_hops(chunk))

    resid_b, routed_b = resid_and_routed([chunk] + hops, hidden_in[rows_a:], mlp_gain_full)
    near_a = gather_near(routed_a, hops_a)
    core_a = gather_core(near_a, hops_a)
    hops_b = gather_hops(routed_b)
    lined = places()
    where = [2 * b + h for h in range(2) for b in lined]

    def experts(piece, x):
        rows = slice(piece * owners // 2, (piece + 1) * owners // 2)
        return run_experts(
            x, output_all, ids_all, where[rows], router_full, wgu, wd, local_experts
        )

    keep_a, joined_0, hidden_0 = experts(0, near_a)
    send_a, joined_1, hidden_1 = experts(1, core_a)
    hops_b, send_a, keep_a = join(hops_b, send_a, keep_a)

    near_b = gather_near(routed_b, hops_b)
    core_b = gather_core(near_b, hops_b)
    come = scatter_swap(send_a)
    keep_b, joined_2, hidden_2 = experts(2, near_b)
    come, core_b, keep_b = join(come, core_b, keep_b)

    sums_a = scatter_sums(keep_a, come)
    hops_a = scatter_hops(sums_a)
    send_b, joined_3, hidden_3 = experts(3, core_b)
    hops_a, send_b = join(hops_a, send_b)
    joined = [joined_0, joined_1, joined_2, joined_3]
    hidden = [hidden_0, hidden_1, hidden_2, hidden_3]
    routed_pieces = [near_a, core_a, near_b, core_b]

    come = scatter_swap(send_b)
    total_a = scatter_total(sums_a, hops_a)
    hops = reduce_hops(total_a)
    come, hidden = join(come, hidden)

    sums_b = scatter_sums(keep_b, come)
    hops_b = scatter_hops(sums_b)
    mixture_parts = mixture_product(hidden, wd, lined)
    chunk_a = reduce_total(total_a, hops)
    spread_a, hops_b, mixture_parts, joined = join(
        spread_hops(chunk_a), hops_b, mixture_parts, joined
    )

    mixture = lax.psum_scatter(mixture_parts, "ep", scatter_dimension=0, tiled=True)
    total_b = scatter_total(sums_b, hops_b)
    (hops,) = join(reduce_hops(total_b))
    chunk_b = reduce_total(total_b, hops)
    (spread_b,) = join(spread_hops(chunk_b))

    columns = (
        [jnp.int32(b) for b in range(attention_output.shape[1] // LANES)] if absolute() else lined
    )
    grad_resid, grad_attended, by_feature, output_keep, output_send = resid_back(
        [chunk_a, *spread_a, chunk_b, *spread_b],
        [resid_a, resid_b],
        [routed_a, routed_b],
        expert_ids,
        router_full,
        mlp_gain_full,
        output_grad,
        attention_output,
        columns,
    )

    feature_part, weights_grad = attention_back(
        lined,
        grad_attended,
        output_weight,
        raw,
        low,
        lse,
        gains,
        cosine,
        sine_table,
        normed_rel,
        weights_rel,
        by_feature,
        key_heads,
    )
    come, feature_part, weights_grad = join(
        scatter_swap(output_send), feature_part, weights_grad
    )

    weights_rows = lax.psum_scatter(weights_grad, "ep", scatter_dimension=0, tiled=True)
    hops = reduce_hops(feature_part)
    output_sums = scatter_sums(output_keep, come)
    output_hops = scatter_hops(output_sums)
    down_grad = down_product(hidden, output_all, where).reshape(down_weight.shape)
    hops, output_hops, down_grad, mixture, joined = join(
        hops, output_hops, down_grad, mixture, joined
    )

    chunk = reduce_total(feature_part, hops)
    hops = spread_hops(chunk)
    mixture_hops = reduce_hops(mixture)
    output_share = scatter_total(output_sums, output_hops)
    gate_up_grad = gate_up_product(routed_pieces, joined, gate_up_weight.shape)
    hops, gate_up_grad, output_share = join(hops, gate_up_grad, output_share)

    output_hops = gather_hops(output_share)
    input_grad, late = input_gradient(
        [chunk, *hops], hidden_in, grad_resid, attn_gain_full, lined
    )
    late_come = scatter_swap(late[owners // 2 :])
    late_come, output_hops, mixture_hops = join(late_come, output_hops, mixture_hops)

    mixture_chunk = reduce_total(mixture, mixture_hops)
    mixture_hops = spread_hops(mixture_chunk)
    near = gather_near(output_share, output_hops)
    output_core = gather_core(near, output_hops)
    late_sums = scatter_sums(late[: owners // 2], late_come)
    late_hops = scatter_hops(late_sums)
    output_weight_grad = widen_blocks(near, output_core, lined)
    late_hops, output_weight_grad, weights_rows, mixture_hops = join(
        late_hops, output_weight_grad, weights_rows, mixture_hops
    )
    weights_rows = weights_rows.astype(F32)
    late = scatter_total(late_sums, late_hops)[0]
    head_grads = lax.dynamic_slice_in_dim(
        late[share:].reshape(2, HEAD_SIZE), lax.axis_index("ep") * head_share, head_share, 1
    )
    early = weights_rows[:, query_width + 2 * key_width :]
    mixture = spread_total(mixture_chunk, mixture_hops)
    block_out = (jnp.concatenate([resid_a, resid_b], axis=0) + mixture.astype(F32)).astype(BF16)
    return (
        block_out,
        input_grad,
        late[:share],
        head_grads[0],
        head_grads[1],
        weights_rows[:, :query_width],
        weights_rows[:, query_width : query_width + key_width],
        weights_rows[:, query_width + key_width : query_width + 2 * key_width],
        output_weight_grad,
        early[:, expert_count],
        early[:, :expert_count],
        gate_up_grad,
        down_grad,
    )


def solution(mesh):
    in_specs = (
        P("ep", None),
        P("ep", None),
        P("ep"),
        P("ep"),
        P("ep"),
        P("ep", "tp"),
        P("ep", "tp"),
        P("ep", "tp"),
        P("tp", None),
        P("ep"),
        P("ep", None),
        P("ep", None, "tp"),
        P("ep", "tp", None),
        P("ep", None),
    )
    out_specs = (
        P("ep", None),
        P("ep", None),
        P("ep"),
        P("ep"),
        P("ep"),
        P("ep", "tp"),
        P("ep", "tp"),
        P("ep", "tp"),
        P("tp", None),
        P("ep"),
        P("ep", None),
        P("ep", None, "tp"),
        P("ep", "tp", None),
    )
    return jax.shard_map(shards, mesh=mesh, in_specs=in_specs, out_specs=out_specs, check_vma=False)
```

```python
import functools
import math

import jax
import jax.numpy as jnp
from jax import lax
from jax.experimental import pallas as pl
from jax.experimental.pallas import tpu as pltpu
from jax.sharding import PartitionSpec as P

HEAD_SIZE = 128
TOP = 8
PAIR = 64
LANES = 128

EPSILON = 1e-06
THETA = 1000000.0
F32 = jnp.float32
BF16 = jnp.bfloat16
SMALL = pl.CostEstimate(flops=0, bytes_accessed=1024, transcendentals=0)


def norm_rows(value_rows, norm_gain):
    return (
        value_rows
        * lax.rsqrt(jnp.mean(value_rows * value_rows, axis=-1, keepdims=True) + EPSILON)
        * norm_gain
    )


def rope_tables(positions, head_size):
    halfway = head_size // 2
    inverse = THETA ** (-(jnp.arange(halfway, dtype=jnp.float32) * 2.0) / head_size)
    angles = positions.astype(jnp.float32)[:, None] * inverse[None, :]
    cosine, sine = jnp.cos(angles), jnp.sin(angles)
    return (
        jnp.concatenate([cosine, cosine], axis=1),
        jnp.concatenate([-sine, sine], axis=1),
    )


SWAPPED = 8


def swap(value, axis, mask):
    count = lax.axis_size(axis)
    return lax.ppermute(value, axis, [(i, i ^ mask) for i in range(count)])


def join(*values):
    return lax.optimization_barrier(values)


ORDER = (0, 2, 4, 6, 1, 3, 5, 7)


def plus(*values):
    total = values[0].astype(F32)
    for v in values[1:]:
        total = total + v.astype(F32)
    return total.astype(values[0].dtype)


def absolute():
    return lax.axis_size("ep") > SWAPPED


def in_hbm(*values):
    return [pltpu.with_memory_space_constraint(v, pltpu.HBM) for v in values]


def stack_kernel(*refs):
    *pieces, result_ref = refs
    rows = pieces[0].shape[0]
    for i, piece in enumerate(pieces):
        result_ref[i * rows : (i + 1) * rows, :] = piece[...]


def stack_rows(pieces):
    rows = pieces[0].shape[0]
    return pl.pallas_call(
        stack_kernel,
        out_shape=jax.ShapeDtypeStruct(
            (len(pieces) * rows,) + pieces[0].shape[1:], pieces[0].dtype
        ),
        compiler_params=pltpu.CompilerParams(vmem_limit_bytes=8 * 1024 * 1024),
        cost_estimate=SMALL,
    )(*pieces)


def gather_hops(value):
    if absolute():
        return [lax.all_gather(value, "ep", axis=0, tiled=True)]
    return [swap(value, "ep", m) for m in ORDER[1:4]]


def gather_near(value, hops):
    if absolute():
        return hops[0][: hops[0].shape[0] // 2]
    return stack_rows([value] + hops)


def gather_core(near, hops):
    if absolute():
        return hops[0][hops[0].shape[0] // 2 :]
    return swap(near, "ep", 1)


def scatter_swap(send):
    return send if absolute() else swap(send, "ep", 1)


def scatter_sums(keep, come):
    if absolute():
        return [jnp.concatenate([keep, come], axis=0)]
    rows = keep.shape[0] // 4
    return [
        plus(keep[i * rows : (i + 1) * rows], come[i * rows : (i + 1) * rows]) for i in range(4)
    ]


def scatter_hops(sums):
    if absolute():
        return [lax.psum_scatter(sums[0], "ep", scatter_dimension=0, tiled=True)]
    return [swap(v, "ep", m) for v, m in zip(sums[1:], ORDER[1:4])]


def scatter_total(sums, hops):
    return hops[0] if absolute() else plus(sums[0], *hops)


def chunk_of(value, index):
    rows = value.shape[0] // lax.axis_size("tp")
    return lax.dynamic_slice_in_dim(value, index * rows, rows, 0)


def reduce_hops(value):
    mine = lax.axis_index("tp")
    return [swap(chunk_of(value, mine ^ m), "tp", m) for m in range(1, lax.axis_size("tp"))]


def reduce_total(value, hops):
    return plus(chunk_of(value, lax.axis_index("tp")), *hops)


def spread_hops(chunk):
    return [swap(chunk, "tp", m) for m in range(1, lax.axis_size("tp"))]


def spread_total(chunk, hops):
    mine = lax.axis_index("tp")
    rows = chunk.shape[0]
    result = jnp.zeros(((len(hops) + 1) * rows,) + chunk.shape[1:], chunk.dtype)
    for m, piece in enumerate([chunk] + hops):
        result = lax.dynamic_update_slice_in_dim(result, piece, (mine ^ m) * rows, 0)
    return result


def places():
    if absolute():
        return [jnp.int32(b) for b in range(lax.axis_size("ep"))]
    return [lax.axis_index("ep") ^ m for m in ORDER]


def pick_blocks(value, axis):
    count = lax.axis_size("ep")
    if count > SWAPPED:
        return value
    mine = lax.axis_index("ep")
    size = value.shape[axis] // count
    return jnp.concatenate(
        [lax.dynamic_slice_in_dim(value, (mine ^ m) * size, size, axis) for m in ORDER],
        axis=axis,
    )


def put_blocks(value, axis):
    count = lax.axis_size("ep")
    if count > SWAPPED:
        return value
    mine = lax.axis_index("ep")
    size = value.shape[axis] // count
    place = lambda m: (m // 2 + (m % 2) * (count // 2)) * size
    return jnp.concatenate(
        [lax.dynamic_slice_in_dim(value, place(mine ^ b), size, axis) for b in range(count)],
        axis=axis,
    )


def expert_kernel(
    local,
    place_ref,
    x_ref,
    g0_ref,
    g1_ref,
    ids0_ref,
    ids1_ref,
    router_ref,
    wgu_in_ref,
    wd_in_ref,
    dx_ref,
    joined_ref,
    hidden_ref,
    wgu_ref,
    wd_ref,
    arrived,
):
    rows = x_ref.shape[0]
    features = x_ref.shape[1]
    expert_count = router_ref.shape[1]
    hidden_count = wd_ref.shape[0]
    group = 3
    count = hidden_count // LANES // group
    copies = [
        pltpu.make_async_copy(wgu_in_ref, wgu_ref, arrived.at[0]),
        pltpu.make_async_copy(wd_in_ref, wd_ref, arrived.at[1]),
    ]

    @pl.when(pl.program_id(0) == 0)
    def _():
        for copy in copies:
            copy.start()

    extra = dx_ref.shape[1] - features
    base = place_ref[0]
    x = x_ref[...]
    upstream = jnp.concatenate([g0_ref[...], g1_ref[...]], axis=0)
    ids = jnp.concatenate([ids0_ref[...], ids1_ref[...]], axis=0)
    logits = jnp.dot(x, router_ref[...], preferred_element_type=F32)
    lane = lax.broadcasted_iota(jnp.int32, (rows, expert_count), 1)
    named = ids[:, 0:1] == lane
    for k in range(1, TOP):
        named = named | (ids[:, k : k + 1] == lane)
    exponent = jnp.exp(logits - jnp.max(logits, axis=1, keepdims=True))
    router = exponent / jnp.sum(exponent, axis=1, keepdims=True)
    chosen = jnp.where(named, router, 0.0)
    gates = chosen / jnp.sum(chosen, axis=1, keepdims=True)
    gate = [
        jnp.sum(jnp.where(lane == base + j, gates, 0.0), axis=1, keepdims=True)
        for j in range(local)
    ]
    left = lax.broadcasted_iota(jnp.int32, (rows, LANES), 1) < PAIR
    per_expert = hidden_count // local // PAIR
    gate_sum = [jnp.zeros((rows, LANES), F32) for _ in range(local)]

    @pl.when(pl.program_id(0) == 0)
    def _():
        for copy in copies:
            copy.wait()

    def products(q):
        wide = group * LANES
        act = jnp.dot(
            x, wgu_ref[:, 2 * q * wide : 2 * (q + 1) * wide], preferred_element_type=F32
        )
        back = lax.dot_general(
            upstream,
            wd_ref[q * wide : (q + 1) * wide, :],
            (((1,), (1,)), ((), ())),
            preferred_element_type=F32,
        )
        return act, back

    def elementwise(q, act, back):
        for i in range(group):
            p = q * group + i
            one, two = 2 * p // per_expert, (2 * p + 1) // per_expert
            first = act[:, 2 * i * LANES : (2 * i + 1) * LANES]
            second = act[:, (2 * i + 1) * LANES : (2 * i + 2) * LANES]
            g = jnp.where(left, first, pltpu.roll(second, PAIR, 1))
            u = jnp.where(left, pltpu.roll(first, PAIR, 1), second)
            gh = back[:, i * LANES : (i + 1) * LANES]
            if one == two:
                scale = jnp.broadcast_to(gate[one], (rows, LANES))
            else:
                scale = jnp.where(left, gate[one], gate[two])
            sig = lax.logistic(g)
            silu = g * sig
            hid = silu * u
            product = hid * gh
            if one == two:
                gate_sum[one] += product
            else:
                gate_sum[one] += jnp.where(left, product, 0.0)
                gate_sum[two] += jnp.where(left, 0.0, product)
            hidden_ref[:, p * LANES : (p + 1) * LANES] = (hid * scale).astype(BF16)
            gs = gh * scale
            dg = gs * u * sig * (1.0 + g * (1.0 - sig))
            du = gs * silu
            joined_ref[:, 2 * p * LANES : (2 * p + 1) * LANES] = jnp.where(
                left, dg, pltpu.roll(du, PAIR, 1)
            ).astype(BF16)
            joined_ref[:, (2 * p + 1) * LANES : (2 * p + 2) * LANES] = jnp.where(
                left, pltpu.roll(dg, PAIR, 1), du
            ).astype(BF16)

    waiting = []
    for q in range(count):
        waiting.append((q, *products(q)))
        if q:
            elementwise(*waiting.pop(0))
    elementwise(*waiting.pop(0))
    dx = lax.dot_general(
        joined_ref[...], wgu_ref[...], (((1,), (1,)), ((), ())), preferred_element_type=F32
    )
    dx_ref[:, :features] = dx.astype(BF16)
    wide = lax.broadcasted_iota(jnp.int32, (rows, extra), 1)
    tail = jnp.zeros((rows, extra), F32)
    for j in range(local):
        total = jnp.sum(gate_sum[j], axis=1, keepdims=True)
        high = total.astype(BF16).astype(F32)
        tail = jnp.where(wide == base + j, high, tail)
        tail = jnp.where(wide == expert_count + base + j, total - high, tail)
    dx_ref[:, features:] = tail.astype(BF16)


def run_experts(x, g, ids, where, router, wgu, wd, local):
    tokens, features = x.shape
    tile = 256
    block = tokens // len(where)
    steps = tokens // tile
    expert_count = router.shape[1]
    extra = -(-2 * expert_count // LANES) * LANES
    place = jnp.stack([lax.axis_index("ep") * local] + list(where)).astype(jnp.int32)
    found = lambda width, j: pl.BlockSpec((block, width), lambda i, s: (s[1 + 2 * i + j], 0))
    whole = pl.BlockSpec(router.shape, lambda i, s: (0, 0), pipeline_mode=pl.Buffered(1))
    anywhere = pl.BlockSpec(memory_space=pl.ANY)
    by_rows = lambda width: pl.BlockSpec((tile, width), lambda i, s: (i, 0))
    in_specs = [
        by_rows(features),
        found(features, 0),
        found(features, 1),
        found(TOP, 0),
        found(TOP, 1),
        whole,
        anywhere,
        anywhere,
    ]
    g, wgu, wd = in_hbm(g, wgu, wd)
    operands = [place, x, g, g, ids, ids, router, wgu, wd]
    return pl.pallas_call(
        functools.partial(expert_kernel, local),
        grid_spec=pltpu.PrefetchScalarGridSpec(
            num_scalar_prefetch=1,
            grid=(steps,),
            in_specs=in_specs,
            out_specs=[
                by_rows(features + extra),
                by_rows(wgu.shape[1]),
                by_rows(wd.shape[0]),
            ],
            scratch_shapes=[
                pltpu.VMEM(wgu.shape, BF16),
                pltpu.VMEM(wd.shape, BF16),
                pltpu.SemaphoreType.DMA((2,)),
            ],
        ),
        out_shape=[
            pltpu.HBM((tokens, features + extra), BF16),
            pltpu.HBM((tokens, wgu.shape[1]), BF16),
            pltpu.HBM((tokens, wd.shape[0]), BF16),
        ],
        compiler_params=pltpu.CompilerParams(vmem_limit_bytes=32 * 1024 * 1024),
        cost_estimate=SMALL,
    )(*operands)


def gate_up_kernel(*refs):
    *operands, result_ref = refs
    count = len(operands) // 2
    total = None
    for x_ref, joined_ref in zip(operands[:count], operands[count:]):
        part = lax.dot_general(
            x_ref[...], joined_ref[...], (((0,), (0,)), ((), ())), preferred_element_type=F32
        )
        total = part if total is None else total + part
    width = result_ref.shape[2]
    for e in range(result_ref.shape[0]):
        result_ref[e] = total[:, e * width : (e + 1) * width]


def gate_up_product(pieces, joined, shape):
    rows, features = pieces[0].shape
    width = joined[0].shape[1]
    tile = 256
    whole = pl.BlockSpec((rows, width), lambda i: (0, 0), pipeline_mode=pl.Buffered(1))
    return pl.pallas_call(
        gate_up_kernel,
        grid=(features // tile,),
        in_specs=[pl.BlockSpec((rows, tile), lambda i: (0, i)) for _ in pieces]
        + [whole for _ in joined],
        out_specs=pl.BlockSpec((shape[0], tile, shape[2]), lambda i: (0, i, 0)),
        out_shape=jax.ShapeDtypeStruct(shape, F32),
        compiler_params=pltpu.CompilerParams(vmem_limit_bytes=56 * 1024 * 1024),
        cost_estimate=SMALL,
    )(*in_hbm(*pieces, *joined))


def down_kernel(place_ref, *refs):
    *pieces, g_ref, result_ref, sorted_ref = refs
    blocks = place_ref.shape[0] // len(pieces)
    block = pieces[0].shape[0] // blocks
    for i, hidden_ref in enumerate(pieces):
        for k in range(blocks):
            start = pl.multiple_of(place_ref[i * blocks + k] * block, block)
            sorted_ref[pl.ds(start, block), :] = hidden_ref[k * block : (k + 1) * block, :]
    result_ref[...] = lax.dot_general(
        sorted_ref[...], g_ref[...], (((0,), (0,)), ((), ())), preferred_element_type=F32
    )


def down_product(hidden, g, where):
    rows, features = g.shape
    width = hidden[0].shape[1]
    tile = 256
    return pl.pallas_call(
        down_kernel,
        grid_spec=pltpu.PrefetchScalarGridSpec(
            num_scalar_prefetch=1,
            grid=(width // tile,),
            in_specs=[pl.BlockSpec((v.shape[0], tile), lambda i, s: (0, i)) for v in hidden]
            + [pl.BlockSpec((rows, features), lambda i, s: (0, 0), pipeline_mode=pl.Buffered(1))],
            out_specs=pl.BlockSpec((tile, features), lambda i, s: (i, 0)),
            scratch_shapes=[pltpu.VMEM((rows, tile), BF16)],
        ),
        out_shape=jax.ShapeDtypeStruct((width, features), F32),
        compiler_params=pltpu.CompilerParams(vmem_limit_bytes=57 * 1024 * 1024),
        cost_estimate=SMALL,
    )(jnp.stack(where).astype(jnp.int32), *in_hbm(*hidden, g))


def mixture_kernel(
    place_ref, upper0_ref, upper1_ref, lower0_ref, lower1_ref, wd_ref, result_ref
):
    early = pl.program_id(0) < pl.num_programs(0) // 2
    rows = jnp.concatenate(
        [
            jnp.where(early, upper0_ref[...], upper1_ref[...]),
            jnp.where(early, lower0_ref[...], lower1_ref[...]),
        ],
        axis=0,
    )
    result_ref[...] = jnp.dot(rows, wd_ref[...], preferred_element_type=F32).astype(BF16)


def mixture_product(hidden, wd, where):
    count = len(where)
    block = 2 * hidden[0].shape[0] // count
    width, features = wd.shape
    first = pl.BlockSpec((block, width), lambda i, s: (jnp.minimum(i, count // 2 - 1), 0))
    second = pl.BlockSpec((block, width), lambda i, s: (jnp.maximum(i - count // 2, 0), 0))
    return pl.pallas_call(
        mixture_kernel,
        grid_spec=pltpu.PrefetchScalarGridSpec(
            num_scalar_prefetch=1,
            grid=(count,),
            in_specs=[first, second, first, second]
            + [pl.BlockSpec((width, features), lambda i, s: (0, 0))],
            out_specs=pl.BlockSpec((2 * block, features), lambda i, s: (s[i], 0)),
        ),
        out_shape=pltpu.HBM((2 * block * count, features), BF16),
        compiler_params=pltpu.CompilerParams(vmem_limit_bytes=24 * 1024 * 1024),
        cost_estimate=SMALL,
    )(jnp.stack(where).astype(jnp.int32), *in_hbm(*hidden, wd))


def rotated(value, cosine, sine):
    return value * cosine + pltpu.roll(value, HEAD_SIZE // 2, 1) * sine


def inverse_rms(value):
    return lax.rsqrt(jnp.mean(value * value, axis=1, keepdims=True) + EPSILON)


def head_columns(h):
    return slice(h * HEAD_SIZE, (h + 1) * HEAD_SIZE)


def against(left, right):
    return lax.dot_general(left, right, (((1,), (1,)), ((), ())), preferred_element_type=F32)


def over_rows(left, right):
    return lax.dot_general(left, right, (((0,), (0,)), ((), ())), preferred_element_type=F32)


def causal(rows):
    return lax.broadcasted_iota(jnp.int32, (rows, rows), 1) <= lax.broadcasted_iota(
        jnp.int32, (rows, rows), 0
    )


def attention_kernel(
    key_heads,
    x_ref,
    near_ref,
    core_ref,
    near_kv_ref,
    core_kv_ref,
    gains_ref,
    cosine_ref,
    sine_ref,
    wo_ref,
    raw_ref,
    low_ref,
    mixed_ref,
    lse_ref,
    upper_ref,
    lower_ref,
):
    rows = x_ref.shape[0]
    split = near_ref.shape[0]
    query_heads = mixed_ref.shape[1] // HEAD_SIZE
    heads = query_heads + key_heads
    queries = query_heads * HEAD_SIZE
    raw_ref[:, :queries] = jnp.dot(
        x_ref[:, :split], near_ref[...], preferred_element_type=F32
    ) + jnp.dot(x_ref[:, split:], core_ref[...], preferred_element_type=F32)
    wide = 2 * key_heads * HEAD_SIZE
    raw = jnp.dot(
        x_ref[:, :split], near_kv_ref[:, :wide], preferred_element_type=F32
    ) + jnp.dot(x_ref[:, split:], core_kv_ref[:, :wide], preferred_element_type=F32)
    raw_ref[:, queries:] = raw[:, : key_heads * HEAD_SIZE]
    low_ref[:, heads * HEAD_SIZE :] = raw[:, key_heads * HEAD_SIZE :].astype(BF16)
    for h in range(heads):
        u = raw_ref[:, head_columns(h)]
        gain = gains_ref[0:1, :] if h < query_heads else gains_ref[1:2, :]
        low_ref[:, head_columns(h)] = rotated(
            u * inverse_rms(u) * gain, cosine_ref[...], sine_ref[...]
        ).astype(BF16)
    allowed = causal(rows)
    for h in range(query_heads):
        k = query_heads + h * key_heads // query_heads
        scores = against(low_ref[:, head_columns(h)], low_ref[:, head_columns(k)]) / math.sqrt(
            HEAD_SIZE
        )
        scores = jnp.where(allowed, scores, -jnp.inf)
        row_max = jnp.max(scores, axis=1, keepdims=True)
        exps = jnp.exp(scores - row_max)
        total = jnp.sum(exps, axis=1, keepdims=True)
        lse_ref[:, h : h + 1] = row_max + jnp.log(total)
        mixed_ref[:, head_columns(h)] = jnp.dot(
            (exps * (1.0 / total)).astype(BF16),
            low_ref[:, head_columns(k + key_heads)],
            preferred_element_type=F32,
        ).astype(BF16)
    part = jnp.dot(mixed_ref[...], wo_ref[...], preferred_element_type=F32)
    upper_ref[...] = part[: rows // 2].astype(BF16)
    lower_ref[...] = part[rows // 2 :].astype(BF16)


def attention(x, near, core, near_kv, core_kv, gains, cosine, sine, wo, key_heads):
    rows = x.shape[0]
    query_width, features = wo.shape
    width = query_width + 2 * key_heads * HEAD_SIZE
    shapes = [
        ((rows, query_width + key_heads * HEAD_SIZE), F32),
        ((rows, width), BF16),
        ((rows, query_width), BF16),
        ((rows, query_width // HEAD_SIZE), F32),
        ((rows // 2, features), BF16),
        ((rows // 2, features), BF16),
    ]
    return pl.pallas_call(
        functools.partial(attention_kernel, key_heads),
        out_shape=[jax.ShapeDtypeStruct(*v) for v in shapes],
        compiler_params=pltpu.CompilerParams(vmem_limit_bytes=32 * 1024 * 1024),
        cost_estimate=SMALL,
    )(x, near, core, near_kv, core_kv, gains, cosine, sine, wo)


def attention_back_kernel(
    key_heads,
    place_ref,
    upstream_ref,
    wo_ref,
    raw_ref,
    low_ref,
    lse_ref,
    gains_ref,
    cosine_ref,
    sine_ref,
    x_ref,
    near_ref,
    core_ref,
    near_kv_ref,
    core_kv_ref,
    beside_ref,
    feature_ref,
    weights_ref,
    mixed_grad_ref,
    raw_grad_ref,
):
    rows = upstream_ref.shape[0]
    split = near_ref.shape[0]
    width = raw_grad_ref.shape[1]
    queries_width = near_ref.shape[1]
    query_heads = mixed_grad_ref.shape[1] // HEAD_SIZE
    group = query_heads // key_heads
    root = math.sqrt(HEAD_SIZE)
    mixed_grad_ref[...] = against(upstream_ref[...], wo_ref[...]).astype(BF16)
    allowed = causal(rows)
    cosine = cosine_ref[...]
    sine = sine_ref[...]

    def norm_back(h, grad, gain):
        u = raw_ref[:, head_columns(h)]
        scale = inverse_rms(u)
        normal = u * scale
        turned = grad * cosine - pltpu.roll(grad, HEAD_SIZE // 2, 1) * sine
        weighted = turned * gain
        inward = scale * (weighted - normal * jnp.mean(weighted * normal, axis=1, keepdims=True))
        raw_grad_ref[:, head_columns(h)] = inward.astype(BF16)
        return turned * normal

    query_terms = jnp.zeros((rows, HEAD_SIZE), F32)
    key_terms = jnp.zeros((rows, HEAD_SIZE), F32)
    for k in range(key_heads):
        keys = low_ref[:, head_columns(query_heads + k)]
        values = low_ref[:, head_columns(query_heads + key_heads + k)]
        key_grad = jnp.zeros((rows, HEAD_SIZE), F32)
        value_grad = jnp.zeros((rows, HEAD_SIZE), F32)
        for h in range(k * group, (k + 1) * group):
            queries = low_ref[:, head_columns(h)]
            mixed_grad = mixed_grad_ref[:, head_columns(h)]
            scores = against(queries, keys) / root
            probs = jnp.where(allowed, jnp.exp(scores - lse_ref[:, h : h + 1]), 0.0)
            probs_grad = against(mixed_grad, values)
            value_grad += over_rows(probs.astype(BF16), mixed_grad)
            inner = jnp.sum(probs * probs_grad, axis=1, keepdims=True)
            scores_grad = (probs * (probs_grad - inner)).astype(BF16)
            query_grad = jnp.dot(scores_grad, keys, preferred_element_type=F32) / root
            key_grad += over_rows(scores_grad, queries)
            query_terms += norm_back(h, query_grad, gains_ref[0:1, :])
        key_terms += norm_back(query_heads + k, key_grad / root, gains_ref[1:2, :])
        raw_grad_ref[:, head_columns(query_heads + key_heads + k)] = value_grad.astype(BF16)
    raw_grad = raw_grad_ref[...]
    for part, (query_ref, kv_ref) in enumerate(
        ((near_ref, near_kv_ref), (core_ref, core_kv_ref))
    ):
        feature_ref[:, part * split : (part + 1) * split] = (
            against(raw_grad[:, :queries_width], query_ref[...])
            + against(raw_grad[:, queries_width:], kv_ref[:, : width - queries_width])
        ).astype(BF16)
    feature_ref[:, 2 * split : 2 * split + HEAD_SIZE] = query_terms.astype(BF16)
    feature_ref[:, 2 * split + HEAD_SIZE :] = key_terms.astype(BF16)
    count = place_ref.shape[0]
    block = 2 * split // count
    for j in range(count):
        at = pl.ds(pl.multiple_of(place_ref[j] * block, block), block)
        if block % LANES == 0:
            columns = x_ref[:, j * block : (j + 1) * block]
            weights_ref[at, :width] = over_rows(columns, raw_grad).astype(BF16)
    if block % LANES:
        weights_ref[:, :width] = over_rows(x_ref[...], raw_grad).astype(BF16)
    weights_ref[:, width:] = beside_ref[...]


def in_vmem(count):
    return [pl.BlockSpec()] * count


def in_smem():
    return [pl.BlockSpec(memory_space=pltpu.SMEM)]


def attention_back(
    where, upstream, wo, raw, low, lse, gains, cosine, sine, x, weights, beside, key_heads
):
    rows, features = upstream.shape
    query_width = wo.shape[0]
    split = weights[0].shape[0]
    width = low.shape[1]
    whole = width + beside.shape[1]
    shapes = [
        jax.ShapeDtypeStruct((rows, features + 2 * HEAD_SIZE), BF16),
        pltpu.HBM((features, whole), BF16),
    ]
    operands = [upstream, wo, raw, low, lse, gains, cosine, sine, x, *weights, beside]
    return pl.pallas_call(
        functools.partial(attention_back_kernel, key_heads),
        in_specs=in_smem() + in_vmem(len(operands)),
        out_specs=in_vmem(2),
        out_shape=shapes,
        scratch_shapes=[pltpu.VMEM((rows, query_width), BF16), pltpu.VMEM((rows, width), BF16)],
        compiler_params=pltpu.CompilerParams(vmem_limit_bytes=40 * 1024 * 1024),
        cost_estimate=SMALL,
    )(jnp.stack(where).astype(jnp.int32), *in_hbm(*operands))


def chunk_places():
    return jnp.stack(
        [lax.axis_index("tp") ^ m for m in range(lax.axis_size("tp"))]
    ).astype(jnp.int32)


def rows_at(index, size):
    return pl.ds(pl.multiple_of(index * size, size), size)


def resid_kernel(place_ref, *refs):
    *pieces, hidden_ref, gain_ref, resid_ref, routed_ref = refs
    rows = pieces[0].shape[0]
    for m, piece in enumerate(pieces):
        at = rows_at(place_ref[m], rows)
        resid = hidden_ref[at, :].astype(F32) + piece[...].astype(F32)
        resid_ref[at, :] = resid
        routed_ref[at, :] = (resid * inverse_rms(resid) * gain_ref[...]).astype(BF16)


def resid_and_routed(pieces, hidden, gain):
    return pl.pallas_call(
        resid_kernel,
        in_specs=in_smem() + in_vmem(len(pieces) + 2),
        out_specs=in_vmem(2),
        out_shape=[
            pltpu.HBM(hidden.shape, F32),
            jax.ShapeDtypeStruct(hidden.shape, BF16),
        ],
        compiler_params=pltpu.CompilerParams(vmem_limit_bytes=6 * 1024 * 1024),
        cost_estimate=SMALL,
    )(chunk_places(), *pieces, hidden, gain)


def resid_back_kernel(parts, place_ref, column_ref, *refs):
    pieces = refs[: 2 * parts]
    (
        resid_a_ref,
        resid_b_ref,
        routed_a_ref,
        routed_b_ref,
        ids_ref,
        router_ref,
        gain_ref,
        upstream_ref,
        mixed_ref,
        grad_ref,
        low_ref,
        beside_ref,
        keep_ref,
        send_ref,
        returned_ref,
        wide_ref,
    ) = refs[2 * parts :]
    rows, features = upstream_ref.shape
    expert_count = router_ref.shape[1]
    chunk = pieces[0].shape[0]
    for h in range(2):
        for m in range(parts):
            returned_ref[rows_at(place_ref[m] + h * parts, chunk), :] = pieces[h * parts + m][...]
    routed = jnp.concatenate([routed_a_ref[...], routed_b_ref[...]], axis=0)
    resid = jnp.concatenate([resid_a_ref[...], resid_b_ref[...]], axis=0)
    logits = jnp.dot(routed, router_ref[...], preferred_element_type=F32)
    lane = lax.broadcasted_iota(jnp.int32, (rows, expert_count), 1)
    named = ids_ref[:, 0:1] == lane
    for k in range(1, TOP):
        named = named | (ids_ref[:, k : k + 1] == lane)
    exponent = jnp.exp(logits - jnp.max(logits, axis=1, keepdims=True))
    router = exponent / jnp.sum(exponent, axis=1, keepdims=True)
    chosen = jnp.where(named, router, 0.0)
    total = jnp.sum(chosen, axis=1, keepdims=True)
    gates = chosen / total
    tail = returned_ref[:, features:].astype(F32)
    tail = tail + pltpu.roll(tail, tail.shape[1] - expert_count, 1)
    grad_gates = jnp.where(named, tail[:, :expert_count], 0.0)
    inner = jnp.sum(grad_gates * gates, axis=1, keepdims=True)
    grad_router = jnp.where(named, (grad_gates - inner) / total, 0.0)
    inner = jnp.sum(router * grad_router, axis=1, keepdims=True)
    grad_logits = (router * (grad_router - inner)).astype(BF16)
    grad_routed = returned_ref[:, :features].astype(F32) + against(grad_logits, router_ref[...])
    scale = inverse_rms(resid)
    normal = resid * scale
    weighted = grad_routed * gain_ref[...]
    inner = jnp.mean(weighted * normal, axis=1, keepdims=True)
    grad = upstream_ref[...].astype(F32) + scale * (weighted - normal * inner)
    grad_ref[...] = grad
    low_ref[...] = grad.astype(BF16)
    half = column_ref.shape[0] // 2
    for j in range(half):
        for k, out_ref in ((j, keep_ref), (half + j, send_ref)):
            columns = pl.ds(pl.multiple_of(column_ref[k] * LANES, LANES), LANES)
            out_ref[j * LANES : (j + 1) * LANES, :] = over_rows(
                mixed_ref[:, columns], low_ref[...]
            ).astype(BF16)
    wide_ref[...] = jnp.zeros(wide_ref.shape, BF16)
    wide_ref[:, :expert_count] = grad_logits
    one = lax.broadcasted_iota(jnp.int32, wide_ref.shape, 1) == expert_count
    beside_ref[...] = (
        over_rows(routed, wide_ref[...])
        + over_rows((grad_routed * normal).astype(BF16), one.astype(F32).astype(BF16))
    ).astype(BF16)


def resid_back(pieces, resid, routed, ids, router, gain, upstream, mixed, columns):
    parts = len(pieces) // 2
    rows, features = upstream.shape
    expert_count = router.shape[1]
    wide = -(-(expert_count + 1) // LANES) * LANES
    half = mixed.shape[1] // 2
    shapes = [
        pltpu.HBM((rows, features), F32),
        jax.ShapeDtypeStruct((rows, features), BF16),
        jax.ShapeDtypeStruct((features, wide), BF16),
        pltpu.HBM((half, features), BF16),
        jax.ShapeDtypeStruct((half, features), BF16),
    ]
    operands = [*pieces, *in_hbm(*resid, *routed, ids, router, gain, upstream, mixed)]
    return pl.pallas_call(
        functools.partial(resid_back_kernel, parts),
        in_specs=in_smem() * 2 + in_vmem(len(operands)),
        out_specs=in_vmem(len(shapes)),
        out_shape=shapes,
        scratch_shapes=[
            pltpu.VMEM((rows, pieces[0].shape[1]), BF16),
            pltpu.VMEM((rows, wide), BF16),
        ],
        compiler_params=pltpu.CompilerParams(vmem_limit_bytes=40 * 1024 * 1024),
        cost_estimate=SMALL,
    )(chunk_places(), jnp.stack(columns).astype(jnp.int32), *operands)


def input_kernel(ordered, place_ref, block_ref, *refs):
    *pieces, hidden_ref, resid_grad_ref, gain_ref, result_ref, late_ref, total_ref = refs
    features = hidden_ref.shape[1]
    rows = pieces[0].shape[0]
    count = block_ref.shape[0]
    block = features // count
    for m, piece in enumerate(pieces):
        total_ref[rows_at(place_ref[m], rows), :] = piece[...]
    hidden = hidden_ref[...].astype(F32)
    scale = inverse_rms(hidden)
    columns = [
        slice(j * block, (j + 1) * block)
        if ordered
        else pl.ds(pl.multiple_of(block_ref[j] * block, block), block)
        for j in range(count)
    ]
    inner = jnp.zeros((hidden.shape[0], 1), F32)
    for j in range(count):
        normal = hidden_ref[:, columns[j]].astype(F32) * scale
        grad = total_ref[:, j * block : (j + 1) * block].astype(F32)
        terms = grad * normal
        inner += jnp.sum(terms * gain_ref[:, columns[j]], axis=1, keepdims=True)
        late_ref[j : j + 1, :block] = jnp.sum(terms, axis=0, keepdims=True)
    inner = inner * (1.0 / features)
    for j in range(count):
        normal = hidden_ref[:, columns[j]].astype(F32) * scale
        weighted = total_ref[:, j * block : (j + 1) * block].astype(F32) * gain_ref[:, columns[j]]
        result_ref[:, columns[j]] = resid_grad_ref[:, columns[j]] + scale * (
            weighted - normal * inner
        )
    heads = jnp.sum(total_ref[:, features:].astype(F32), axis=0, keepdims=True)
    late_ref[:, block:] = jnp.broadcast_to(heads, (count, heads.shape[1]))


def input_gradient(pieces, hidden, resid_grad, gain, where):
    rows, features = hidden.shape
    count = len(where)
    extra = pieces[0].shape[1] - features
    return pl.pallas_call(
        functools.partial(input_kernel, absolute()),
        in_specs=in_smem() * 2 + in_vmem(len(pieces) + 3),
        out_specs=in_vmem(2),
        out_shape=[
            jax.ShapeDtypeStruct((rows, features), F32),
            jax.ShapeDtypeStruct((count, features // count + extra), F32),
        ],
        scratch_shapes=[pltpu.VMEM((rows, pieces[0].shape[1]), BF16)],
        compiler_params=pltpu.CompilerParams(vmem_limit_bytes=24 * 1024 * 1024),
        cost_estimate=SMALL,
    )(chunk_places(), jnp.stack(where).astype(jnp.int32), *pieces, *in_hbm(hidden, resid_grad, gain))


def widen_kernel(place_ref, near_ref, core_ref, result_ref):
    early = pl.program_id(0) < pl.num_programs(0) // 2
    result_ref[...] = jnp.where(early, near_ref[...], core_ref[...]).astype(F32)


def widen_blocks(near, core, where):
    count = len(where)
    features = near.shape[1]
    block = 2 * near.shape[0] // count
    half = count // 2
    first = pl.BlockSpec((block, features), lambda i, s: (jnp.minimum(i, half - 1), 0))
    second = pl.BlockSpec((block, features), lambda i, s: (jnp.maximum(i - half, 0), 0))
    return pl.pallas_call(
        widen_kernel,
        grid_spec=pltpu.PrefetchScalarGridSpec(
            num_scalar_prefetch=1,
            grid=(count,),
            in_specs=[first, second],
            out_specs=pl.BlockSpec((block, features), lambda i, s: (s[i], 0)),
        ),
        out_shape=jax.ShapeDtypeStruct((block * count, features), F32),
        compiler_params=pltpu.CompilerParams(vmem_limit_bytes=24 * 1024 * 1024),
        cost_estimate=SMALL,
    )(jnp.stack(where).astype(jnp.int32), near, core)


def shards(
    hidden_in,
    expert_ids,
    attention_gain,
    query_gain,
    key_gain,
    query_weight,
    key_matrix,
    value_matrix,
    output_weight,
    expert_gain,
    router_weight,
    gate_up_weight,
    down_weight,
    output_grad,
):
    tokens, features = hidden_in.shape
    owners = lax.axis_size("ep")
    local_experts = gate_up_weight.shape[0]
    expert_count = local_experts * owners
    rows_a = tokens // 2

    head_share = query_gain.shape[0]
    share = router_weight.shape[0]
    small_rows = max(tokens, share)
    padded = lambda v: jnp.pad(v.astype(BF16), ((0, small_rows - v.shape[0]), (0, 0)))
    small = jnp.concatenate(
        [
            padded(router_weight),
            padded(jnp.stack([attention_gain, expert_gain], axis=1)),
            padded(jnp.stack([query_gain, key_gain], axis=1)),
            padded(expert_ids),
        ],
        axis=1,
    )
    small_width = small.shape[1]
    small = jnp.pad(small, ((0, 0), (0, -small_width % LANES)))
    packed = jnp.concatenate([key_matrix, value_matrix], axis=1)
    packed_width = packed.shape[1]
    together = small_rows == share
    if together:
        packed = jnp.concatenate([packed, small], axis=1)
    packed_hops = gather_hops(packed)
    hops = gather_hops(query_weight)
    packed_near = gather_near(packed, packed_hops)
    packed_core = gather_core(packed_near, packed_hops)
    if together:
        small = jnp.concatenate(
            [packed_near[:, packed_width:], packed_core[:, packed_width:]], axis=0
        )
    else:
        small = lax.all_gather(small, "ep", axis=0, tiled=True)
    small = put_blocks(small, 0).reshape(owners, small_rows, -1)
    by_feature = small[:, :share, : expert_count + 2].reshape(features, -1)
    router_full = by_feature[:, :expert_count]
    attn_gain_full = by_feature[:, expert_count].astype(F32)[None, :]
    mlp_gain_full = by_feature[:, expert_count + 1].astype(F32)[None, :]
    gains = (
        small[:, :head_share, expert_count + 2 : expert_count + 4]
        .reshape(HEAD_SIZE, 2)
        .astype(F32)
        .T
    )
    ids_all = small[:, :tokens, expert_count + 4 : small_width].reshape(-1, TOP).astype(jnp.int32)
    wd = down_weight.reshape(-1, features)
    normed_low = norm_rows(hidden_in.astype(F32), attn_gain_full).astype(BF16)
    normed_rel = pick_blocks(normed_low, 1)
    positions = jnp.arange(tokens, dtype=jnp.int32)
    cosine, sine_table = rope_tables(positions, HEAD_SIZE)
    (
        hops,
        packed_core,
        normed_rel,
        cosine,
        sine_table,
        gains,
        router_full,
        attn_gain_full,
        mlp_gain_full,
        ids_all,
        output_all,
        gate_up_low,
    ) = join(
        hops,
        packed_core,
        normed_rel,
        cosine,
        sine_table,
        gains,
        router_full,
        attn_gain_full,
        mlp_gain_full,
        ids_all,
        output_grad,
        gate_up_weight,
    )

    near = gather_near(query_weight, hops)
    weights_rel = [near, gather_core(near, hops), packed_near, packed_core]
    output_all = lax.all_gather(output_all, "ep", axis=0, tiled=True)
    query_width = query_weight.shape[1]
    key_width = key_matrix.shape[1]
    key_heads = key_width // HEAD_SIZE
    raw, low, attention_output, lse, *head_parts = attention(
        normed_rel, *weights_rel, gains, cosine, sine_table, output_weight, key_heads
    )
    (head_parts,) = join(head_parts)
    head_parts = list(head_parts)

    hops = reduce_hops(head_parts[0])
    wgu = gate_up_low.transpose(1, 0, 2).reshape(features, -1)
    hops, wgu, head_parts[1] = join(hops, wgu, head_parts[1])

    chunk = reduce_total(head_parts[0], hops)
    hops_b = reduce_hops(head_parts[1])
    (hops,) = join(spread_hops(chunk))

    resid_a, routed_a = resid_and_routed([chunk] + hops, hidden_in[:rows_a], mlp_gain_full)
    chunk = reduce_total(head_parts[1], hops_b)
    hops_a, hops = join(gather_hops(routed_a), spread_hops(chunk))

    resid_b, routed_b = resid_and_routed([chunk] + hops, hidden_in[rows_a:], mlp_gain_full)
    near_a = gather_near(routed_a, hops_a)
    core_a = gather_core(near_a, hops_a)
    hops_b = gather_hops(routed_b)
    lined = places()
    where = [2 * b + h for h in range(2) for b in lined]

    def experts(piece, x):
        rows = slice(piece * owners // 2, (piece + 1) * owners // 2)
        return run_experts(
            x, output_all, ids_all, where[rows], router_full, wgu, wd, local_experts
        )

    keep_a, joined_0, hidden_0 = experts(0, near_a)
    send_a, joined_1, hidden_1 = experts(1, core_a)
    hops_b, send_a, keep_a = join(hops_b, send_a, keep_a)

    near_b = gather_near(routed_b, hops_b)
    core_b = gather_core(near_b, hops_b)
    come = scatter_swap(send_a)
    keep_b, joined_2, hidden_2 = experts(2, near_b)
    come, core_b, keep_b = join(come, core_b, keep_b)

    sums_a = scatter_sums(keep_a, come)
    hops_a = scatter_hops(sums_a)
    send_b, joined_3, hidden_3 = experts(3, core_b)
    hops_a, send_b = join(hops_a, send_b)
    joined = [joined_0, joined_1, joined_2, joined_3]
    hidden = [hidden_0, hidden_1, hidden_2, hidden_3]
    routed_pieces = [near_a, core_a, near_b, core_b]

    come = scatter_swap(send_b)
    total_a = scatter_total(sums_a, hops_a)
    hops = reduce_hops(total_a)
    come, hidden = join(come, hidden)

    sums_b = scatter_sums(keep_b, come)
    hops_b = scatter_hops(sums_b)
    mixture_parts = mixture_product(hidden, wd, lined)
    chunk_a = reduce_total(total_a, hops)
    spread_a, hops_b, mixture_parts, joined = join(
        spread_hops(chunk_a), hops_b, mixture_parts, joined
    )

    mixture = lax.psum_scatter(mixture_parts, "ep", scatter_dimension=0, tiled=True)
    total_b = scatter_total(sums_b, hops_b)
    (hops,) = join(reduce_hops(total_b))
    chunk_b = reduce_total(total_b, hops)
    (spread_b,) = join(spread_hops(chunk_b))

    columns = (
        [jnp.int32(b) for b in range(attention_output.shape[1] // LANES)] if absolute() else lined
    )
    grad_resid, grad_attended, by_feature, output_keep, output_send = resid_back(
        [chunk_a, *spread_a, chunk_b, *spread_b],
        [resid_a, resid_b],
        [routed_a, routed_b],
        expert_ids,
        router_full,
        mlp_gain_full,
        output_grad,
        attention_output,
        columns,
    )

    feature_part, weights_grad = attention_back(
        lined,
        grad_attended,
        output_weight,
        raw,
        low,
        lse,
        gains,
        cosine,
        sine_table,
        normed_rel,
        weights_rel,
        by_feature,
        key_heads,
    )
    come, feature_part, weights_grad = join(
        scatter_swap(output_send), feature_part, weights_grad
    )

    weights_rows = lax.psum_scatter(weights_grad, "ep", scatter_dimension=0, tiled=True)
    hops = reduce_hops(feature_part)
    output_sums = scatter_sums(output_keep, come)
    output_hops = scatter_hops(output_sums)
    down_grad = down_product(hidden, output_all, where).reshape(down_weight.shape)
    hops, output_hops, down_grad, mixture, joined = join(
        hops, output_hops, down_grad, mixture, joined
    )

    chunk = reduce_total(feature_part, hops)
    hops = spread_hops(chunk)
    mixture_hops = reduce_hops(mixture)
    output_share = scatter_total(output_sums, output_hops)
    gate_up_grad = gate_up_product(routed_pieces, joined, gate_up_weight.shape)
    hops, gate_up_grad, output_share = join(hops, gate_up_grad, output_share)

    output_hops = gather_hops(output_share)
    input_grad, late = input_gradient(
        [chunk, *hops], hidden_in, grad_resid, attn_gain_full, lined
    )
    late_come = scatter_swap(late[owners // 2 :])
    late_come, output_hops, mixture_hops = join(late_come, output_hops, mixture_hops)

    mixture_chunk = reduce_total(mixture, mixture_hops)
    mixture_hops = spread_hops(mixture_chunk)
    near = gather_near(output_share, output_hops)
    output_core = gather_core(near, output_hops)
    late_sums = scatter_sums(late[: owners // 2], late_come)
    late_hops = scatter_hops(late_sums)
    output_weight_grad = widen_blocks(near, output_core, lined)
    late_hops, output_weight_grad, weights_rows, mixture_hops = join(
        late_hops, output_weight_grad, weights_rows, mixture_hops
    )
    weights_rows = weights_rows.astype(F32)
    late = scatter_total(late_sums, late_hops)[0]
    head_grads = lax.dynamic_slice_in_dim(
        late[share:].reshape(2, HEAD_SIZE), lax.axis_index("ep") * head_share, head_share, 1
    )
    early = weights_rows[:, query_width + 2 * key_width :]
    mixture = spread_total(mixture_chunk, mixture_hops)
    block_out = (jnp.concatenate([resid_a, resid_b], axis=0) + mixture.astype(F32)).astype(BF16)
    return (
        block_out,
        input_grad,
        late[:share],
        head_grads[0],
        head_grads[1],
        weights_rows[:, :query_width],
        weights_rows[:, query_width : query_width + key_width],
        weights_rows[:, query_width + key_width : query_width + 2 * key_width],
        output_weight_grad,
        early[:, expert_count],
        early[:, :expert_count],
        gate_up_grad,
        down_grad,
    )


def solution(mesh):
    in_specs = (
        P("ep", None),
        P("ep", None),
        P("ep"),
        P("ep"),
        P("ep"),
        P("ep", "tp"),
        P("ep", "tp"),
        P("ep", "tp"),
        P("tp", None),
        P("ep"),
        P("ep", None),
        P("ep", None, "tp"),
        P("ep", "tp", None),
        P("ep", None),
    )
    out_specs = (
        P("ep", None),
        P("ep", None),
        P("ep"),
        P("ep"),
        P("ep"),
        P("ep", "tp"),
        P("ep", "tp"),
        P("ep", "tp"),
        P("tp", None),
        P("ep"),
        P("ep", None),
        P("ep", None, "tp"),
        P("ep", "tp", None),
    )
    return jax.shard_map(shards, mesh=mesh, in_specs=in_specs, out_specs=out_specs, check_vma=False)
```
